128 devices in a mesh: span: 16 (over z, x_lo, core), head: 8 (over y, x_hi).
Axes of the slice: x: 4 (x_hi: 2, x_lo: 2; x = x_hi * 2 + x_lo), y: 4, z: 4, core: 2. Of those that a mesh axis runs over, the one named last changes fastest.
Arguments:
- queries: bfloat16 [16384, 3072], P(('span', 'head')), may hold values from -15 to 15
- keys: bfloat16 [16384, 3072], P(('span', 'head')), may hold values from -6 to 6
- values: bfloat16 [16384, 3072], P(('span', 'head')), may hold values from -6 to 6
- span_ids: int32 [16384], P(('span', 'head')), may hold values from 0 to 23, never falling along the last dimension, each value on 1 to 1365 neighbouring positions
- timesteps: int32 [24], replicated, may hold values from 0 to 999
- time_weight: bfloat16 [256, 3072], replicated, may hold values from -0.375 to 0.375
Outputs:
- gated: bfloat16 [16384, 3072], P(('span', 'head'))
The draws below stay inside these ranges and needn't reach their ends.
Inputs may be any that keep to these rules, and one draw needn't show every extreme that they name: span_ids never fall along the tokens; each span holds 1 to 1365 tokens.
All inputs are finite; a program needn't handle non-finite values.
Results may differ from the reference program's by a relative error of at most 0.0057.
Values may be sent and summed in bfloat16 or wider, within the bound.
No kernel may reach another device: no remote copies, remote signals or barrier semaphores. Data moves between devices by JAX's collectives and lax.ppermute only.
A program may use at most 128 MiB of HBM per device.

```python
import math
import jax
import jax.numpy as jnp
import numpy as np
from jax import lax

HEADS = 24
HEAD_DIM = 128
FREQ = 256
SPANS = 24
DM = 3072
TOKENS = 16384
SPAN_MOST = 1365


def draw_queries(key, part):
    key = jax.random.fold_in(key, 11)
    base = jnp.clip(2.5 * jax.random.normal(key, (TOKENS, DM), jnp.float32), -15.0, 15.0)
    return base.astype(jnp.bfloat16)


def draw_keys(key, part):
    key = jax.random.fold_in(key, 23)
    base = jnp.clip(jax.random.normal(key, (TOKENS, DM), jnp.float32), -6.0, 6.0)
    return base.astype(jnp.bfloat16)


def place_ends(values, rng, smallest, largest):
    dims = values.shape
    index_at = [jax.random.randint(jax.random.fold_in(rng, axis), (), 0, dims[axis]) for axis in range(len(dims))]
    values = values.at[tuple(index_at)].set(smallest)
    longest = dims.index(max(dims))
    index_at[longest] = (index_at[longest] + 1) % dims[longest]
    return values.at[tuple(index_at)].set(largest)


def levels(key, shape, cuts, least, largest):
    level = 1.0
    for dim, blocks in cuts:
        draws = jax.random.uniform(jax.random.fold_in(jax.random.fold_in(key, 6), dim), (blocks,), jnp.float32, least / len(cuts), largest / len(cuts))
        level = level * jnp.repeat(jnp.exp(draws), shape[dim] // blocks).reshape((-1,) + (1,) * (len(shape) - 1 - dim))
    return level


def length_profile(count, total, limit, slope):
    loads = [(1 << 20) // math.isqrt(standing ** slope) + 1 for standing in range(2, count + 1)]
    spare, given = total - limit - (count - 1), [1] * (count - 1)
    while spare > 0:
        movable = [i for i in range(count - 1) if given[i] < limit]
        pool, left = sum([loads[i] for i in movable]), spare
        for i in movable:
            more = min(limit - given[i], max(1, left * loads[i] // pool), spare)
            given[i] = given[i] + more
            spare = spare - more
    return np.array([limit] + given)


def ragged(own_key, number_of, total, reach, slope):
    if number_of == 2:
        one = jax.random.randint(own_key, (), max(1, total - reach), min(reach, total - 1) + 1)
        return jnp.stack([one, total - one])
    lengths = jnp.asarray(length_profile(number_of, total, reach, slope), jnp.int32)
    twos = (number_of - 1) // 2
    giver, taker = lengths[1:1 + 2 * twos:2], lengths[2:2 + 2 * twos:2]
    room = jnp.minimum(giver - 1, reach - taker)
    shifted = jax.random.randint(jax.random.fold_in(own_key, 1), (twos,), 0, 1 << 20) % (room + 1)
    lengths = lengths.at[1:1 + 2 * twos:2].set(giver - shifted).at[2:2 + 2 * twos:2].set(taker + shifted)
    return lengths[jax.random.permutation(jax.random.fold_in(own_key, 2), number_of)]


def noise(key, shape, deviation, reach, shards=(), held_as=jnp.bfloat16):
    level = levels(key, shape, shards, -0.22, 0.18) if shards else 1.0
    drawn = jax.random.normal(key, shape, jnp.float32) * deviation * level
    return jnp.minimum(jnp.maximum(drawn, -reach), reach).astype(held_as)


def setup_inputs(seed: int = 0) -> dict:
    arg_keys = jax.random.split(jax.random.key(seed), 7)
    return {
        "queries": draw_queries(jax.random.fold_in(arg_keys[6], 71), 0),
        "keys": draw_keys(jax.random.fold_in(arg_keys[6], 71), 0),
        "values": noise(arg_keys[2], (TOKENS, DM), 1.0, 6.0, ((0, 128),)),
        "span_ids": jnp.searchsorted(jnp.cumsum(ragged(arg_keys[3], SPANS, TOKENS, SPAN_MOST, 0)), jnp.arange(TOKENS), side="right").astype(jnp.int32),
        "timesteps": place_ends(jax.random.randint(arg_keys[4], (SPANS,), 0, 1000), jax.random.fold_in(arg_keys[4], 1), 0, 999).astype(jnp.int32),
        "time_weight": noise(arg_keys[5], (FREQ, DM), FREQ ** -0.5, 0.375),
    }


def gate_rows(span_ids, timesteps, time_weight):
    half = FREQ // 2
    freqs = jnp.exp(-math.log(10000.0) * jnp.arange(half, dtype=jnp.float32) / half)
    angles = timesteps.astype(jnp.float32)[:, None] * freqs[None, :]
    embed = jnp.concatenate([jnp.cos(angles), jnp.sin(angles)], axis=1).astype(jnp.bfloat16)
    gate_table = jnp.dot(embed, time_weight, preferred_element_type=jnp.float32)
    onehot = (span_ids[:, None] == jnp.arange(SPANS, dtype=jnp.int32)[None, :]).astype(jnp.float32)
    return jnp.dot(onehot, gate_table, precision=lax.Precision.HIGHEST)


def reference(queries, keys, values, span_ids, timesteps, time_weight):
    score_scale = HEAD_DIM ** -0.5
    rows_block = math.gcd(TOKENS, 1024)
    query_heads = queries.reshape(TOKENS, HEADS, HEAD_DIM).transpose(1, 0, 2)
    key_heads = keys.reshape(TOKENS, HEADS, HEAD_DIM).transpose(1, 0, 2)
    value_heads = values.reshape(TOKENS, HEADS, HEAD_DIM).transpose(1, 0, 2)
    id_blocks = span_ids.reshape(TOKENS // rows_block, rows_block)

    def one_head(triple):
        head_q, head_k, head_v = triple
        q_blocks = head_q.reshape(TOKENS // rows_block, rows_block, HEAD_DIM)

        def one_block(pair):
            q_block, q_ids = pair
            scores = jnp.dot(q_block, head_k.T, preferred_element_type=jnp.float32) * score_scale
            visible = span_ids[None, :] <= q_ids[:, None]
            scores = jnp.where(visible, scores, -1e30)
            top = jnp.max(scores, axis=1, keepdims=True)
            weights = jnp.where(visible, jnp.exp(scores - top), 0.0)
            total = jnp.sum(weights, axis=1, keepdims=True)
            summed = jnp.dot(weights.astype(jnp.bfloat16), head_v, preferred_element_type=jnp.float32)
            return (summed / total).astype(jnp.bfloat16)

        return lax.map(one_block, (q_blocks, id_blocks)).reshape(TOKENS, HEAD_DIM)

    attended = lax.map(one_head, (query_heads, key_heads, value_heads))
    attended = attended.transpose(1, 0, 2).reshape(TOKENS, DM)
    gates = gate_rows(span_ids, timesteps, time_weight)
    return (gates * attended.astype(jnp.float32)).astype(jnp.bfloat16)
```

```python
import functools
import math

import jax
import jax.numpy as jnp
from jax import lax
from jax.experimental import pallas as pl
from jax.experimental.pallas import tpu as pltpu
from jax.sharding import PartitionSpec as P

HEAD_DIM = 128
SCALE = HEAD_DIM**-0.5
BOTH = ("span", "head")
ZONES = 4
SEGMENT = 256
WIDE = 1024
WIDTH = 512
ITEMS = 4
K_NORM, Q_NORM = 32, 40
NOTE = 16
PLAIN_LIMIT = 70.0
LOW = -1e30


def dot(a, b):
    return jnp.dot(a, b, preferred_element_type=jnp.float32)


def attend_kernel(head, ringed, info_ref, own_q, their_q, end_ref, *refs):
    sources, refs = refs[: 4 if ringed else 1], refs[4 if ringed else 1 :]
    own_out, their_out, kv_ref, qt_ref, weight_ref, acc_ref, top_ref, sems = refs
    core, rank, side = info_ref[0], info_ref[1], info_ref[2]
    blocks = 2 * ZONES

    copies = []
    if ringed:
        near, near_last, far, far_last = sources
        for j, (src, last, c) in enumerate(((near, near_last, core), (far, far_last, 1 - core))):
            pieces = [(src.at[0], 0), (src.at[1], 1), (last.at[0], 2), (src.at[2], 3)]
            for piece, step in pieces:
                copies.append(
                    pltpu.make_async_copy(
                        piece.at[:, :, pl.ds(0, 2 * HEAD_DIM)],
                        kv_ref.at[(rank + step) % 4, c],
                        sems.at[4 * j + step],
                    )
                )
    else:
        copies.append(pltpu.make_async_copy(sources[0], kv_ref, sems.at[0]))
    for copy in copies:
        copy.start()

    for zone in range(ZONES):
        for q_ref, half in ((own_q, side), (their_q, 1 - side)):
            qt_ref[2 * zone + half] = q_ref[zone].astype(jnp.float32).T.astype(jnp.bfloat16)
    acc_ref[...] = jnp.zeros_like(acc_ref)
    top_ref[...] = jnp.zeros_like(top_ref)
    ones = jnp.ones((NOTE, WIDTH), jnp.bfloat16)
    for copy in copies:
        copy.wait()

    def part(i, rows):
        return kv_ref[pl.ds((i % 2) * 2, 2), (i // 2) % 2, i // 4, :, rows]

    def keys_at(i):
        return part(i, slice(0, HEAD_DIM)).reshape(WIDTH, HEAD_DIM)

    def values_at(i):
        block = part(i, slice(HEAD_DIM, 2 * HEAD_DIM))
        block = jnp.concatenate([block[y, x] for y in range(2) for x in range(2)], axis=1)
        return jnp.concatenate([block, ones], axis=0)

    def visible_at(r, i):
        row = i * WIDTH + lax.broadcasted_iota(jnp.int32, (WIDTH, SEGMENT), 0)
        return row < end_ref[r]

    def weigh(slot, r, i):
        r = jnp.minimum(r, blocks - 1)
        weights = jnp.exp(dot(keys_at(i), qt_ref[r]) * SCALE)
        weights = jnp.where(visible_at(r, i), weights, 0.0)
        weight_ref[slot] = weights.astype(jnp.bfloat16)

    def absorb(slot, r, i):
        acc_ref[r] += dot(values_at(i), weight_ref[slot])

    def careful(r, i):
        scores = dot(keys_at(i), qt_ref[r]) * SCALE
        visible = visible_at(r, i)
        scores = jnp.where(visible, scores, LOW)
        old = top_ref[r, :1]
        new = jnp.maximum(old, jnp.max(scores, axis=0, keepdims=True))
        weights = jnp.where(visible, jnp.exp(scores - new), 0.0).astype(jnp.bfloat16)
        acc_ref[r] = acc_ref[r] * jnp.exp(old - new) + dot(values_at(i), weights)
        top_ref[r] = jnp.broadcast_to(new, top_ref.shape[1:])

    def count(r):
        return info_ref[3 + r]

    plain = info_ref[3 + blocks + head] == 1

    @pl.when(plain)
    def _():
        def following(item):
            r, i = item
            over = i + 1 >= count(jnp.minimum(r, blocks - 1))
            over = jnp.logical_or(over, r >= blocks)
            return jnp.where(over, jnp.minimum(r + 1, blocks), r), jnp.where(over, 0, i + 1)

        def run(item):
            items = [item]
            for _ in range(ITEMS - 1):
                items.append(following(items[-1]))
            return tuple(items)

        def step(_, items):
            later = run(following(items[-1]))
            for slot in range(ITEMS):
                absorb(slot, *items[slot])
                weigh(slot, *later[slot])
            return later

        items = run((jnp.int32(0), jnp.int32(0)))
        for slot in range(ITEMS):
            weigh(slot, *items[slot])
        total = sum(count(r) for r in range(blocks))
        items = lax.fori_loop(0, (total + ITEMS - 1) // ITEMS - 1, step, items)
        for slot in range(ITEMS):
            absorb(slot, *items[slot])

    @pl.when(jnp.logical_not(plain))
    def _():
        top_ref[...] = jnp.full_like(top_ref, LOW)

        def over_block(r, carry):
            def over_chunk(i, carry):
                careful(r, i)
                return carry

            return lax.fori_loop(0, count(r), over_chunk, carry)

        lax.fori_loop(0, blocks, over_block, 0)

    for zone in range(ZONES):
        for out, half in ((own_out, side), (their_out, 1 - side)):
            r = 2 * zone + half
            acc = acc_ref[r]
            total = acc[HEAD_DIM : HEAD_DIM + 1]
            some = total > 0.0
            safe = jnp.where(some, total, 1.0)
            mean = (acc[:HEAD_DIM] * jnp.where(some, 1.0 / safe, 0.0)).T
            level = jnp.where(some, top_ref[r, :1] + jnp.log(safe), LOW)
            level = jnp.concatenate([level[:, :HEAD_DIM], level[:, HEAD_DIM:]], axis=0)
            high = level.astype(jnp.bfloat16).astype(jnp.float32)
            middle = (level - high).astype(jnp.bfloat16).astype(jnp.float32)
            low = level - high - middle
            spare = jnp.zeros((NOTE - 6, HEAD_DIM), jnp.float32)
            out[zone, :SEGMENT, :] = mean.astype(jnp.bfloat16)
            out[zone, SEGMENT:, :] = jnp.concatenate([high, middle, low, spare]).astype(jnp.bfloat16)


def attend(info, own_q, their_q, ends, sources, head):
    rows = 2 * ZONES * SEGMENT
    tokens = 2 * ZONES * WIDE
    blocks = 2 * ZONES
    out = jax.ShapeDtypeStruct((ZONES, SEGMENT + NOTE, HEAD_DIM), jnp.bfloat16)
    q_spec = pl.BlockSpec((ZONES, SEGMENT, HEAD_DIM), lambda i, *_: (0, 0, head))
    whole = pl.BlockSpec(memory_space=pltpu.VMEM)
    return pl.pallas_call(
        functools.partial(attend_kernel, head, len(sources) > 1),
        grid_spec=pltpu.PrefetchScalarGridSpec(
            num_scalar_prefetch=1,
            grid=(1,),
            in_specs=[q_spec, q_spec, whole] + [pl.BlockSpec(memory_space=pl.ANY)] * len(sources),
            out_specs=[whole, whole],
            scratch_shapes=[
                pltpu.VMEM((4, 2, ZONES, 2, 2 * HEAD_DIM, HEAD_DIM), jnp.bfloat16),
                pltpu.VMEM((blocks, HEAD_DIM, SEGMENT), jnp.bfloat16),
                pltpu.VMEM((ITEMS, WIDTH, SEGMENT), jnp.bfloat16),
                pltpu.VMEM((blocks + 1, HEAD_DIM + NOTE, SEGMENT), jnp.float32),
                pltpu.VMEM((blocks, 8, SEGMENT), jnp.float32),
                pltpu.SemaphoreType.DMA((8,)),
            ],
        ),
        out_shape=[out, out],
        compiler_params=pltpu.CompilerParams(vmem_limit_bytes=58 << 20),
        cost_estimate=pl.CostEstimate(
            flops=4 * rows * tokens * HEAD_DIM,
            bytes_accessed=4 * tokens * HEAD_DIM + 4 * rows * HEAD_DIM,
            transcendentals=rows * tokens // 2,
        ),
    )(info, own_q, their_q, ends, *sources)


def pack_first_kernel(queries_ref, keys_ref, values_ref, ids_ref, out_ref):
    groups = out_ref.shape[0]
    heads = keys_ref.shape[1] // HEAD_DIM // groups
    ids = jnp.broadcast_to(ids_ref[...].astype(jnp.float32), (HEAD_DIM, HEAD_DIM)).T
    lane = lax.broadcasted_iota(jnp.int32, (HEAD_DIM, HEAD_DIM), 1)
    counts = jnp.sum(jnp.where(ids <= lane.astype(jnp.float32), 1.0, 0.0), axis=0, keepdims=True)
    ones = jnp.ones((HEAD_DIM, HEAD_DIM), jnp.bfloat16)
    lane = lane[:1]
    for g in range(groups):
        at = slice(g * heads * HEAD_DIM, (g * heads + 1) * HEAD_DIM)
        out_ref[g, :HEAD_DIM] = keys_ref[:, at]
        out_ref[g, HEAD_DIM : 2 * HEAD_DIM] = values_ref[:, at].T
        note = counts
        for first, ref in ((K_NORM, keys_ref), (Q_NORM, queries_ref)):
            for head in range(heads):
                start = (g * heads + head) * HEAD_DIM
                rows = ref[:, start : start + HEAD_DIM].astype(jnp.float32)
                norm = jnp.max(dot((rows * rows).astype(jnp.bfloat16), ones), axis=0, keepdims=True)
                note = jnp.where(lane == first + head, norm * 1.02, note)
        out_ref[g, 2 * HEAD_DIM :] = jnp.broadcast_to(note, (NOTE, HEAD_DIM)).astype(jnp.bfloat16)


def pack_rest_kernel(keys_ref, values_ref, queries_ref, one_ref, two_ref, q_ref):
    groups = q_ref.shape[0]
    local = q_ref.shape[2]
    for g in range(groups):
        q_ref[g] = queries_ref[:, g * local : (g + 1) * local]
        for head, out_ref in ((1, one_ref), (2, two_ref)):
            start = g * local + head * HEAD_DIM
            out_ref[g, :HEAD_DIM] = keys_ref[:, start : start + HEAD_DIM]
            out_ref[g, HEAD_DIM:] = values_ref[:, start : start + HEAD_DIM].T


def packed(groups, rows, columns):
    return jax.ShapeDtypeStruct((groups, rows, columns), jnp.bfloat16)


def pack_first(queries, keys, values, span_ids, groups):
    return pl.pallas_call(
        pack_first_kernel, out_shape=packed(groups, 2 * HEAD_DIM + NOTE, HEAD_DIM)
    )(queries, keys, values, span_ids.reshape(1, -1))


def pack_rest(keys, values, queries, groups):
    chunk, width = keys.shape
    pair = packed(groups, 2 * HEAD_DIM, HEAD_DIM)
    return pl.pallas_call(
        pack_rest_kernel, out_shape=[pair, pair, packed(groups, chunk, width // groups)]
    )(keys, values, queries)


def merge_kernel(*refs):
    out = refs[-1]
    pieces = SEGMENT // HEAD_DIM

    def level(note, j):
        parts = [note[k * pieces + j : k * pieces + j + 1] for k in range(3)]
        return parts[0] + parts[1] + parts[2]

    for head in range(len(refs) // 2):
        one, two = refs[2 * head], refs[2 * head + 1]
        for zone in range(ZONES):
            note_one = one[zone, SEGMENT:, :].astype(jnp.float32)
            note_two = two[zone, SEGMENT:, :].astype(jnp.float32)
            for j in range(pieces):
                at = slice(j * HEAD_DIM, (j + 1) * HEAD_DIM)
                share = 1.0 / (1.0 + jnp.exp(level(note_two, j) - level(note_one, j)))
                share = jnp.broadcast_to(share, (HEAD_DIM, HEAD_DIM)).T
                a, b = one[zone, at, :].astype(jnp.float32), two[zone, at, :].astype(jnp.float32)
                merged = (b + (a - b) * share).astype(jnp.bfloat16)
                out[zone * pieces + j, :, head * HEAD_DIM : (head + 1) * HEAD_DIM] = merged


def merge(parts):
    heads = len(parts) // 2
    shape = (ZONES * SEGMENT // HEAD_DIM, HEAD_DIM, heads * HEAD_DIM)
    return pl.pallas_call(merge_kernel, out_shape=jax.ShapeDtypeStruct(shape, jnp.bfloat16))(*parts)


def gate_kernel(gate_ref, mixed_ref, out_ref):
    groups, _, local = mixed_ref.shape
    for g in range(groups):
        at = slice(g * local, (g + 1) * local)
        out_ref[:, at] = (gate_ref[:, at] * mixed_ref[g].astype(jnp.float32)).astype(jnp.bfloat16)


def gate_rows(span_ids, timesteps, time_weight):
    half = time_weight.shape[0] // 2
    freqs = jnp.exp(-math.log(10000.0) * jnp.arange(half, dtype=jnp.float32) / half)
    angles = timesteps.astype(jnp.float32)[:, None] * freqs[None, :]
    embed = jnp.concatenate([jnp.cos(angles), jnp.sin(angles)], axis=1).astype(jnp.bfloat16)
    gate_table = jnp.dot(embed, time_weight, preferred_element_type=jnp.float32)
    onehot = (span_ids[:, None] == jnp.arange(timesteps.shape[0], dtype=jnp.int32)[None, :]).astype(
        jnp.float32
    )
    return jnp.dot(onehot, gate_table, precision=lax.Precision.HIGHEST)


def per_device(queries, keys, values, span_ids, timesteps, time_weight):
    runs, groups = lax.axis_size("span"), lax.axis_size("head")
    run, rank = lax.axis_index("span"), lax.axis_index("head")
    spans = timesteps.shape[0]
    chunk, width = queries.shape
    local = width // groups
    heads = local // HEAD_DIM

    across = [
        [(4 * z + xc) * groups + 2 * y + x for z in range(ZONES) for x in range(2)]
        for xc in range(4)
        for y in range(4)
    ]
    along_y = [
        [(4 * z + 2 * side + c) * groups + 2 * y + x for y in range(4) for c in range(2)]
        for z in range(ZONES)
        for side in range(2)
        for x in range(2)
    ]
    up = [(h, (h + 2) % groups) for h in range(groups)]
    down = [(h, (h - 2) % groups) for h in range(groups)]
    core_swap = [(s, s ^ 1) for s in range(runs)]
    partner = [(s, s ^ 2) for s in range(runs)]
    other = [(s, s ^ 3) for s in range(runs)]

    def exchange(parts):
        return lax.all_to_all(
            parts, BOTH, split_axis=0, concat_axis=0, axis_index_groups=across, tiled=True
        )

    def after(*values):
        return lax.optimization_barrier(values)

    def sides(block):
        return lax.ppermute(block, "head", up), lax.ppermute(block, "head", down)

    def opposite(below, above):
        half = below.shape[0] // 2
        return lax.ppermute(below[:half], "head", up), lax.ppermute(above[half:], "head", down)

    def zoned(block):
        return block.reshape((-1, ZONES, 2) + block.shape[1:])

    def swapped(block):
        return [block, lax.ppermute(block, "span", core_swap)]

    block = exchange(pack_first(queries, keys, values, span_ids, groups))
    below, above = sides(block)
    queries, block = after(queries, block)
    one, two, split_q = pack_rest(keys, values, queries, groups)
    block_one = exchange(one)
    split_q, block_one, below, above = after(split_q, block_one, below, above)
    last = zoned(jnp.concatenate(opposite(below, above)))
    near = zoned(jnp.concatenate([block, above, below]))
    own_q = exchange(split_q)
    two, own_q = after(two, own_q)
    block_two = exchange(two)
    own_q = own_q.reshape(ZONES, SEGMENT, local)
    their_q = lax.ppermute(own_q, "span", partner)
    gathered = [
        lax.all_gather(x, BOTH, axis_index_groups=along_y, axis=0, tiled=True)
        for x in (block_one, block_two)
    ]
    gathered = [x.reshape(4, 2, ZONES, 2, 2 * HEAD_DIM, HEAD_DIM) for x in gathered]

    def combined(notes):
        is_count = jnp.arange(HEAD_DIM) < K_NORM
        return jnp.where(is_count, jnp.sum(notes, axis=0), jnp.max(notes, axis=0))

    notes = jnp.concatenate([x[:, :, :, 2 * HEAD_DIM].reshape(-1, HEAD_DIM) for x in (near, last)])
    note = combined(notes.astype(jnp.float32))[None]
    notes = [note] + [lax.ppermute(note, "span", move) for move in (core_swap, partner, other)]
    note = combined(jnp.concatenate(notes))
    squares = note[K_NORM : K_NORM + heads] * note[Q_NORM : Q_NORM + heads]
    plain = (squares * (1.05 * SCALE**2) < PLAIN_LIMIT**2).astype(jnp.int32)
    ends = note[:spans].astype(jnp.int32)

    core, side = run % 2, (run // 2) % 2
    zone_start = jnp.arange(ZONES)[:, None, None] * 4096
    inside = core * 1024 + (rank // 2) * SEGMENT + jnp.arange(SEGMENT)[None, None, :]
    position = zone_start + jnp.arange(2)[None, :, None] * 2048 + inside
    reach = jnp.min(
        jnp.where(ends > position[..., None], ends, runs * groups * chunk), axis=3
    )
    starts = (jnp.arange(ZONES)[:, None] * 4096 + side * 2048 + jnp.arange(2)[None, :] * 1024).reshape(-1)
    seen = jnp.sum(jnp.clip(reach[..., None] - starts, 0, 1024), axis=3).astype(jnp.int32)
    counts = jnp.maximum((seen[:, :, -1].reshape(-1) + WIDTH - 1) // WIDTH, 1)
    info = jnp.concatenate([jnp.stack([core, rank // 2, side]), counts, plain]).astype(jnp.int32)
    seen = seen.reshape(2 * ZONES, 1, SEGMENT)

    (near, near_other), (last, last_other) = swapped(near), swapped(last)
    sources = [(near, last, near_other, last_other), (gathered[0],), (gathered[1],)]
    info, block_two = after(info, block_two)
    parts = []
    for head in range(heads):
        mine, theirs = attend(info, own_q, their_q, seen, sources[head], head)
        info, theirs = after(info, theirs)
        parts += [mine, lax.ppermute(theirs, "span", partner)]
    mixed = exchange(merge(parts))
    gates = gate_rows(span_ids, timesteps, time_weight)
    return pl.pallas_call(
        gate_kernel, out_shape=jax.ShapeDtypeStruct((chunk, width), jnp.bfloat16)
    )(gates, mixed)


def solution(mesh):
    return jax.shard_map(
        per_device,
        mesh=mesh,
        in_specs=(
            P(("span", "head"), None),
            P(("span", "head"), None),
            P(("span", "head"), None),
            P(("span", "head")),
            P(),
            P(),
        ),
        out_specs=P(("span", "head"), None),
        check_vma=False,
    )
```

```python
import functools
import math

import jax
import jax.numpy as jnp
from jax import lax
from jax.experimental import pallas as pl
from jax.experimental.pallas import tpu as pltpu
from jax.sharding import PartitionSpec as P

HEAD_DIM = 128
SCALE = HEAD_DIM**-0.5
SCALE_LOG2 = SCALE * math.log2(math.e)
BOTH = ("span", "head")
ZONES = 8
SEGMENT = 2 * HEAD_DIM
KEYS = 8192
WIDTH = 512
ITEMS = 4
K_NORM, Q_NORM = 32, 40
NOTE = 16
PLAIN_LIMIT = 70.0
LOW = -1e30


def dot(a, b):
    return jnp.dot(a, b, preferred_element_type=jnp.float32)


def attend_kernel(head, ringed, info_ref, own_q, their_q, end_ref, *refs):
    sources, refs = refs[: 4 if ringed else 1], refs[4 if ringed else 1 :]
    own_out, their_out, kv_ref, qt_ref, weight_ref, acc_ref, top_ref, sems = refs
    core, rank = info_ref[0], info_ref[1]
    blocks = ZONES

    copies = []
    if ringed:
        near, near_last, far, far_last = sources
        for j, (src, last, c) in enumerate(((near, near_last, core), (far, far_last, 1 - core))):
            pieces = [(src.at[0], 0), (src.at[1], 1), (last.at[0], 2), (src.at[2], 3)]
            for piece, step in pieces:
                copies.append(
                    pltpu.make_async_copy(
                        piece, kv_ref.at[(rank + step) % 4, c], sems.at[4 * j + step]
                    )
                )
    else:
        whole = sources[0].at[:, :, :, pl.ds(0, 2 * HEAD_DIM)]
        copies.append(pltpu.make_async_copy(whole, kv_ref, sems.at[0]))
    for copy in copies:
        copy.start()

    for zone in range(ZONES):
        qt_ref[zone] = jnp.concatenate([own_q[zone], their_q[zone]], axis=1)
    acc_ref[...] = jnp.zeros_like(acc_ref)
    top_ref[...] = jnp.zeros_like(top_ref)
    ones = jnp.ones((NOTE, WIDTH), jnp.bfloat16)
    for copy in copies:
        copy.wait()

    def part(i, rows):
        return kv_ref[:, i % 2, i // 2, rows]

    def keys_at(i):
        return part(i, slice(0, HEAD_DIM)).reshape(WIDTH, HEAD_DIM)

    def values_at(i):
        block = part(i, slice(HEAD_DIM, 2 * HEAD_DIM))
        block = jnp.concatenate([block[y] for y in range(4)], axis=1)
        return jnp.concatenate([block, ones], axis=0)

    def visible_at(r, i):
        row = lax.broadcasted_iota(jnp.int32, (WIDTH, SEGMENT), 0)
        return row < end_ref[r] - i * WIDTH

    def weigh(slot, r, i):
        r = jnp.minimum(r, blocks - 1)
        weights = jnp.exp2(dot(keys_at(i), qt_ref[r]) * SCALE_LOG2)
        weights = jnp.where(visible_at(r, i), weights, 0.0)
        weight_ref[slot] = weights.astype(jnp.bfloat16)

    def absorb(slot, r, i):
        acc_ref[r] += dot(values_at(i), weight_ref[slot])

    def careful(r, i):
        scores = dot(keys_at(i), qt_ref[r]) * SCALE_LOG2
        visible = visible_at(r, i)
        scores = jnp.where(visible, scores, LOW)
        old = top_ref[r, :1]
        new = jnp.maximum(old, jnp.max(scores, axis=0, keepdims=True))
        weights = jnp.where(visible, jnp.exp2(scores - new), 0.0).astype(jnp.bfloat16)
        acc_ref[r] = acc_ref[r] * jnp.exp2(old - new) + dot(values_at(i), weights)
        top_ref[r] = jnp.broadcast_to(new, top_ref.shape[1:])

    def count(r):
        return info_ref[2 + r]

    plain = info_ref[2 + blocks + head] == 1

    @pl.when(plain)
    def _():
        def following(item):
            r, i = item
            over = i + 1 >= count(jnp.minimum(r, blocks - 1))
            over = jnp.logical_or(over, r >= blocks)
            return jnp.where(over, jnp.minimum(r + 1, blocks), r), jnp.where(over, 0, i + 1)

        def run(item):
            items = [item]
            for _ in range(ITEMS - 1):
                items.append(following(items[-1]))
            return tuple(items)

        def step(_, items):
            later = run(following(items[-1]))
            for slot in range(ITEMS):
                absorb(slot, *items[slot])
                weigh(slot, *later[slot])
            return later

        items = run((jnp.int32(0), jnp.int32(0)))
        for slot in range(ITEMS):
            weigh(slot, *items[slot])
        total = sum(count(r) for r in range(blocks))
        items = lax.fori_loop(0, (total + ITEMS - 1) // ITEMS - 1, step, items)
        for slot in range(ITEMS):
            absorb(slot, *items[slot])

    @pl.when(jnp.logical_not(plain))
    def _():
        top_ref[...] = jnp.full_like(top_ref, LOW)

        def over_block(r, carry):
            def over_chunk(i, carry):
                careful(r, i)
                return carry

            return lax.fori_loop(0, count(r), over_chunk, carry)

        lax.fori_loop(0, blocks, over_block, 0)

    for r in range(blocks):
        acc = acc_ref[r]
        total = acc[HEAD_DIM : HEAD_DIM + 1]
        some = total > 0.0
        safe = jnp.where(some, total, 1.0)
        mean = (acc[:HEAD_DIM] * jnp.where(some, 1.0 / safe, 0.0)).astype(jnp.bfloat16)
        level = jnp.where(some, top_ref[r, :1] + jnp.log2(safe), LOW)
        high = level.astype(jnp.bfloat16).astype(jnp.float32)
        middle = (level - high).astype(jnp.bfloat16).astype(jnp.float32)
        low = level - high - middle
        spare = jnp.zeros((NOTE - 3, SEGMENT), jnp.float32)
        note = jnp.concatenate([high, middle, low, spare]).astype(jnp.bfloat16)
        for out, at in ((own_out, slice(0, HEAD_DIM)), (their_out, slice(HEAD_DIM, SEGMENT))):
            out[r, :HEAD_DIM, :] = mean[:, at]
            out[r, HEAD_DIM:, :] = note[:, at]


def attend(info, own_q, their_q, ends, sources, head):
    rows = ZONES * SEGMENT
    out = jax.ShapeDtypeStruct((ZONES, HEAD_DIM + NOTE, HEAD_DIM), jnp.bfloat16)
    first = own_q.shape[1] // HEAD_DIM - 3
    own_spec = pl.BlockSpec((ZONES, HEAD_DIM, HEAD_DIM), lambda i, *_: (0, first + head, 0))
    whole = pl.BlockSpec(memory_space=pltpu.VMEM)
    return pl.pallas_call(
        functools.partial(attend_kernel, head, len(sources) > 1),
        grid_spec=pltpu.PrefetchScalarGridSpec(
            num_scalar_prefetch=1,
            grid=(1,),
            in_specs=[own_spec, whole, whole]
            + [pl.BlockSpec(memory_space=pl.ANY)] * len(sources),
            out_specs=[whole, whole],
            scratch_shapes=[
                pltpu.VMEM((4, 2, ZONES, 2 * HEAD_DIM, HEAD_DIM), jnp.bfloat16),
                pltpu.VMEM((ZONES, HEAD_DIM, SEGMENT), jnp.bfloat16),
                pltpu.VMEM((ITEMS, WIDTH, SEGMENT), jnp.bfloat16),
                pltpu.VMEM((ZONES + 1, HEAD_DIM + NOTE, SEGMENT), jnp.float32),
                pltpu.VMEM((ZONES, 8, SEGMENT), jnp.float32),
                pltpu.SemaphoreType.DMA((8,)),
            ],
        ),
        out_shape=[out, out],
        compiler_params=pltpu.CompilerParams(vmem_limit_bytes=58 << 20),
        cost_estimate=pl.CostEstimate(
            flops=4 * rows * KEYS * HEAD_DIM,
            bytes_accessed=4 * KEYS * HEAD_DIM + 4 * rows * HEAD_DIM,
            transcendentals=rows * KEYS // 2,
        ),
    )(info, own_q, their_q, ends, *sources)


def pack_first_kernel(head, queries_ref, keys_ref, values_ref, ids_ref, out_ref):
    groups = out_ref.shape[0]
    heads = keys_ref.shape[1] // HEAD_DIM // groups
    ids = jnp.broadcast_to(ids_ref[...].astype(jnp.float32), (HEAD_DIM, HEAD_DIM)).T
    lane = lax.broadcasted_iota(jnp.int32, (HEAD_DIM, HEAD_DIM), 1)
    counts = jnp.sum(jnp.where(ids <= lane.astype(jnp.float32), 1.0, 0.0), axis=0, keepdims=True)
    ones = jnp.ones((HEAD_DIM, HEAD_DIM), jnp.bfloat16)
    lane = lane[:1]
    for g in range(groups):
        at = slice((g * heads + head) * HEAD_DIM, (g * heads + head + 1) * HEAD_DIM)
        out_ref[g, :HEAD_DIM] = keys_ref[:, at]
        out_ref[g, HEAD_DIM : 2 * HEAD_DIM] = values_ref[:, at].T
        note = counts
        for first, ref in ((K_NORM, keys_ref), (Q_NORM, queries_ref)):
            for h in range(heads):
                start = (g * heads + h) * HEAD_DIM
                rows = ref[:, start : start + HEAD_DIM].astype(jnp.float32)
                norm = jnp.max(dot((rows * rows).astype(jnp.bfloat16), ones), axis=0, keepdims=True)
                note = jnp.where(lane == first + h, norm * 1.02, note)
        out_ref[g, 2 * HEAD_DIM :] = jnp.broadcast_to(note, (NOTE, HEAD_DIM)).astype(jnp.bfloat16)


def pack_rest_kernel(others, queries_ref, keys_ref, values_ref, out_ref):
    groups = out_ref.shape[0]
    heads = keys_ref.shape[1] // HEAD_DIM // groups
    for g in range(groups):
        parts = [p for head in others for p in ((keys_ref, head, False), (values_ref, head, True))]
        parts += [(queries_ref, head, True) for head in range(heads)]
        for j, (ref, head, turn) in enumerate(parts):
            at = slice((g * heads + head) * HEAD_DIM, (g * heads + head + 1) * HEAD_DIM)
            out_ref[g, j * HEAD_DIM : (j + 1) * HEAD_DIM] = ref[:, at].T if turn else ref[:, at]


def pack(kernel, rows, *args):
    return pl.pallas_call(
        kernel, out_shape=jax.ShapeDtypeStruct((ZONES, rows, HEAD_DIM), jnp.bfloat16)
    )(*args)


def merge_kernel(*refs):
    out = refs[-1]

    def level(ref, zone):
        note = ref[zone, HEAD_DIM:, :].astype(jnp.float32)
        return note[0:1] + note[1:2] + note[2:3]

    for head in range(len(refs) // 2):
        one, two = refs[2 * head], refs[2 * head + 1]
        at = slice(head * HEAD_DIM, (head + 1) * HEAD_DIM)
        for zone in range(ZONES):
            share = 1.0 / (1.0 + jnp.exp2(level(two, zone) - level(one, zone)))
            a, b = (ref[zone, :HEAD_DIM, :].astype(jnp.float32) for ref in (one, two))
            out[zone, at, :] = (b + (a - b) * share).astype(jnp.bfloat16)


def merge(parts):
    return pack(merge_kernel, len(parts) // 2 * HEAD_DIM, *parts)


def gate_kernel(gate_ref, mixed_ref, out_ref):
    groups, local, _ = mixed_ref.shape
    for g in range(groups):
        for h in range(0, local, HEAD_DIM):
            at = slice(g * local + h, g * local + h + HEAD_DIM)
            attended = mixed_ref[g, h : h + HEAD_DIM, :].T.astype(jnp.float32)
            out_ref[:, at] = (gate_ref[:, at] * attended).astype(jnp.bfloat16)


def gate_rows(span_ids, timesteps, time_weight):
    half = time_weight.shape[0] // 2
    freqs = jnp.exp(-math.log(10000.0) * jnp.arange(half, dtype=jnp.float32) / half)
    angles = timesteps.astype(jnp.float32)[:, None] * freqs[None, :]
    embed = jnp.concatenate([jnp.cos(angles), jnp.sin(angles)], axis=1).astype(jnp.bfloat16)
    gate_table = jnp.dot(embed, time_weight, preferred_element_type=jnp.float32)
    onehot = (span_ids[:, None] == jnp.arange(timesteps.shape[0], dtype=jnp.int32)[None, :]).astype(
        jnp.float32
    )
    return jnp.dot(onehot, gate_table, precision=lax.Precision.HIGHEST)


def per_device(queries, keys, values, span_ids, timesteps, time_weight):
    runs, groups = lax.axis_size("span"), lax.axis_size("head")
    run, rank = lax.axis_index("span"), lax.axis_index("head")
    spans = timesteps.shape[0]
    chunk, width = queries.shape
    local = width // groups
    heads = local // HEAD_DIM

    def device(zone, core, y, x):
        return (2 * zone + core) * groups + 2 * y + x

    across = [
        [device(zone, core, y, x) for zone in range(ZONES)]
        for core in range(2)
        for y in range(4)
        for x in range(2)
    ]
    along_y = [
        [device(zone, core, y, x) for y in range(4) for core in range(2)]
        for zone in range(ZONES)
        for x in range(2)
    ]
    up = [(h, (h + 2) % groups) for h in range(groups)]
    down = [(h, (h - 2) % groups) for h in range(groups)]
    core_swap = [(s, s ^ 1) for s in range(runs)]
    partner = [(h, h ^ 1) for h in range(groups)]

    def exchange(parts):
        return lax.all_to_all(
            parts, BOTH, split_axis=0, concat_axis=0, axis_index_groups=across, tiled=True
        )

    def gather(block):
        block = lax.all_gather(block, BOTH, axis_index_groups=along_y, axis=0, tiled=True)
        return block.reshape(4, 2, ZONES, -1, HEAD_DIM)

    def after(*values):
        return lax.optimization_barrier(values)

    def swapped(block):
        return block, lax.ppermute(block, "span", core_swap)

    pair = 2 * HEAD_DIM
    note_rows = span_ids.reshape(1, -1)
    first = pack(
        functools.partial(pack_first_kernel, 1), pair + NOTE, queries, keys, values, note_rows
    )
    first = exchange(first)
    queries, first = after(queries, first)
    rest = pack(
        functools.partial(pack_rest_kernel, (0, 2)), 2 * pair + local, queries, keys, values
    )
    rest = exchange(rest)
    gathered = gather(first)
    block = rest[:, :pair]
    half = ZONES // 2
    below, above = lax.ppermute(block, "head", up), lax.ppermute(block, "head", down)
    their_q = [None] * heads
    for head in (1, 0, 2):
        start = 2 * pair + head * HEAD_DIM
        their_q[head] = lax.ppermute(rest[:, start : start + HEAD_DIM], "head", partner)

    def combined(notes):
        is_count = jnp.arange(HEAD_DIM) < K_NORM
        return jnp.where(is_count, jnp.sum(notes, axis=0), jnp.max(notes, axis=0))

    note = combined(gathered[:, :, :, pair].reshape(-1, HEAD_DIM).astype(jnp.float32))[None]
    note = combined(jnp.concatenate([note, lax.ppermute(note, "head", partner)]))
    squares = note[K_NORM : K_NORM + heads] * note[Q_NORM : Q_NORM + heads]
    plain = (squares * (1.05 * SCALE**2) < PLAIN_LIMIT**2).astype(jnp.int32)
    ends = note[:spans].astype(jnp.int32)

    core, y, side = run % 2, rank // 2, rank % 2
    sides = jnp.stack([side, 1 - side])[None, :, None] * HEAD_DIM
    position = jnp.arange(ZONES)[:, None, None] * 2048 + sides + jnp.arange(HEAD_DIM)[None, None, :]
    position = (position + (core * 1024 + y * SEGMENT)).reshape(ZONES, SEGMENT)
    reach = jnp.min(
        jnp.where(ends > position[..., None], ends, runs * groups * chunk), axis=2
    )
    reach = jnp.maximum(reach - side * HEAD_DIM, 0)
    seen = (reach // SEGMENT) * HEAD_DIM + jnp.minimum(reach % SEGMENT, HEAD_DIM)
    seen = seen.astype(jnp.int32)
    counts = jnp.maximum((jnp.max(seen, axis=1) + WIDTH - 1) // WIDTH, 1)
    info = jnp.concatenate([jnp.stack([core, y]), counts, plain]).astype(jnp.int32)
    seen = seen.reshape(ZONES, 1, SEGMENT)

    parts = [None] * (2 * heads)

    def attended(info, head, sources):
        parts[2 * head], theirs = attend(info, rest, their_q[head], seen, sources, head)
        info, theirs = after(info, theirs)
        parts[2 * head + 1] = lax.ppermute(theirs, "head", partner)
        return info

    info, below, above = after(info, below, above)
    pieces = [lax.ppermute(below[:half], "head", up), lax.ppermute(above[half:], "head", down)]
    near, far = swapped(jnp.stack([block, above, below]))
    info = attended(info, 1, (gathered,))
    info, *pieces = after(info, *pieces)
    near_last, far_last = swapped(jnp.concatenate(pieces)[None])
    info = attended(info, 0, (near, near_last, far, far_last))
    info = attended(info, 2, (gather(rest[:, pair : 2 * pair]),))
    mixed = exchange(merge(parts))
    gates = gate_rows(span_ids, timesteps, time_weight)
    return pl.pallas_call(
        gate_kernel, out_shape=jax.ShapeDtypeStruct((chunk, width), jnp.bfloat16)
    )(gates, mixed)


def solution(mesh):
    return jax.shard_map(
        per_device,
        mesh=mesh,
        in_specs=(
            P(("span", "head"), None),
            P(("span", "head"), None),
            P(("span", "head"), None),
            P(("span", "head")),
            P(),
            P(),
        ),
        out_specs=P(("span", "head"), None),
        check_vma=False,
    )
```

```python
import functools
import math

import jax
import jax.numpy as jnp
from jax import lax
from jax.experimental import pallas as pl
from jax.experimental.pallas import tpu as pltpu
from jax.sharding import PartitionSpec as P

HEAD_DIM = 128
SCALE = HEAD_DIM**-0.5
SCALE_LOG2 = SCALE * math.log2(math.e)
BOTH = ("span", "head")
ZONES = 8
SEGMENT = 2 * HEAD_DIM
KEYS = 8192
WIDTH = 512
SUB = 256
ITEMS = 4
K_NORM, Q_NORM = 32, 40
NOTE = 16
PLAIN_LIMIT = 70.0
LOW = -1e30


def dot(a, b):
    return jnp.dot(a, b, preferred_element_type=jnp.float32)


def attend_kernel(head, ringed, info_ref, own_q, their_q, end_ref, *refs):
    sources, refs = refs[: 4 if ringed else 1], refs[4 if ringed else 1 :]
    own_out, their_out, kv_ref, qt_ref, weight_ref, acc_ref, top_ref, sems = refs
    core, rank = info_ref[0], info_ref[1]
    blocks = ZONES

    copies = []
    if ringed:
        near, near_last, far, far_last = sources
        for j, (src, last, c) in enumerate(((near, near_last, core), (far, far_last, 1 - core))):
            pieces = [(src.at[0], 0), (src.at[1], 1), (last.at[0], 2), (src.at[2], 3)]
            for piece, step in pieces:
                copies.append(
                    pltpu.make_async_copy(
                        piece, kv_ref.at[(rank + step) % 4, c], sems.at[4 * j + step]
                    )
                )
    else:
        whole = sources[0].at[:, :, :, pl.ds(0, 2 * HEAD_DIM)]
        copies.append(pltpu.make_async_copy(whole, kv_ref, sems.at[0]))
    for copy in copies:
        copy.start()

    for zone in range(ZONES):
        qt_ref[zone] = jnp.concatenate([own_q[zone], their_q[zone]], axis=1)
    acc_ref[...] = jnp.zeros_like(acc_ref)
    top_ref[...] = jnp.zeros_like(top_ref)
    ones = jnp.ones((NOTE, WIDTH), jnp.bfloat16)
    for copy in copies:
        copy.wait()

    def part(i, rows):
        return kv_ref[:, i % 2, i // 2, rows]

    def keys_at(i):
        return part(i, slice(0, HEAD_DIM)).reshape(WIDTH, HEAD_DIM)

    def values_at(i):
        block = part(i, slice(HEAD_DIM, 2 * HEAD_DIM))
        block = jnp.concatenate([block[y] for y in range(4)], axis=1)
        return jnp.concatenate([block, ones], axis=0)

    def visible_at(r, i):
        row = lax.broadcasted_iota(jnp.int32, (WIDTH, SEGMENT), 0)
        return row < end_ref[r] - i * WIDTH

    def score(item, half):
        r, i = item
        keys = kv_ref[2 * half : 2 * half + 2, i % 2, i // 2, :HEAD_DIM].reshape(SUB, HEAD_DIM)
        return dot(keys, qt_ref[jnp.minimum(r, blocks - 1)])

    def weigh(slot, item, half, scores):
        r, i = item
        row = lax.broadcasted_iota(jnp.int32, (SUB, SEGMENT), 0)
        visible = row < end_ref[jnp.minimum(r, blocks - 1)] - (i * WIDTH + half * SUB)
        weights = jnp.where(visible, jnp.exp2(scores * SCALE_LOG2), 0.0)
        weight_ref[slot, half * SUB : (half + 1) * SUB] = weights.astype(jnp.bfloat16)

    def absorb(slot, item, half):
        r, i = item
        block = kv_ref[2 * half : 2 * half + 2, i % 2, i // 2, HEAD_DIM:]
        values = jnp.concatenate([jnp.concatenate([block[0], block[1]], axis=1), ones[:, :SUB]], axis=0)
        acc_ref[r] += dot(values, weight_ref[slot, half * SUB : (half + 1) * SUB])

    def careful(r, i):
        scores = dot(keys_at(i), qt_ref[r]) * SCALE_LOG2
        visible = visible_at(r, i)
        scores = jnp.where(visible, scores, LOW)
        old = top_ref[r, :1]
        new = jnp.maximum(old, jnp.max(scores, axis=0, keepdims=True))
        weights = jnp.where(visible, jnp.exp2(scores - new), 0.0).astype(jnp.bfloat16)
        acc_ref[r] = acc_ref[r] * jnp.exp2(old - new) + dot(values_at(i), weights)
        top_ref[r] = jnp.broadcast_to(new, top_ref.shape[1:])

    def count(r):
        return info_ref[2 + r]

    parts = [(slot, half) for slot in range(ITEMS) for half in range(2)]
    plain = info_ref[2 + blocks + head] == 1

    @pl.when(plain)
    def _():
        def following(item):
            r, i = item
            over = i + 1 >= count(jnp.minimum(r, blocks - 1))
            over = jnp.logical_or(over, r >= blocks)
            return jnp.where(over, jnp.minimum(r + 1, blocks), r), jnp.where(over, 0, i + 1)

        def run(item):
            items = [item]
            for _ in range(ITEMS - 1):
                items.append(following(items[-1]))
            return tuple(items)

        def step(_, items):
            later = run(following(items[-1]))
            scores = score(later[0], 0)
            for slot, half in parts:
                now = scores
                if (slot, half) != parts[-1]:
                    scores = score(later[slot + half], 1 - half)
                absorb(slot, items[slot], half)
                weigh(slot, later[slot], half, now)
            return later

        items = run((jnp.int32(0), jnp.int32(0)))
        for slot, half in parts:
            weigh(slot, items[slot], half, score(items[slot], half))
        total = sum(count(r) for r in range(blocks))
        items = lax.fori_loop(0, (total + ITEMS - 1) // ITEMS - 1, step, items)
        for slot, half in parts:
            absorb(slot, items[slot], half)

    @pl.when(jnp.logical_not(plain))
    def _():
        top_ref[...] = jnp.full_like(top_ref, LOW)

        def over_block(r, carry):
            def over_chunk(i, carry):
                careful(r, i)
                return carry

            return lax.fori_loop(0, count(r), over_chunk, carry)

        lax.fori_loop(0, blocks, over_block, 0)

    for r in range(blocks):
        acc = acc_ref[r]
        total = acc[HEAD_DIM : HEAD_DIM + 1]
        some = total > 0.0
        safe = jnp.where(some, total, 1.0)
        mean = (acc[:HEAD_DIM] * jnp.where(some, 1.0 / safe, 0.0)).astype(jnp.bfloat16)
        level = jnp.where(some, top_ref[r, :1] + jnp.log2(safe), LOW)
        high = level.astype(jnp.bfloat16).astype(jnp.float32)
        middle = (level - high).astype(jnp.bfloat16).astype(jnp.float32)
        low = level - high - middle
        spare = jnp.zeros((NOTE - 3, SEGMENT), jnp.float32)
        note = jnp.concatenate([high, middle, low, spare]).astype(jnp.bfloat16)
        for out, at in ((own_out, slice(0, HEAD_DIM)), (their_out, slice(HEAD_DIM, SEGMENT))):
            out[r, :HEAD_DIM, :] = mean[:, at]
            out[r, HEAD_DIM:, :] = note[:, at]


def attend(info, own_q, their_q, ends, sources, head):
    rows = ZONES * SEGMENT
    out = jax.ShapeDtypeStruct((ZONES, HEAD_DIM + NOTE, HEAD_DIM), jnp.bfloat16)
    first = own_q.shape[1] // HEAD_DIM - 3
    own_spec = pl.BlockSpec((ZONES, HEAD_DIM, HEAD_DIM), lambda i, *_: (0, first + head, 0))
    whole = pl.BlockSpec(memory_space=pltpu.VMEM)
    return pl.pallas_call(
        functools.partial(attend_kernel, head, len(sources) > 1),
        grid_spec=pltpu.PrefetchScalarGridSpec(
            num_scalar_prefetch=1,
            grid=(1,),
            in_specs=[own_spec, whole, whole]
            + [pl.BlockSpec(memory_space=pl.ANY)] * len(sources),
            out_specs=[whole, whole],
            scratch_shapes=[
                pltpu.VMEM((4, 2, ZONES, 2 * HEAD_DIM, HEAD_DIM), jnp.bfloat16),
                pltpu.VMEM((ZONES, HEAD_DIM, SEGMENT), jnp.bfloat16),
                pltpu.VMEM((ITEMS, WIDTH, SEGMENT), jnp.bfloat16),
                pltpu.VMEM((ZONES + 1, HEAD_DIM + NOTE, SEGMENT), jnp.float32),
                pltpu.VMEM((ZONES, 8, SEGMENT), jnp.float32),
                pltpu.SemaphoreType.DMA((8,)),
            ],
        ),
        out_shape=[out, out],
        compiler_params=pltpu.CompilerParams(vmem_limit_bytes=58 << 20),
        cost_estimate=pl.CostEstimate(
            flops=4 * rows * KEYS * HEAD_DIM,
            bytes_accessed=4 * KEYS * HEAD_DIM + 4 * rows * HEAD_DIM,
            transcendentals=rows * KEYS // 2,
        ),
    )(info, own_q, their_q, ends, *sources)


def pack_first_kernel(head, queries_ref, keys_ref, values_ref, ids_ref, out_ref):
    groups = out_ref.shape[0]
    heads = keys_ref.shape[1] // HEAD_DIM // groups
    ids = jnp.broadcast_to(ids_ref[...].astype(jnp.float32), (HEAD_DIM, HEAD_DIM)).T
    lane = lax.broadcasted_iota(jnp.int32, (HEAD_DIM, HEAD_DIM), 1)
    counts = jnp.sum(jnp.where(ids <= lane.astype(jnp.float32), 1.0, 0.0), axis=0, keepdims=True)
    ones = jnp.ones((HEAD_DIM, HEAD_DIM), jnp.bfloat16)
    lane = lane[:1]
    for g in range(groups):
        at = slice((g * heads + head) * HEAD_DIM, (g * heads + head + 1) * HEAD_DIM)
        out_ref[g, :HEAD_DIM] = keys_ref[:, at]
        out_ref[g, HEAD_DIM : 2 * HEAD_DIM] = values_ref[:, at].T
        note = counts
        for first, ref in ((K_NORM, keys_ref), (Q_NORM, queries_ref)):
            for h in range(heads):
                start = (g * heads + h) * HEAD_DIM
                rows = ref[:, start : start + HEAD_DIM].astype(jnp.float32)
                norm = jnp.max(dot((rows * rows).astype(jnp.bfloat16), ones), axis=0, keepdims=True)
                note = jnp.where(lane == first + h, norm * 1.02, note)
        out_ref[g, 2 * HEAD_DIM :] = jnp.broadcast_to(note, (NOTE, HEAD_DIM)).astype(jnp.bfloat16)


def pack_rest_kernel(others, queries_ref, keys_ref, values_ref, out_ref):
    groups = out_ref.shape[0]
    heads = keys_ref.shape[1] // HEAD_DIM // groups
    for g in range(groups):
        parts = [p for head in others for p in ((keys_ref, head, False), (values_ref, head, True))]
        parts += [(queries_ref, head, True) for head in range(heads)]
        for j, (ref, head, turn) in enumerate(parts):
            at = slice((g * heads + head) * HEAD_DIM, (g * heads + head + 1) * HEAD_DIM)
            out_ref[g, j * HEAD_DIM : (j + 1) * HEAD_DIM] = ref[:, at].T if turn else ref[:, at]


def pack(kernel, rows, *args):
    return pl.pallas_call(
        kernel, out_shape=jax.ShapeDtypeStruct((ZONES, rows, HEAD_DIM), jnp.bfloat16)
    )(*args)


def merge_kernel(*refs):
    out = refs[-1]

    def level(ref, zone):
        note = ref[zone, HEAD_DIM:, :].astype(jnp.float32)
        return note[0:1] + note[1:2] + note[2:3]

    for head in range(len(refs) // 2):
        one, two = refs[2 * head], refs[2 * head + 1]
        at = slice(head * HEAD_DIM, (head + 1) * HEAD_DIM)
        for zone in range(ZONES):
            share = 1.0 / (1.0 + jnp.exp2(level(two, zone) - level(one, zone)))
            a, b = (ref[zone, :HEAD_DIM, :].astype(jnp.float32) for ref in (one, two))
            out[zone, at, :] = (b + (a - b) * share).astype(jnp.bfloat16)


def merge(parts):
    return pack(merge_kernel, len(parts) // 2 * HEAD_DIM, *parts)


def gate_kernel(gate_ref, mixed_ref, out_ref):
    groups, local, _ = mixed_ref.shape
    for g in range(groups):
        for h in range(0, local, HEAD_DIM):
            at = slice(g * local + h, g * local + h + HEAD_DIM)
            attended = mixed_ref[g, h : h + HEAD_DIM, :].T.astype(jnp.float32)
            out_ref[:, at] = (gate_ref[:, at] * attended).astype(jnp.bfloat16)


def gate_rows(span_ids, timesteps, time_weight):
    half = time_weight.shape[0] // 2
    freqs = jnp.exp(-math.log(10000.0) * jnp.arange(half, dtype=jnp.float32) / half)
    angles = timesteps.astype(jnp.float32)[:, None] * freqs[None, :]
    embed = jnp.concatenate([jnp.cos(angles), jnp.sin(angles)], axis=1).astype(jnp.bfloat16)
    gate_table = jnp.dot(embed, time_weight, preferred_element_type=jnp.float32)
    onehot = (span_ids[:, None] == jnp.arange(timesteps.shape[0], dtype=jnp.int32)[None, :]).astype(
        jnp.float32
    )
    return jnp.dot(onehot, gate_table, precision=lax.Precision.HIGHEST)


def per_device(queries, keys, values, span_ids, timesteps, time_weight):
    runs, groups = lax.axis_size("span"), lax.axis_size("head")
    run, rank = lax.axis_index("span"), lax.axis_index("head")
    spans = timesteps.shape[0]
    chunk, width = queries.shape
    local = width // groups
    heads = local // HEAD_DIM

    def device(zone, core, y, x):
        return (2 * zone + core) * groups + 2 * y + x

    across = [
        [device(zone, core, y, x) for zone in range(ZONES)]
        for core in range(2)
        for y in range(4)
        for x in range(2)
    ]
    along_y = [
        [device(zone, core, y, x) for y in range(4) for core in range(2)]
        for zone in range(ZONES)
        for x in range(2)
    ]
    up = [(h, (h + 2) % groups) for h in range(groups)]
    down = [(h, (h - 2) % groups) for h in range(groups)]
    core_swap = [(s, s ^ 1) for s in range(runs)]
    partner = [(h, h ^ 1) for h in range(groups)]

    def exchange(parts):
        return lax.all_to_all(
            parts, BOTH, split_axis=0, concat_axis=0, axis_index_groups=across, tiled=True
        )

    def gather(block):
        block = lax.all_gather(block, BOTH, axis_index_groups=along_y, axis=0, tiled=True)
        return block.reshape(4, 2, ZONES, -1, HEAD_DIM)

    def after(*values):
        return lax.optimization_barrier(values)

    def swapped(block):
        return block, lax.ppermute(block, "span", core_swap)

    pair = 2 * HEAD_DIM
    note_rows = span_ids.reshape(1, -1)
    first = pack(
        functools.partial(pack_first_kernel, 1), pair + NOTE, queries, keys, values, note_rows
    )
    first = exchange(first)
    queries, first = after(queries, first)
    rest = pack(
        functools.partial(pack_rest_kernel, (0, 2)), 2 * pair + local, queries, keys, values
    )
    rest = exchange(rest)
    gathered = gather(first)
    block = rest[:, :pair]
    half = ZONES // 2
    below, above = lax.ppermute(block, "head", up), lax.ppermute(block, "head", down)
    own_q = [rest[:, start : start + HEAD_DIM] for start in range(2 * pair, rest.shape[1], HEAD_DIM)]
    their_q = [None, lax.ppermute(own_q[1], "head", partner), None]

    def combined(notes):
        is_count = jnp.arange(HEAD_DIM) < K_NORM
        return jnp.where(is_count, jnp.sum(notes, axis=0), jnp.max(notes, axis=0))

    note = combined(gathered[:, :, :, pair].reshape(-1, HEAD_DIM).astype(jnp.float32))[None]
    note, their_q[1] = after(note, their_q[1])
    note_other = lax.ppermute(note, "head", partner)
    own_q[0], note_other = after(own_q[0], note_other)
    their_q[0] = lax.ppermute(own_q[0], "head", partner)
    note = combined(jnp.concatenate([note, note_other]))
    squares = note[K_NORM : K_NORM + heads] * note[Q_NORM : Q_NORM + heads]
    plain = (squares * (1.05 * SCALE**2) < PLAIN_LIMIT**2).astype(jnp.int32)
    ends = note[:spans].astype(jnp.int32)

    core, y, side = run % 2, rank // 2, rank % 2
    sides = jnp.stack([side, 1 - side])[None, :, None] * HEAD_DIM
    position = jnp.arange(ZONES)[:, None, None] * 2048 + sides + jnp.arange(HEAD_DIM)[None, None, :]
    position = (position + (core * 1024 + y * SEGMENT)).reshape(ZONES, SEGMENT)
    reach = jnp.min(
        jnp.where(ends > position[..., None], ends, runs * groups * chunk), axis=2
    )
    reach = jnp.maximum(reach - side * HEAD_DIM, 0)
    seen = (reach // SEGMENT) * HEAD_DIM + jnp.minimum(reach % SEGMENT, HEAD_DIM)
    seen = seen.astype(jnp.int32)
    counts = jnp.maximum((jnp.max(seen, axis=1) + WIDTH - 1) // WIDTH, 1)
    info = jnp.concatenate([jnp.stack([core, y]), counts, plain]).astype(jnp.int32)
    seen = seen.reshape(ZONES, 1, SEGMENT)

    parts = [None] * (2 * heads)

    def attended(info, head, sources):
        parts[2 * head], theirs = attend(info, rest, their_q[head], seen, sources, head)
        info, theirs = after(info, theirs)
        parts[2 * head + 1] = lax.ppermute(theirs, "head", partner)
        return info

    pieces = [lax.ppermute(below[:half], "head", up), lax.ppermute(above[half:], "head", down)]
    near, far = swapped(jnp.stack([block, above, below]))
    info, their_q[0], *pieces = after(info, their_q[0], *pieces)
    near_last, far_last = swapped(jnp.concatenate(pieces)[None])
    info = attended(info, 1, (gathered,))
    own_q[2], info = after(own_q[2], info)
    their_q[2] = lax.ppermute(own_q[2], "head", partner)
    info = attended(info, 0, (near, near_last, far, far_last))
    info = attended(info, 2, (gather(rest[:, pair : 2 * pair]),))
    mixed = exchange(merge(parts))
    gates = gate_rows(span_ids, timesteps, time_weight)
    return pl.pallas_call(
        gate_kernel, out_shape=jax.ShapeDtypeStruct((chunk, width), jnp.bfloat16)
    )(gates, mixed)


def solution(mesh):
    return jax.shard_map(
        per_device,
        mesh=mesh,
        in_specs=(
            P(("span", "head"), None),
            P(("span", "head"), None),
            P(("span", "head"), None),
            P(("span", "head")),
            P(),
            P(),
        ),
        out_specs=P(("span", "head"), None),
        check_vma=False,
    )
```

```python
import functools
import math

import jax
import jax.numpy as jnp
from jax import lax
from jax.experimental import pallas as pl
from jax.experimental.pallas import tpu as pltpu
from jax.sharding import PartitionSpec as P

HEAD_DIM = 128
SCALE = HEAD_DIM**-0.5
SCALE_LOG2 = SCALE * math.log2(math.e)
BOTH = ("span", "head")
ZONES = 8
SEGMENT = 2 * HEAD_DIM
KEYS = 8192
WIDTH = 512
SUB = 256
ITEMS = 4
K_NORM, Q_NORM = 32, 40
NOTE = 16
PLAIN_LIMIT = 70.0
LOW = -1e30


def dot(a, b):
    return jnp.dot(a, b, preferred_element_type=jnp.float32)


def attend_kernel(head, info_ref, own_q, their_q, end_ref, *refs):
    sources, refs = refs[:-8], refs[-8:]
    own_out, their_out, kv_ref, qt_ref, weight_ref, acc_ref, top_ref, sems = refs
    core, rank = info_ref[0], info_ref[1]
    blocks = ZONES

    copies = []
    if len(sources) == 1:
        whole = sources[0].at[:, :, :, pl.ds(0, 2 * HEAD_DIM)]
        copies.append(pltpu.make_async_copy(whole, kv_ref, sems.at[0]))
        sources = ()
    half = len(sources) // 2
    for j, (group, c) in enumerate(((sources[:half], core), (sources[half:], 1 - core))):
        pieces = [src.at[k] for src in group for k in range(src.shape[0])]
        for k, (piece, step) in enumerate(zip(pieces, (0, 1, 3, 2))):
            copies.append(
                pltpu.make_async_copy(
                    piece.at[:, pl.ds(0, 2 * HEAD_DIM)],
                    kv_ref.at[(rank + step) % 4, c],
                    sems.at[4 * j + k],
                )
            )
    for copy in copies:
        copy.start()

    for zone in range(ZONES):
        qt_ref[zone] = jnp.concatenate([own_q[zone], their_q[zone]], axis=1)
    acc_ref[...] = jnp.zeros_like(acc_ref)
    top_ref[...] = jnp.zeros_like(top_ref)
    ones = jnp.ones((NOTE, WIDTH), jnp.bfloat16)
    for copy in copies:
        copy.wait()

    def part(i, rows):
        return kv_ref[:, i % 2, i // 2, rows]

    def keys_at(i):
        return part(i, slice(0, HEAD_DIM)).reshape(WIDTH, HEAD_DIM)

    def values_at(i):
        block = part(i, slice(HEAD_DIM, 2 * HEAD_DIM))
        block = jnp.concatenate([block[y] for y in range(4)], axis=1)
        return jnp.concatenate([block, ones], axis=0)

    def visible_at(r, i):
        row = lax.broadcasted_iota(jnp.int32, (WIDTH, SEGMENT), 0)
        return row < end_ref[r] - i * WIDTH

    def score(item, half):
        r, i = item
        keys = kv_ref[2 * half : 2 * half + 2, i % 2, i // 2, :HEAD_DIM].reshape(SUB, HEAD_DIM)
        return dot(keys, qt_ref[jnp.minimum(r, blocks - 1)])

    def weigh(slot, item, half, scores):
        r, i = item
        row = lax.broadcasted_iota(jnp.int32, (SUB, SEGMENT), 0)
        visible = row < end_ref[jnp.minimum(r, blocks - 1)] - (i * WIDTH + half * SUB)
        weights = jnp.where(visible, jnp.exp2(scores * SCALE_LOG2), 0.0)
        weight_ref[slot, half * SUB : (half + 1) * SUB] = weights.astype(jnp.bfloat16)

    def absorb(slot, item, half):
        r, i = item
        block = kv_ref[2 * half : 2 * half + 2, i % 2, i // 2, HEAD_DIM:]
        values = jnp.concatenate([jnp.concatenate([block[0], block[1]], axis=1), ones[:, :SUB]], axis=0)
        acc_ref[r] += dot(values, weight_ref[slot, half * SUB : (half + 1) * SUB])

    def careful(r, i):
        scores = dot(keys_at(i), qt_ref[r]) * SCALE_LOG2
        visible = visible_at(r, i)
        scores = jnp.where(visible, scores, LOW)
        old = top_ref[r, :1]
        new = jnp.maximum(old, jnp.max(scores, axis=0, keepdims=True))
        weights = jnp.where(visible, jnp.exp2(scores - new), 0.0).astype(jnp.bfloat16)
        acc_ref[r] = acc_ref[r] * jnp.exp2(old - new) + dot(values_at(i), weights)
        top_ref[r] = jnp.broadcast_to(new, top_ref.shape[1:])

    def count(r):
        return info_ref[2 + r]

    parts = [(slot, half) for slot in range(ITEMS) for half in range(2)]
    plain = info_ref[2 + blocks + head] == 1

    @pl.when(plain)
    def _():
        def following(item):
            r, i = item
            over = i + 1 >= count(jnp.minimum(r, blocks - 1))
            over = jnp.logical_or(over, r >= blocks)
            return jnp.where(over, jnp.minimum(r + 1, blocks), r), jnp.where(over, 0, i + 1)

        def run(item):
            items = [item]
            for _ in range(ITEMS - 1):
                items.append(following(items[-1]))
            return tuple(items)

        def step(_, items):
            later = run(following(items[-1]))
            scores = score(later[0], 0)
            for slot, half in parts:
                now = scores
                if (slot, half) != parts[-1]:
                    scores = score(later[slot + half], 1 - half)
                absorb(slot, items[slot], half)
                weigh(slot, later[slot], half, now)
            return later

        items = run((jnp.int32(0), jnp.int32(0)))
        for slot, half in parts:
            weigh(slot, items[slot], half, score(items[slot], half))
        total = sum(count(r) for r in range(blocks))
        items = lax.fori_loop(0, (total + ITEMS - 1) // ITEMS - 1, step, items)
        for slot, half in parts:
            absorb(slot, items[slot], half)

    @pl.when(jnp.logical_not(plain))
    def _():
        top_ref[...] = jnp.full_like(top_ref, LOW)

        def over_block(r, carry):
            def over_chunk(i, carry):
                careful(r, i)
                return carry

            return lax.fori_loop(0, count(r), over_chunk, carry)

        lax.fori_loop(0, blocks, over_block, 0)

    for r in range(blocks):
        acc = acc_ref[r]
        total = acc[HEAD_DIM : HEAD_DIM + 1]
        some = total > 0.0
        safe = jnp.where(some, total, 1.0)
        mean = (acc[:HEAD_DIM] * jnp.where(some, 1.0 / safe, 0.0)).astype(jnp.bfloat16)
        level = jnp.where(some, top_ref[r, :1] + jnp.log2(safe), LOW)
        high = level.astype(jnp.bfloat16).astype(jnp.float32)
        middle = (level - high).astype(jnp.bfloat16).astype(jnp.float32)
        low = level - high - middle
        spare = jnp.zeros((NOTE - 3, SEGMENT), jnp.float32)
        note = jnp.concatenate([high, middle, low, spare]).astype(jnp.bfloat16)
        for out, at in ((own_out, slice(0, HEAD_DIM)), (their_out, slice(HEAD_DIM, SEGMENT))):
            out[r, :HEAD_DIM, :] = mean[:, at]
            out[r, HEAD_DIM:, :] = note[:, at]


def attend(info, own_q, their_q, at, ends, sources, head):
    rows = ZONES * SEGMENT
    out = jax.ShapeDtypeStruct((ZONES, HEAD_DIM + NOTE, HEAD_DIM), jnp.bfloat16)
    first = own_q.shape[1] // HEAD_DIM - 3
    own_spec = pl.BlockSpec((ZONES, HEAD_DIM, HEAD_DIM), lambda i, *_: (0, first + head, 0))
    their_spec = pl.BlockSpec((ZONES, HEAD_DIM, HEAD_DIM), lambda i, *_: (0, at, 0))
    whole = pl.BlockSpec(memory_space=pltpu.VMEM)
    return pl.pallas_call(
        functools.partial(attend_kernel, head),
        grid_spec=pltpu.PrefetchScalarGridSpec(
            num_scalar_prefetch=1,
            grid=(1,),
            in_specs=[own_spec, their_spec, whole]
            + [pl.BlockSpec(memory_space=pl.ANY)] * len(sources),
            out_specs=[whole, whole],
            scratch_shapes=[
                pltpu.VMEM((4, 2, ZONES, 2 * HEAD_DIM, HEAD_DIM), jnp.bfloat16),
                pltpu.VMEM((ZONES, HEAD_DIM, SEGMENT), jnp.bfloat16),
                pltpu.VMEM((ITEMS, WIDTH, SEGMENT), jnp.bfloat16),
                pltpu.VMEM((ZONES + 1, HEAD_DIM + NOTE, SEGMENT), jnp.float32),
                pltpu.VMEM((ZONES, 8, SEGMENT), jnp.float32),
                pltpu.SemaphoreType.DMA((8,)),
            ],
        ),
        out_shape=[out, out],
        compiler_params=pltpu.CompilerParams(vmem_limit_bytes=58 << 20),
        cost_estimate=pl.CostEstimate(
            flops=4 * rows * KEYS * HEAD_DIM,
            bytes_accessed=4 * KEYS * HEAD_DIM + 4 * rows * HEAD_DIM,
            transcendentals=rows * KEYS // 2,
        ),
    )(info, own_q, their_q, ends, *sources)


def pack_first_kernel(head, queries_ref, keys_ref, values_ref, ids_ref, out_ref):
    groups = out_ref.shape[0]
    heads = keys_ref.shape[1] // HEAD_DIM // groups
    ids = jnp.broadcast_to(ids_ref[...].astype(jnp.float32), (HEAD_DIM, HEAD_DIM)).T
    lane = lax.broadcasted_iota(jnp.int32, (HEAD_DIM, HEAD_DIM), 1)
    counts = jnp.sum(jnp.where(ids <= lane.astype(jnp.float32), 1.0, 0.0), axis=0, keepdims=True)
    ones = jnp.ones((HEAD_DIM, HEAD_DIM), jnp.bfloat16)
    lane = lane[:1]
    for g in range(groups):
        at = slice((g * heads + head) * HEAD_DIM, (g * heads + head + 1) * HEAD_DIM)
        out_ref[g, :HEAD_DIM] = keys_ref[:, at]
        out_ref[g, HEAD_DIM : 2 * HEAD_DIM] = values_ref[:, at].T
        note = counts
        for first, ref in ((K_NORM, keys_ref), (Q_NORM, queries_ref)):
            for h in range(heads):
                start = (g * heads + h) * HEAD_DIM
                rows = ref[:, start : start + HEAD_DIM].astype(jnp.float32)
                norm = jnp.max(dot((rows * rows).astype(jnp.bfloat16), ones), axis=0, keepdims=True)
                note = jnp.where(lane == first + h, norm * 1.02, note)
        out_ref[g, 2 * HEAD_DIM :] = jnp.broadcast_to(note, (NOTE, HEAD_DIM)).astype(jnp.bfloat16)


def pack_rest_kernel(others, queries_ref, keys_ref, values_ref, out_ref):
    groups = out_ref.shape[0]
    heads = keys_ref.shape[1] // HEAD_DIM // groups
    for g in range(groups):
        parts = [p for head in others for p in ((keys_ref, head, False), (values_ref, head, True))]
        parts += [(queries_ref, head, True) for head in range(heads)]
        for j, (ref, head, turn) in enumerate(parts):
            at = slice((g * heads + head) * HEAD_DIM, (g * heads + head + 1) * HEAD_DIM)
            out_ref[g, j * HEAD_DIM : (j + 1) * HEAD_DIM] = ref[:, at].T if turn else ref[:, at]


def pack(kernel, rows, *args):
    return pl.pallas_call(
        kernel, out_shape=jax.ShapeDtypeStruct((ZONES, rows, HEAD_DIM), jnp.bfloat16)
    )(*args)


def merge_kernel(*refs):
    out = refs[-1]

    def level(ref, zone):
        note = ref[zone, HEAD_DIM:, :].astype(jnp.float32)
        return note[0:1] + note[1:2] + note[2:3]

    for head in range(len(refs) // 2):
        one, two = refs[2 * head], refs[2 * head + 1]
        at = slice(head * HEAD_DIM, (head + 1) * HEAD_DIM)
        for zone in range(ZONES):
            share = 1.0 / (1.0 + jnp.exp2(level(two, zone) - level(one, zone)))
            a, b = (ref[zone, :HEAD_DIM, :].astype(jnp.float32) for ref in (one, two))
            out[zone, at, :] = (b + (a - b) * share).astype(jnp.bfloat16)


def merge(parts):
    return pack(merge_kernel, len(parts) // 2 * HEAD_DIM, *parts)


def gate_kernel(gate_ref, mixed_ref, out_ref):
    groups, local, _ = mixed_ref.shape
    for g in range(groups):
        for h in range(0, local, HEAD_DIM):
            at = slice(g * local + h, g * local + h + HEAD_DIM)
            attended = mixed_ref[g, h : h + HEAD_DIM, :].T.astype(jnp.float32)
            out_ref[:, at] = (gate_ref[:, at] * attended).astype(jnp.bfloat16)


def gate_rows(span_ids, timesteps, time_weight):
    half = time_weight.shape[0] // 2
    freqs = jnp.exp(-math.log(10000.0) * jnp.arange(half, dtype=jnp.float32) / half)
    angles = timesteps.astype(jnp.float32)[:, None] * freqs[None, :]
    embed = jnp.concatenate([jnp.cos(angles), jnp.sin(angles)], axis=1).astype(jnp.bfloat16)
    gate_table = jnp.dot(embed, time_weight, preferred_element_type=jnp.float32)
    onehot = (span_ids[:, None] == jnp.arange(timesteps.shape[0], dtype=jnp.int32)[None, :]).astype(
        jnp.float32
    )
    return jnp.dot(onehot, gate_table, precision=lax.Precision.HIGHEST)


def per_device(queries, keys, values, span_ids, timesteps, time_weight):
    runs, groups = lax.axis_size("span"), lax.axis_size("head")
    run, rank = lax.axis_index("span"), lax.axis_index("head")
    spans = timesteps.shape[0]
    chunk, width = queries.shape
    local = width // groups
    heads = local // HEAD_DIM

    def device(zone, core, y, x):
        return (2 * zone + core) * groups + 2 * y + x

    across = [
        [device(zone, core, y, x) for zone in range(ZONES)]
        for core in range(2)
        for y in range(4)
        for x in range(2)
    ]
    along_y = [
        [device(zone, core, y, x) for y in range(4) for core in range(2)]
        for zone in range(ZONES)
        for x in range(2)
    ]
    up = [(h, (h + 2) % groups) for h in range(groups)]
    down = [(h, (h - 2) % groups) for h in range(groups)]
    core_swap = [(s, s ^ 1) for s in range(runs)]
    partner = [(h, h ^ 1) for h in range(groups)]

    def exchange(parts):
        return lax.all_to_all(
            parts, BOTH, split_axis=0, concat_axis=0, axis_index_groups=across, tiled=True
        )

    def gather(block):
        block = lax.all_gather(block, BOTH, axis_index_groups=along_y, axis=0, tiled=True)
        return block.reshape(4, 2, ZONES, -1, HEAD_DIM)

    def after(*values):
        return lax.optimization_barrier(values)

    def swapped(block):
        return block, lax.ppermute(block, "span", core_swap)

    pair = 2 * HEAD_DIM
    note_rows = span_ids.reshape(1, -1)
    first = pack(
        functools.partial(pack_first_kernel, 1), pair + NOTE, queries, keys, values, note_rows
    )
    first = exchange(first)
    queries, first = after(queries, first)
    rest = pack(
        functools.partial(pack_rest_kernel, (0, 2)), 2 * pair + local, queries, keys, values
    )
    rest = exchange(rest)
    gathered = gather(first)
    block = rest[:, :pair]
    own_q = [rest[:, start : start + HEAD_DIM] for start in range(2 * pair, rest.shape[1], HEAD_DIM)]
    their_q = [None, lax.ppermute(own_q[1], "head", partner), None]
    above, below = lax.ppermute(block, "head", down), lax.ppermute(block, "head", up)

    def combined(notes):
        is_count = jnp.arange(HEAD_DIM) < K_NORM
        return jnp.where(is_count, jnp.sum(notes, axis=0), jnp.max(notes, axis=0))

    note = combined(gathered[:, :, :, pair].reshape(-1, HEAD_DIM).astype(jnp.float32))[None]
    note_other = lax.ppermute(note, "head", partner)
    note = combined(jnp.concatenate([note, note_other]))
    squares = note[K_NORM : K_NORM + heads] * note[Q_NORM : Q_NORM + heads]
    plain = (squares * (1.05 * SCALE**2) < PLAIN_LIMIT**2).astype(jnp.int32)
    ends = note[:spans].astype(jnp.int32)

    core, y, side = run % 2, rank // 2, rank % 2
    offsets = jnp.stack([side, 1 - side])[None, :, None] * HEAD_DIM
    position = jnp.arange(ZONES)[:, None, None] * 2048 + offsets + jnp.arange(HEAD_DIM)[None, None, :]
    position = (position + (core * 1024 + y * SEGMENT)).reshape(ZONES, SEGMENT)
    reach = jnp.min(
        jnp.where(ends > position[..., None], ends, runs * groups * chunk), axis=2
    )
    reach = jnp.maximum(reach - side * HEAD_DIM, 0)
    seen = (reach // SEGMENT) * HEAD_DIM + jnp.minimum(reach % SEGMENT, HEAD_DIM)
    seen = seen.astype(jnp.int32)
    counts = jnp.maximum((jnp.max(seen, axis=1) + WIDTH - 1) // WIDTH, 1)
    info = jnp.concatenate([jnp.stack([core, y]), counts, plain]).astype(jnp.int32)
    seen = seen.reshape(ZONES, 1, SEGMENT)

    parts = [None] * (2 * heads)

    def attended(info, head, their_q, at, sources):
        parts[2 * head], theirs = attend(info, rest, their_q, at, seen, sources, head)
        info, theirs = after(info, theirs)
        parts[2 * head + 1] = lax.ppermute(theirs, "head", partner)
        return info

    info, above, below = after(info, above, below)
    opposite = lax.ppermute(below, "head", up)
    own_q[0], own_q[2], info = after(own_q[0], own_q[2], info)
    their_q[2] = lax.ppermute(own_q[2], "head", partner)
    info = attended(info, 1, their_q[1], 0, (gathered,))
    info, opposite, their_q[2] = after(info, opposite, their_q[2])
    near, far = swapped(jnp.stack([block, above, below, opposite]))
    their_q[0] = lax.ppermute(own_q[0], "head", partner)
    info = attended(info, 2, their_q[2], 0, (gather(rest[:, pair : 2 * pair]),))
    info, parts[3] = after(info, parts[3])
    info = attended(info, 0, their_q[0], 0, (near, far))
    mixed = exchange(merge(parts))
    gates = gate_rows(span_ids, timesteps, time_weight)
    return pl.pallas_call(
        gate_kernel, out_shape=jax.ShapeDtypeStruct((chunk, width), jnp.bfloat16)
    )(gates, mixed)


def solution(mesh):
    return jax.shard_map(
        per_device,
        mesh=mesh,
        in_specs=(
            P(("span", "head"), None),
            P(("span", "head"), None),
            P(("span", "head"), None),
            P(("span", "head")),
            P(),
            P(),
        ),
        out_specs=P(("span", "head"), None),
        check_vma=False,
    )
```

```python
import functools
import math

import jax
import jax.numpy as jnp
from jax import lax
from jax.experimental import pallas as pl
from jax.experimental.pallas import tpu as pltpu
from jax.sharding import PartitionSpec as P

HEAD_DIM = 128
SCALE = HEAD_DIM**-0.5
SCALE_LOG2 = SCALE * math.log2(math.e)
BOTH = ("span", "head")
ZONES = 8
SEGMENT = 2 * HEAD_DIM
KEYS = 8192
WIDTH = 512
SUB = 256
ITEMS = 4
K_NORM, Q_NORM = 32, 40
NOTE = 16
PLAIN_LIMIT = 70.0
LOW = -1e30


def dot(a, b):
    return jnp.dot(a, b, preferred_element_type=jnp.float32)


def attend_kernel(head, info_ref, own_q, their_q, end_ref, *refs):
    sources, refs = refs[:-8], refs[-8:]
    own_out, their_out, kv_ref, qt_ref, weight_ref, acc_ref, top_ref, sems = refs
    core, rank = info_ref[0], info_ref[1]
    blocks = ZONES

    copies = []
    if len(sources) == 1:
        whole = sources[0].at[:, :, :, pl.ds(0, 2 * HEAD_DIM)]
        copies.append(pltpu.make_async_copy(whole, kv_ref, sems.at[0]))
        sources = ()
    half = len(sources) // 2
    for j, (group, c) in enumerate(((sources[:half], core), (sources[half:], 1 - core))):
        pieces = [src.at[k] for src in group for k in range(src.shape[0])]
        for k, (piece, step) in enumerate(zip(pieces, (0, 1, 3, 2))):
            copies.append(
                pltpu.make_async_copy(
                    piece.at[:, pl.ds(0, 2 * HEAD_DIM)],
                    kv_ref.at[(rank + step) % 4, c],
                    sems.at[4 * j + k],
                )
            )
    for copy in copies:
        copy.start()

    for zone in range(ZONES):
        qt_ref[zone] = jnp.concatenate([own_q[zone], their_q[zone]], axis=1)
    acc_ref[...] = jnp.zeros_like(acc_ref)
    top_ref[...] = jnp.zeros_like(top_ref)
    ones = jnp.ones((NOTE, WIDTH), jnp.bfloat16)
    for copy in copies:
        copy.wait()

    def part(i, rows):
        return kv_ref[:, i % 2, i // 2, rows]

    def keys_at(i):
        return part(i, slice(0, HEAD_DIM)).reshape(WIDTH, HEAD_DIM)

    def values_at(i):
        block = part(i, slice(HEAD_DIM, 2 * HEAD_DIM))
        block = jnp.concatenate([block[y] for y in range(4)], axis=1)
        return jnp.concatenate([block, ones], axis=0)

    def visible_at(r, i):
        row = lax.broadcasted_iota(jnp.int32, (WIDTH, SEGMENT), 0)
        return row < end_ref[r] - i * WIDTH

    def score(item, half):
        r, i = item
        keys = kv_ref[2 * half : 2 * half + 2, i % 2, i // 2, :HEAD_DIM].reshape(SUB, HEAD_DIM)
        return dot(keys, qt_ref[jnp.minimum(r, blocks - 1)])

    def weigh(slot, item, half, scores):
        r, i = item
        row = lax.broadcasted_iota(jnp.int32, (SUB, SEGMENT), 0)
        visible = row < end_ref[jnp.minimum(r, blocks - 1)] - (i * WIDTH + half * SUB)
        weights = jnp.where(visible, jnp.exp2(scores * SCALE_LOG2), 0.0)
        weight_ref[slot, half * SUB : (half + 1) * SUB] = weights.astype(jnp.bfloat16)

    def absorb(slot, item, half):
        r, i = item
        block = kv_ref[2 * half : 2 * half + 2, i % 2, i // 2, HEAD_DIM:]
        values = jnp.concatenate([jnp.concatenate([block[0], block[1]], axis=1), ones[:, :SUB]], axis=0)
        acc_ref[r] += dot(values, weight_ref[slot, half * SUB : (half + 1) * SUB])

    def careful(r, i):
        scores = dot(keys_at(i), qt_ref[r]) * SCALE_LOG2
        visible = visible_at(r, i)
        scores = jnp.where(visible, scores, LOW)
        old = top_ref[r, :1]
        new = jnp.maximum(old, jnp.max(scores, axis=0, keepdims=True))
        weights = jnp.where(visible, jnp.exp2(scores - new), 0.0).astype(jnp.bfloat16)
        acc_ref[r] = acc_ref[r] * jnp.exp2(old - new) + dot(values_at(i), weights)
        top_ref[r] = jnp.broadcast_to(new, top_ref.shape[1:])

    def count(r):
        return info_ref[2 + r]

    parts = [(slot, half) for slot in range(ITEMS) for half in range(2)]
    plain = info_ref[2 + blocks + head] == 1

    @pl.when(plain)
    def _():
        def following(item):
            r, i = item
            over = i + 1 >= count(jnp.minimum(r, blocks - 1))
            over = jnp.logical_or(over, r >= blocks)
            return jnp.where(over, jnp.minimum(r + 1, blocks), r), jnp.where(over, 0, i + 1)

        def run(item):
            items = [item]
            for _ in range(ITEMS - 1):
                items.append(following(items[-1]))
            return tuple(items)

        def step(_, items):
            later = run(following(items[-1]))
            scores = score(later[0], 0)
            for slot, half in parts:
                now = scores
                if (slot, half) != parts[-1]:
                    scores = score(later[slot + half], 1 - half)
                absorb(slot, items[slot], half)
                weigh(slot, later[slot], half, now)
            return later

        items = run((jnp.int32(0), jnp.int32(0)))
        for slot, half in parts:
            weigh(slot, items[slot], half, score(items[slot], half))
        total = sum(count(r) for r in range(blocks))
        items = lax.fori_loop(0, (total + ITEMS - 1) // ITEMS - 1, step, items)
        for slot, half in parts:
            absorb(slot, items[slot], half)

    @pl.when(jnp.logical_not(plain))
    def _():
        top_ref[...] = jnp.full_like(top_ref, LOW)

        def over_block(r, carry):
            def over_chunk(i, carry):
                careful(r, i)
                return carry

            return lax.fori_loop(0, count(r), over_chunk, carry)

        lax.fori_loop(0, blocks, over_block, 0)

    for r in range(blocks):
        acc = acc_ref[r]
        total = acc[HEAD_DIM : HEAD_DIM + 1]
        some = total > 0.0
        safe = jnp.where(some, total, 1.0)
        mean = (acc[:HEAD_DIM] * jnp.where(some, 1.0 / safe, 0.0)).astype(jnp.bfloat16)
        level = jnp.where(some, top_ref[r, :1] + jnp.log2(safe), LOW)
        high = level.astype(jnp.bfloat16).astype(jnp.float32)
        middle = (level - high).astype(jnp.bfloat16).astype(jnp.float32)
        low = level - high - middle
        spare = jnp.zeros((NOTE - 3, SEGMENT), jnp.float32)
        note = jnp.concatenate([high, middle, low, spare]).astype(jnp.bfloat16)
        for out, at in ((own_out, slice(0, HEAD_DIM)), (their_out, slice(HEAD_DIM, SEGMENT))):
            out[r, :HEAD_DIM, :] = mean[:, at]
            out[r, HEAD_DIM:, :] = note[:, at]


def attend(info, own_q, their_q, at, ends, sources, head):
    rows = ZONES * SEGMENT
    out = jax.ShapeDtypeStruct((ZONES, HEAD_DIM + NOTE, HEAD_DIM), jnp.bfloat16)
    first = own_q.shape[1] // HEAD_DIM - 3
    own_spec = pl.BlockSpec((ZONES, HEAD_DIM, HEAD_DIM), lambda i, *_: (0, first + head, 0))
    their_spec = pl.BlockSpec((ZONES, HEAD_DIM, HEAD_DIM), lambda i, *_: (0, at, 0))
    whole = pl.BlockSpec(memory_space=pltpu.VMEM)
    return pl.pallas_call(
        functools.partial(attend_kernel, head),
        grid_spec=pltpu.PrefetchScalarGridSpec(
            num_scalar_prefetch=1,
            grid=(1,),
            in_specs=[own_spec, their_spec, whole]
            + [pl.BlockSpec(memory_space=pl.ANY)] * len(sources),
            out_specs=[whole, whole],
            scratch_shapes=[
                pltpu.VMEM((4, 2, ZONES, 2 * HEAD_DIM, HEAD_DIM), jnp.bfloat16),
                pltpu.VMEM((ZONES, HEAD_DIM, SEGMENT), jnp.bfloat16),
                pltpu.VMEM((ITEMS, WIDTH, SEGMENT), jnp.bfloat16),
                pltpu.VMEM((ZONES + 1, HEAD_DIM + NOTE, SEGMENT), jnp.float32),
                pltpu.VMEM((ZONES, 8, SEGMENT), jnp.float32),
                pltpu.SemaphoreType.DMA((8,)),
            ],
        ),
        out_shape=[out, out],
        compiler_params=pltpu.CompilerParams(vmem_limit_bytes=58 << 20),
        cost_estimate=pl.CostEstimate(
            flops=4 * rows * KEYS * HEAD_DIM,
            bytes_accessed=4 * KEYS * HEAD_DIM + 4 * rows * HEAD_DIM,
            transcendentals=rows * KEYS // 2,
        ),
    )(info, own_q, their_q, ends, *sources)


def pack_first_kernel(head, queries_ref, keys_ref, values_ref, ids_ref, out_ref):
    groups = out_ref.shape[0]
    heads = keys_ref.shape[1] // HEAD_DIM // groups
    ids = jnp.broadcast_to(ids_ref[...].astype(jnp.float32), (HEAD_DIM, HEAD_DIM)).T
    lane = lax.broadcasted_iota(jnp.int32, (HEAD_DIM, HEAD_DIM), 1)
    counts = jnp.sum(jnp.where(ids <= lane.astype(jnp.float32), 1.0, 0.0), axis=0, keepdims=True)
    local = heads * HEAD_DIM
    row = lax.broadcasted_iota(jnp.int32, (2 * local, HEAD_DIM), 0) // HEAD_DIM
    column = lax.broadcasted_iota(jnp.int32, (2 * local, HEAD_DIM), 1)
    wanted = jnp.where(row < heads, row + K_NORM, row - heads + Q_NORM)
    pick = jnp.where(column == wanted, 1.0, 0.0).astype(jnp.bfloat16)
    is_count = lane[:1] < K_NORM
    for g in range(groups):
        at = slice((g * heads + head) * HEAD_DIM, (g * heads + head + 1) * HEAD_DIM)
        out_ref[g, :HEAD_DIM] = keys_ref[:, at]
        out_ref[g, HEAD_DIM : 2 * HEAD_DIM] = values_ref[:, at].T
        rows = [ref[:, g * local : (g + 1) * local].astype(jnp.float32) for ref in (keys_ref, queries_ref)]
        squares = jnp.concatenate([(x * x).astype(jnp.bfloat16) for x in rows], axis=1)
        norms = jnp.max(dot(squares, pick), axis=0, keepdims=True) * 1.02
        note = jnp.where(is_count, counts, norms)
        out_ref[g, 2 * HEAD_DIM :] = jnp.broadcast_to(note, (NOTE, HEAD_DIM)).astype(jnp.bfloat16)


def pack_rest_kernel(others, queries_ref, keys_ref, values_ref, out_ref):
    groups = out_ref.shape[0]
    heads = keys_ref.shape[1] // HEAD_DIM // groups
    for g in range(groups):
        parts = [p for head in others for p in ((keys_ref, head, False), (values_ref, head, True))]
        parts += [(queries_ref, head, True) for head in range(heads)]
        for j, (ref, head, turn) in enumerate(parts):
            at = slice((g * heads + head) * HEAD_DIM, (g * heads + head + 1) * HEAD_DIM)
            out_ref[g, j * HEAD_DIM : (j + 1) * HEAD_DIM] = ref[:, at].T if turn else ref[:, at]


def pack(kernel, rows, *args):
    return pl.pallas_call(
        kernel, out_shape=jax.ShapeDtypeStruct((ZONES, rows, HEAD_DIM), jnp.bfloat16)
    )(*args)


def merge_kernel(*refs):
    out = refs[-1]

    def level(ref, zone):
        note = ref[zone, HEAD_DIM:, :].astype(jnp.float32)
        return note[0:1] + note[1:2] + note[2:3]

    for head in range(out.shape[1] // HEAD_DIM):
        one, two = refs[2 * head], refs[2 * head + 1]
        at = slice(head * HEAD_DIM, (head + 1) * HEAD_DIM)
        for zone in range(ZONES):
            share = 1.0 / (1.0 + jnp.exp2(level(two, zone) - level(one, zone)))
            a, b = (ref[zone, :HEAD_DIM, :].astype(jnp.float32) for ref in (one, two))
            out[zone, at, :] = (b + (a - b) * share).astype(jnp.bfloat16)


def merge(parts, follows=None):
    heads = len(parts) // 2
    rest = [] if follows is None else [follows]
    specs = [pl.BlockSpec(memory_space=pltpu.VMEM)] * len(parts)
    specs += [pl.BlockSpec(memory_space=pl.ANY)] * len(rest)
    shape = jax.ShapeDtypeStruct((ZONES, heads * HEAD_DIM, HEAD_DIM), jnp.bfloat16)
    return pl.pallas_call(merge_kernel, in_specs=specs, out_shape=shape)(*parts, *rest)


def gate_kernel(gate_ref, early_ref, late_ref, out_ref):
    groups = early_ref.shape[0]
    heads = [(late_ref, 0), (early_ref, 0), (early_ref, HEAD_DIM)]
    for g in range(groups):
        for head, (ref, h) in enumerate(heads):
            start = (g * len(heads) + head) * HEAD_DIM
            at = slice(start, start + HEAD_DIM)
            attended = ref[g, h : h + HEAD_DIM, :].T.astype(jnp.float32)
            out_ref[:, at] = (gate_ref[:, at] * attended).astype(jnp.bfloat16)


def gate_rows(span_ids, timesteps, time_weight):
    half = time_weight.shape[0] // 2
    freqs = jnp.exp(-math.log(10000.0) * jnp.arange(half, dtype=jnp.float32) / half)
    angles = timesteps.astype(jnp.float32)[:, None] * freqs[None, :]
    embed = jnp.concatenate([jnp.cos(angles), jnp.sin(angles)], axis=1).astype(jnp.bfloat16)
    gate_table = jnp.dot(embed, time_weight, preferred_element_type=jnp.float32)
    onehot = (span_ids[:, None] == jnp.arange(timesteps.shape[0], dtype=jnp.int32)[None, :]).astype(
        jnp.float32
    )
    return jnp.dot(onehot, gate_table, precision=lax.Precision.HIGHEST)


def per_device(queries, keys, values, span_ids, timesteps, time_weight):
    runs, groups = lax.axis_size("span"), lax.axis_size("head")
    run, rank = lax.axis_index("span"), lax.axis_index("head")
    spans = timesteps.shape[0]
    chunk, width = queries.shape
    local = width // groups
    heads = local // HEAD_DIM

    def device(zone, core, y, x):
        return (2 * zone + core) * groups + 2 * y + x

    across = [
        [device(zone, core, y, x) for zone in range(ZONES)]
        for core in range(2)
        for y in range(4)
        for x in range(2)
    ]
    along_y = [
        [device(zone, core, y, x) for y in range(4) for core in range(2)]
        for zone in range(ZONES)
        for x in range(2)
    ]
    up = [(h, (h + 2) % groups) for h in range(groups)]
    down = [(h, (h - 2) % groups) for h in range(groups)]
    core_swap = [(s, s ^ 1) for s in range(runs)]
    partner = [(h, h ^ 1) for h in range(groups)]

    def exchange(parts):
        return lax.all_to_all(
            parts, BOTH, split_axis=0, concat_axis=0, axis_index_groups=across, tiled=True
        )

    def gather(block):
        block = lax.all_gather(block, BOTH, axis_index_groups=along_y, axis=0, tiled=True)
        return block.reshape(4, 2, ZONES, -1, HEAD_DIM)

    def after(*values):
        return lax.optimization_barrier(values)

    def swapped(block):
        return block, lax.ppermute(block, "span", core_swap)

    pair = 2 * HEAD_DIM
    note_rows = span_ids.reshape(1, -1)
    first = pack(
        functools.partial(pack_first_kernel, 1), pair + NOTE, queries, keys, values, note_rows
    )
    first = exchange(first)
    queries, first = after(queries, first)
    rest = pack(
        functools.partial(pack_rest_kernel, (0, 2)), 2 * pair + local, queries, keys, values
    )
    rest = exchange(rest)
    gathered = gather(first)
    own_q = [rest[:, start : start + HEAD_DIM] for start in range(2 * pair, rest.shape[1], HEAD_DIM)]
    own_q[1], block, second = after(own_q[1], rest[:, :pair], rest[:, pair : 2 * pair])
    their_q = [None, lax.ppermute(own_q[1], "head", partner), None]
    above, below = lax.ppermute(block, "head", down), lax.ppermute(block, "head", up)

    def combined(notes):
        is_count = jnp.arange(HEAD_DIM) < K_NORM
        return jnp.where(is_count, jnp.sum(notes, axis=0), jnp.max(notes, axis=0))

    note = combined(gathered[:, :, :, pair].reshape(-1, HEAD_DIM).astype(jnp.float32))[None]
    note, their_q[1] = after(note, their_q[1])
    note_other = lax.ppermute(note, "head", partner)
    note = combined(jnp.concatenate([note, note_other]))
    squares = note[K_NORM : K_NORM + heads] * note[Q_NORM : Q_NORM + heads]
    plain = (squares * (1.05 * SCALE**2) < PLAIN_LIMIT**2).astype(jnp.int32)
    ends = note[:spans].astype(jnp.int32)

    core, y, side = run % 2, rank // 2, rank % 2
    offsets = jnp.stack([side, 1 - side])[None, :, None] * HEAD_DIM
    position = jnp.arange(ZONES)[:, None, None] * 2048 + offsets + jnp.arange(HEAD_DIM)[None, None, :]
    position = (position + (core * 1024 + y * SEGMENT)).reshape(ZONES, SEGMENT)
    reach = jnp.min(
        jnp.where(ends > position[..., None], ends, runs * groups * chunk), axis=2
    )
    reach = jnp.maximum(reach - side * HEAD_DIM, 0)
    seen = (reach // SEGMENT) * HEAD_DIM + jnp.minimum(reach % SEGMENT, HEAD_DIM)
    seen = seen.astype(jnp.int32)
    counts = jnp.maximum((jnp.max(seen, axis=1) + WIDTH - 1) // WIDTH, 1)
    info = jnp.concatenate([jnp.stack([core, y]), counts, plain]).astype(jnp.int32)
    seen = seen.reshape(ZONES, 1, SEGMENT)

    parts = [None] * (2 * heads)

    def attended(info, head, their_q, at, sources):
        parts[2 * head], theirs = attend(info, rest, their_q, at, seen, sources, head)
        info, theirs = after(info, theirs)
        parts[2 * head + 1] = lax.ppermute(theirs, "head", partner)
        return info

    info, above, below = after(info, above, below)
    opposite = lax.ppermute(above, "head", down)
    own_q[0], own_q[2], info = after(own_q[0], own_q[2], info)
    their_q[2] = lax.ppermute(own_q[2], "head", partner)
    info = attended(info, 1, their_q[1], 0, (gathered,))
    info, opposite, their_q[2] = after(info, opposite, their_q[2])
    near, far = swapped(jnp.stack([block, above, below, opposite]))
    their_q[0] = lax.ppermute(own_q[0], "head", partner)
    info = attended(info, 2, their_q[2], 0, (gather(second),))
    info, parts[3] = after(info, parts[3])
    info = attended(info, 0, their_q[0], 0, (near, far))
    mixed = [exchange(merge(parts[2:], parts[0])), exchange(merge(parts[:2]))]
    gates = gate_rows(span_ids, timesteps, time_weight)
    return pl.pallas_call(
        gate_kernel, out_shape=jax.ShapeDtypeStruct((chunk, width), jnp.bfloat16)
    )(gates, *mixed)


def solution(mesh):
    return jax.shard_map(
        per_device,
        mesh=mesh,
        in_specs=(
            P(("span", "head"), None),
            P(("span", "head"), None),
            P(("span", "head"), None),
            P(("span", "head")),
            P(),
            P(),
        ),
        out_specs=P(("span", "head"), None),
        check_vma=False,
    )
```

```python
import functools
import math

import jax
import jax.numpy as jnp
from jax import lax
from jax.experimental import pallas as pl
from jax.experimental.pallas import tpu as pltpu
from jax.sharding import PartitionSpec as P

HEAD_DIM = 128
SCALE = HEAD_DIM**-0.5
SCALE_LOG2 = SCALE * math.log2(math.e)
BOTH = ("span", "head")
ZONES = 8
SEGMENT = 2 * HEAD_DIM
KEYS = 8192
WIDTH = 512
SUB = 256
ITEMS = 4
K_NORM, Q_NORM = 32, 40
NOTE = 16
PLAIN_LIMIT = 70.0
LOW = -1e30


def dot(a, b):
    return jnp.dot(a, b, preferred_element_type=jnp.float32)


def attend_kernel(head, info_ref, own_q, their_q, end_ref, *refs):
    sources, refs = refs[:-8], refs[-8:]
    own_out, their_out, kv_ref, qt_ref, weight_ref, acc_ref, top_ref, sems = refs
    core, rank = info_ref[0], info_ref[1]
    blocks = ZONES

    copies = []
    if len(sources) == 1:
        whole = sources[0].at[:, :, :, pl.ds(0, 2 * HEAD_DIM)]
        copies.append(pltpu.make_async_copy(whole, kv_ref, sems.at[0]))
        sources = ()
    half = len(sources) // 2
    for j, (group, c) in enumerate(((sources[:half], core), (sources[half:], 1 - core))):
        pieces = [src.at[k] for src in group for k in range(src.shape[0])]
        for k, (piece, step) in enumerate(zip(pieces, (0, 1, 3, 2))):
            copies.append(
                pltpu.make_async_copy(
                    piece.at[:, pl.ds(0, 2 * HEAD_DIM)],
                    kv_ref.at[(rank + step) % 4, c],
                    sems.at[4 * j + k],
                )
            )
    for copy in copies:
        copy.start()

    for zone in range(ZONES):
        qt_ref[zone] = jnp.concatenate([own_q[zone], their_q[zone]], axis=1)
    acc_ref[...] = jnp.zeros_like(acc_ref)
    top_ref[...] = jnp.zeros_like(top_ref)
    ones = jnp.ones((NOTE, WIDTH), jnp.bfloat16)
    for copy in copies:
        copy.wait()

    def part(i, rows):
        return kv_ref[:, i % 2, i // 2, rows]

    def keys_at(i):
        return part(i, slice(0, HEAD_DIM)).reshape(WIDTH, HEAD_DIM)

    def values_at(i):
        block = part(i, slice(HEAD_DIM, 2 * HEAD_DIM))
        block = jnp.concatenate([block[y] for y in range(4)], axis=1)
        return jnp.concatenate([block, ones], axis=0)

    def visible_at(r, i):
        row = lax.broadcasted_iota(jnp.int32, (WIDTH, SEGMENT), 0)
        return row < end_ref[r] - i * WIDTH

    def score(item, half):
        r, i = item
        keys = kv_ref[2 * half : 2 * half + 2, i % 2, i // 2, :HEAD_DIM].reshape(SUB, HEAD_DIM)
        return dot(keys, qt_ref[jnp.minimum(r, blocks - 1)])

    def weigh(slot, item, half, scores):
        r, i = item
        row = lax.broadcasted_iota(jnp.int32, (SUB, SEGMENT), 0)
        visible = row < end_ref[jnp.minimum(r, blocks - 1)] - (i * WIDTH + half * SUB)
        weights = jnp.where(visible, jnp.exp2(scores * SCALE_LOG2), 0.0)
        weight_ref[slot, half * SUB : (half + 1) * SUB] = weights.astype(jnp.bfloat16)

    def absorb(slot, item, half):
        r, i = item
        block = kv_ref[2 * half : 2 * half + 2, i % 2, i // 2, HEAD_DIM:]
        values = jnp.concatenate([jnp.concatenate([block[0], block[1]], axis=1), ones[:, :SUB]], axis=0)
        acc_ref[r] += dot(values, weight_ref[slot, half * SUB : (half + 1) * SUB])

    def careful(r, i):
        scores = dot(keys_at(i), qt_ref[r]) * SCALE_LOG2
        visible = visible_at(r, i)
        scores = jnp.where(visible, scores, LOW)
        old = top_ref[r, :1]
        new = jnp.maximum(old, jnp.max(scores, axis=0, keepdims=True))
        weights = jnp.where(visible, jnp.exp2(scores - new), 0.0).astype(jnp.bfloat16)
        acc_ref[r] = acc_ref[r] * jnp.exp2(old - new) + dot(values_at(i), weights)
        top_ref[r] = jnp.broadcast_to(new, top_ref.shape[1:])

    def count(r):
        return info_ref[2 + r]

    parts = [(slot, half) for slot in range(ITEMS) for half in range(2)]
    plain = info_ref[2 + blocks + head] == 1

    @pl.when(plain)
    def _():
        def following(item):
            r, i = item
            over = i + 1 >= count(jnp.minimum(r, blocks - 1))
            over = jnp.logical_or(over, r >= blocks)
            return jnp.where(over, jnp.minimum(r + 1, blocks), r), jnp.where(over, 0, i + 1)

        def run(item):
            items = [item]
            for _ in range(ITEMS - 1):
                items.append(following(items[-1]))
            return tuple(items)

        def step(_, items):
            later = run(following(items[-1]))
            scores = score(later[0], 0)
            for slot, half in parts:
                now = scores
                if (slot, half) != parts[-1]:
                    scores = score(later[slot + half], 1 - half)
                absorb(slot, items[slot], half)
                weigh(slot, later[slot], half, now)
            return later

        items = run((jnp.int32(0), jnp.int32(0)))
        for slot, half in parts:
            weigh(slot, items[slot], half, score(items[slot], half))
        total = sum(count(r) for r in range(blocks))
        items = lax.fori_loop(0, (total + ITEMS - 1) // ITEMS - 1, step, items)
        for slot, half in parts:
            absorb(slot, items[slot], half)

    @pl.when(jnp.logical_not(plain))
    def _():
        top_ref[...] = jnp.full_like(top_ref, LOW)

        def over_block(r, carry):
            def over_chunk(i, carry):
                careful(r, i)
                return carry

            return lax.fori_loop(0, count(r), over_chunk, carry)

        lax.fori_loop(0, blocks, over_block, 0)

    for r in range(blocks):
        acc = acc_ref[r]
        total = acc[HEAD_DIM : HEAD_DIM + 1]
        some = total > 0.0
        safe = jnp.where(some, total, 1.0)
        mean = (acc[:HEAD_DIM] * jnp.where(some, 1.0 / safe, 0.0)).astype(jnp.bfloat16)
        level = jnp.where(some, top_ref[r, :1] + jnp.log2(safe), LOW)
        high = level.astype(jnp.bfloat16).astype(jnp.float32)
        middle = (level - high).astype(jnp.bfloat16).astype(jnp.float32)
        low = level - high - middle
        spare = jnp.zeros((NOTE - 3, SEGMENT), jnp.float32)
        note = jnp.concatenate([high, middle, low, spare]).astype(jnp.bfloat16)
        for out, at in ((own_out, slice(0, HEAD_DIM)), (their_out, slice(HEAD_DIM, SEGMENT))):
            out[r, :HEAD_DIM, :] = mean[:, at]
            out[r, HEAD_DIM:, :] = note[:, at]


def attend(info, own_q, their_q, at, ends, sources, head):
    rows = ZONES * SEGMENT
    out = jax.ShapeDtypeStruct((ZONES, HEAD_DIM + NOTE, HEAD_DIM), jnp.bfloat16)
    first = own_q.shape[1] // HEAD_DIM - 3
    own_spec = pl.BlockSpec((ZONES, HEAD_DIM, HEAD_DIM), lambda i, *_: (0, first + head, 0))
    their_spec = pl.BlockSpec((ZONES, HEAD_DIM, HEAD_DIM), lambda i, *_: (0, at, 0))
    whole = pl.BlockSpec(memory_space=pltpu.VMEM)
    return pl.pallas_call(
        functools.partial(attend_kernel, head),
        grid_spec=pltpu.PrefetchScalarGridSpec(
            num_scalar_prefetch=1,
            grid=(1,),
            in_specs=[own_spec, their_spec, whole]
            + [pl.BlockSpec(memory_space=pl.ANY)] * len(sources),
            out_specs=[whole, whole],
            scratch_shapes=[
                pltpu.VMEM((4, 2, ZONES, 2 * HEAD_DIM, HEAD_DIM), jnp.bfloat16),
                pltpu.VMEM((ZONES, HEAD_DIM, SEGMENT), jnp.bfloat16),
                pltpu.VMEM((ITEMS, WIDTH, SEGMENT), jnp.bfloat16),
                pltpu.VMEM((ZONES + 1, HEAD_DIM + NOTE, SEGMENT), jnp.float32),
                pltpu.VMEM((ZONES, 8, SEGMENT), jnp.float32),
                pltpu.SemaphoreType.DMA((8,)),
            ],
        ),
        out_shape=[out, out],
        compiler_params=pltpu.CompilerParams(vmem_limit_bytes=58 << 20),
        cost_estimate=pl.CostEstimate(
            flops=4 * rows * KEYS * HEAD_DIM,
            bytes_accessed=4 * KEYS * HEAD_DIM + 4 * rows * HEAD_DIM,
            transcendentals=rows * KEYS // 2,
        ),
    )(info, own_q, their_q, ends, *sources)


def pack_first_kernel(head, queries_ref, keys_ref, values_ref, ids_ref, out_ref):
    groups = out_ref.shape[0]
    heads = keys_ref.shape[1] // HEAD_DIM // groups
    ids = jnp.broadcast_to(ids_ref[...].astype(jnp.float32), (HEAD_DIM, HEAD_DIM)).T
    lane = lax.broadcasted_iota(jnp.int32, (HEAD_DIM, HEAD_DIM), 1)
    counts = jnp.sum(jnp.where(ids <= lane.astype(jnp.float32), 1.0, 0.0), axis=0, keepdims=True)
    ones = jnp.ones((HEAD_DIM, HEAD_DIM), jnp.bfloat16)
    lane = lane[:1]
    for g in range(groups):
        at = slice((g * heads + head) * HEAD_DIM, (g * heads + head + 1) * HEAD_DIM)
        out_ref[g, :HEAD_DIM] = keys_ref[:, at]
        out_ref[g, HEAD_DIM : 2 * HEAD_DIM] = values_ref[:, at].T
        note = counts
        for first, ref in ((K_NORM, keys_ref), (Q_NORM, queries_ref)):
            for h in range(heads):
                start = (g * heads + h) * HEAD_DIM
                rows = ref[:, start : start + HEAD_DIM].astype(jnp.float32)
                norm = jnp.max(dot((rows * rows).astype(jnp.bfloat16), ones), axis=0, keepdims=True)
                note = jnp.where(lane == first + h, norm * 1.02, note)
        out_ref[g, 2 * HEAD_DIM :] = jnp.broadcast_to(note, (NOTE, HEAD_DIM)).astype(jnp.bfloat16)


def pack_rest_kernel(others, queries_ref, keys_ref, values_ref, out_ref):
    groups = out_ref.shape[0]
    heads = keys_ref.shape[1] // HEAD_DIM // groups
    for g in range(groups):
        parts = [p for head in others for p in ((keys_ref, head, False), (values_ref, head, True))]
        parts += [(queries_ref, head, True) for head in range(heads)]
        for j, (ref, head, turn) in enumerate(parts):
            at = slice((g * heads + head) * HEAD_DIM, (g * heads + head + 1) * HEAD_DIM)
            out_ref[g, j * HEAD_DIM : (j + 1) * HEAD_DIM] = ref[:, at].T if turn else ref[:, at]


def pack(kernel, rows, *args):
    return pl.pallas_call(
        kernel, out_shape=jax.ShapeDtypeStruct((ZONES, rows, HEAD_DIM), jnp.bfloat16)
    )(*args)


def merge_kernel(*refs):
    out = refs[-1]

    def level(ref, zone):
        note = ref[zone, HEAD_DIM:, :].astype(jnp.float32)
        return note[0:1] + note[1:2] + note[2:3]

    for head in range(len(refs) // 2):
        one, two = refs[2 * head], refs[2 * head + 1]
        at = slice(head * HEAD_DIM, (head + 1) * HEAD_DIM)
        for zone in range(ZONES):
            share = 1.0 / (1.0 + jnp.exp2(level(two, zone) - level(one, zone)))
            a, b = (ref[zone, :HEAD_DIM, :].astype(jnp.float32) for ref in (one, two))
            out[zone, at, :] = (b + (a - b) * share).astype(jnp.bfloat16)


def merge(parts):
    return pack(merge_kernel, len(parts) // 2 * HEAD_DIM, *parts)


def gate_kernel(gate_ref, mixed_ref, out_ref):
    groups, local, _ = mixed_ref.shape
    for g in range(groups):
        for h in range(0, local, HEAD_DIM):
            at = slice(g * local + h, g * local + h + HEAD_DIM)
            attended = mixed_ref[g, h : h + HEAD_DIM, :].T.astype(jnp.float32)
            out_ref[:, at] = (gate_ref[:, at] * attended).astype(jnp.bfloat16)


def gate_rows(span_ids, timesteps, time_weight):
    half = time_weight.shape[0] // 2
    freqs = jnp.exp(-math.log(10000.0) * jnp.arange(half, dtype=jnp.float32) / half)
    angles = timesteps.astype(jnp.float32)[:, None] * freqs[None, :]
    embed = jnp.concatenate([jnp.cos(angles), jnp.sin(angles)], axis=1).astype(jnp.bfloat16)
    gate_table = jnp.dot(embed, time_weight, preferred_element_type=jnp.float32)
    onehot = (span_ids[:, None] == jnp.arange(timesteps.shape[0], dtype=jnp.int32)[None, :]).astype(
        jnp.float32
    )
    return jnp.dot(onehot, gate_table, precision=lax.Precision.HIGHEST)


def per_device(queries, keys, values, span_ids, timesteps, time_weight):
    runs, groups = lax.axis_size("span"), lax.axis_size("head")
    run, rank = lax.axis_index("span"), lax.axis_index("head")
    spans = timesteps.shape[0]
    chunk, width = queries.shape
    local = width // groups
    heads = local // HEAD_DIM

    def device(zone, core, y, x):
        return (2 * zone + core) * groups + 2 * y + x

    across = [
        [device(zone, core, y, x) for zone in range(ZONES)]
        for core in range(2)
        for y in range(4)
        for x in range(2)
    ]
    up = [(h, (h + 2) % groups) for h in range(groups)]
    down = [(h, (h - 2) % groups) for h in range(groups)]
    core_swap = [(s, s ^ 1) for s in range(runs)]
    other = [((s * groups + h), ((s ^ 1) * groups + (h ^ 1))) for s in range(runs) for h in range(groups)]
    partner = [(h, h ^ 1) for h in range(groups)]

    def exchange(parts):
        return lax.all_to_all(
            parts, BOTH, split_axis=0, concat_axis=0, axis_index_groups=across, tiled=True
        )

    def after(*values):
        return lax.optimization_barrier(values)

    def swapped(block):
        return block, lax.ppermute(block, "span", core_swap)

    def sides(block):
        return lax.ppermute(block, "head", down), lax.ppermute(block, "head", up)

    pair = 2 * HEAD_DIM
    note_rows = span_ids.reshape(1, -1)
    first = pack(
        functools.partial(pack_first_kernel, 0), pair + NOTE, queries, keys, values, note_rows
    )
    first = exchange(first)
    above, below = sides(first)
    queries, first = after(queries, first)
    rest = pack(
        functools.partial(pack_rest_kernel, (1, 2)), 2 * pair + local, queries, keys, values
    )
    rest = exchange(rest)
    near = jnp.stack([first, above, below, lax.ppermute(above, "head", down)])

    def combined(notes):
        is_count = jnp.arange(HEAD_DIM) < K_NORM
        return jnp.where(is_count, jnp.sum(notes, axis=0), jnp.max(notes, axis=0))

    note = combined(near[:, :, pair].reshape(-1, HEAD_DIM).astype(jnp.float32))[None]
    rest, near, note = after(rest, near, note)
    notes = [
        note,
        lax.ppermute(note, "span", core_swap),
        lax.ppermute(note, "head", partner),
        lax.ppermute(note, BOTH, other),
    ]
    near, far = swapped(near)
    own_q = [rest[:, start : start + HEAD_DIM] for start in range(2 * pair, rest.shape[1], HEAD_DIM)]
    own_q[0], block_one, block_two = after(own_q[0], rest[:, :pair], rest[:, pair : 2 * pair])
    their_q = [lax.ppermute(own_q[0], "head", partner), None, None]
    above, below = sides(block_one)
    note = combined(jnp.concatenate(notes))
    squares = note[K_NORM : K_NORM + heads] * note[Q_NORM : Q_NORM + heads]
    plain = (squares * (1.05 * SCALE**2) < PLAIN_LIMIT**2).astype(jnp.int32)
    ends = note[:spans].astype(jnp.int32)

    core, y, side = run % 2, rank // 2, rank % 2
    offsets = jnp.stack([side, 1 - side])[None, :, None] * HEAD_DIM
    position = jnp.arange(ZONES)[:, None, None] * 2048 + offsets + jnp.arange(HEAD_DIM)[None, None, :]
    position = (position + (core * 1024 + y * SEGMENT)).reshape(ZONES, SEGMENT)
    reach = jnp.min(
        jnp.where(ends > position[..., None], ends, runs * groups * chunk), axis=2
    )
    reach = jnp.maximum(reach - side * HEAD_DIM, 0)
    seen = (reach // SEGMENT) * HEAD_DIM + jnp.minimum(reach % SEGMENT, HEAD_DIM)
    seen = seen.astype(jnp.int32)
    counts = jnp.maximum((jnp.max(seen, axis=1) + WIDTH - 1) // WIDTH, 1)
    info = jnp.concatenate([jnp.stack([core, y]), counts, plain]).astype(jnp.int32)
    seen = seen.reshape(ZONES, 1, SEGMENT)

    parts = [None] * (2 * heads)

    def attended(info, head, their_q, at, sources):
        parts[2 * head], theirs = attend(info, rest, their_q, at, seen, sources, head)
        info, theirs = after(info, theirs)
        parts[2 * head + 1] = lax.ppermute(theirs, "head", partner)
        return info

    info, block_two, above, below = after(info, block_two, above, below)
    opposite = lax.ppermute(below, "head", up)
    above_two, below_two = sides(block_two)
    own_q[1], own_q[2], info = after(own_q[1], own_q[2], info)
    their_q[1] = lax.ppermute(own_q[1], "head", partner)
    info = attended(info, 0, their_q[0], 0, (near, far))
    info, opposite, above_two, below_two, their_q[1] = after(
        info, opposite, above_two, below_two, their_q[1]
    )
    near, far = swapped(jnp.stack([block_one, above, below, opposite]))
    opposite = lax.ppermute(above_two, "head", down)
    near_two, far_two = swapped(jnp.stack([block_two, above_two, below_two]))
    their_q[2] = lax.ppermute(own_q[2], "head", partner)
    info = attended(info, 1, their_q[1], 0, (near, far))
    info, opposite, their_q[2] = after(info, opposite, their_q[2])
    last, far_last = swapped(opposite[None])
    info = attended(info, 2, their_q[2], 0, (near_two, last, far_two, far_last))
    mixed = exchange(merge(parts))
    gates = gate_rows(span_ids, timesteps, time_weight)
    return pl.pallas_call(
        gate_kernel, out_shape=jax.ShapeDtypeStruct((chunk, width), jnp.bfloat16)
    )(gates, mixed)


def solution(mesh):
    return jax.shard_map(
        per_device,
        mesh=mesh,
        in_specs=(
            P(("span", "head"), None),
            P(("span", "head"), None),
            P(("span", "head"), None),
            P(("span", "head")),
            P(),
            P(),
        ),
        out_specs=P(("span", "head"), None),
        check_vma=False,
    )
```

```python
import functools
import math

import jax
import jax.numpy as jnp
from jax import lax
from jax.experimental import pallas as pl
from jax.experimental.pallas import tpu as pltpu
from jax.sharding import PartitionSpec as P

HEAD_DIM = 128
SCALE = HEAD_DIM**-0.5
SCALE_LOG2 = SCALE * math.log2(math.e)
BOTH = ("span", "head")
ZONES = 8
SEGMENT = 2 * HEAD_DIM
KEYS = 8192
WIDTH = 256
ITEMS = 8
FIRST_ZONES = 2
K_NORM, Q_NORM = 32, 40
NOTE = 16
PLAIN_LIMIT = 70.0
LOW = -1e30


def dot(a, b):
    return jnp.dot(a, b, preferred_element_type=jnp.float32)


def attend_kernel(head, info_ref, own_q, their_q, end_ref, *refs):
    sources, refs = refs[:-8], refs[-8:]
    own_out, their_out, kv_ref, qt_ref, weight_ref, acc_ref, top_ref, sems = refs
    core, rank = info_ref[0], info_ref[1]
    blocks = ZONES

    copies = []
    half = len(sources) // 2
    for j, zones in enumerate((pl.ds(0, FIRST_ZONES), pl.ds(FIRST_ZONES, ZONES - FIRST_ZONES))):
        for group, c in ((sources[:half], core), (sources[half:], 1 - core)):
            pieces = [src.at[k] for src in group for k in range(src.shape[0])]
            for piece, step in zip(pieces, (0, 1, 3, 2)):
                copies.append(
                    pltpu.make_async_copy(
                        piece.at[zones, pl.ds(0, 2 * HEAD_DIM)],
                        kv_ref.at[(rank + step) % 4, c, zones],
                        sems.at[len(copies)],
                    )
                )
    for copy in copies:
        copy.start()

    for zone in range(ZONES):
        qt_ref[zone] = jnp.concatenate([own_q[zone], their_q[zone]], axis=1)
    acc_ref[...] = jnp.zeros_like(acc_ref)
    top_ref[...] = jnp.zeros_like(top_ref)
    ones = jnp.ones((NOTE, WIDTH), jnp.bfloat16)
    for copy in copies[: len(copies) // 2]:
        copy.wait()

    def part(i, rows):
        return kv_ref[pl.ds((i % 2) * 2, 2), (i // 2) % 2, i // 4, rows]

    def keys_at(i):
        return part(i, slice(0, HEAD_DIM)).reshape(WIDTH, HEAD_DIM)

    def values_at(i):
        block = part(i, slice(HEAD_DIM, 2 * HEAD_DIM))
        return jnp.concatenate([jnp.concatenate([block[0], block[1]], axis=1), ones], axis=0)

    def visible_at(r, i):
        row = lax.broadcasted_iota(jnp.int32, (WIDTH, SEGMENT), 0)
        return row < end_ref[r] - i * WIDTH

    def score(item):
        r, i = item
        return dot(keys_at(i), qt_ref[jnp.minimum(r, blocks - 1)])

    def weigh(slot, item, scores):
        r, i = item
        weights = jnp.exp2(scores * SCALE_LOG2)
        weights = jnp.where(visible_at(jnp.minimum(r, blocks - 1), i), weights, 0.0)
        weight_ref[slot] = weights.astype(jnp.bfloat16)

    def absorb(slot, item):
        r, i = item
        acc_ref[r] += dot(values_at(i), weight_ref[slot])

    def careful(r, i):
        scores = dot(keys_at(i), qt_ref[r]) * SCALE_LOG2
        visible = visible_at(r, i)
        scores = jnp.where(visible, scores, LOW)
        old = top_ref[r, :1]
        new = jnp.maximum(old, jnp.max(scores, axis=0, keepdims=True))
        weights = jnp.where(visible, jnp.exp2(scores - new), 0.0).astype(jnp.bfloat16)
        acc_ref[r] = acc_ref[r] * jnp.exp2(old - new) + dot(values_at(i), weights)
        top_ref[r] = jnp.broadcast_to(new, top_ref.shape[1:])

    def count(r):
        return info_ref[2 + r]

    plain = info_ref[2 + blocks + head] == 1

    @pl.when(plain)
    def _():
        def following(item):
            r, i = item
            over = i + 1 >= count(jnp.minimum(r, blocks - 1))
            over = jnp.logical_or(over, r >= blocks)
            return jnp.where(over, jnp.minimum(r + 1, blocks), r), jnp.where(over, 0, i + 1)

        def run(item):
            items = [item]
            for _ in range(ITEMS - 1):
                items.append(following(items[-1]))
            return tuple(items)

        def step(_, items):
            later = run(following(items[-1]))
            scores = score(later[0])
            for slot in range(ITEMS):
                now = scores
                if slot + 1 < ITEMS:
                    scores = score(later[slot + 1])
                absorb(slot, items[slot])
                weigh(slot, later[slot], now)
            return later

        items = run((jnp.int32(0), jnp.int32(0)))
        for slot in range(ITEMS):
            weigh(slot, items[slot], score(items[slot]))
        for copy in copies[len(copies) // 2 :]:
            copy.wait()
        total = sum(count(r) for r in range(blocks))
        items = lax.fori_loop(0, (total + ITEMS - 1) // ITEMS - 1, step, items)
        for slot in range(ITEMS):
            absorb(slot, items[slot])

    @pl.when(jnp.logical_not(plain))
    def _():
        top_ref[...] = jnp.full_like(top_ref, LOW)
        for copy in copies[len(copies) // 2 :]:
            copy.wait()

        def over_block(r, carry):
            def over_chunk(i, carry):
                careful(r, i)
                return carry

            return lax.fori_loop(0, count(r), over_chunk, carry)

        lax.fori_loop(0, blocks, over_block, 0)

    for r in range(blocks):
        acc = acc_ref[r]
        total = acc[HEAD_DIM : HEAD_DIM + 1]
        some = total > 0.0
        safe = jnp.where(some, total, 1.0)
        mean = (acc[:HEAD_DIM] * jnp.where(some, 1.0 / safe, 0.0)).astype(jnp.bfloat16)
        level = jnp.where(some, top_ref[r, :1] + jnp.log2(safe), LOW)
        high = level.astype(jnp.bfloat16).astype(jnp.float32)
        middle = (level - high).astype(jnp.bfloat16).astype(jnp.float32)
        low = level - high - middle
        spare = jnp.zeros((NOTE - 3, SEGMENT), jnp.float32)
        note = jnp.concatenate([high, middle, low, spare]).astype(jnp.bfloat16)
        for out, at in ((own_out, slice(0, HEAD_DIM)), (their_out, slice(HEAD_DIM, SEGMENT))):
            out[r, :HEAD_DIM, :] = mean[:, at]
            out[r, HEAD_DIM:, :] = note[:, at]


def attend(info, own_q, their_q, at, ends, sources, head):
    rows = ZONES * SEGMENT
    out = jax.ShapeDtypeStruct((ZONES, HEAD_DIM + NOTE, HEAD_DIM), jnp.bfloat16)
    first = own_q.shape[1] // HEAD_DIM - 3
    own_spec = pl.BlockSpec((ZONES, HEAD_DIM, HEAD_DIM), lambda i, *_: (0, first + head, 0))
    their_spec = pl.BlockSpec((ZONES, HEAD_DIM, HEAD_DIM), lambda i, *_: (0, at, 0))
    whole = pl.BlockSpec(memory_space=pltpu.VMEM)
    return pl.pallas_call(
        functools.partial(attend_kernel, head),
        grid_spec=pltpu.PrefetchScalarGridSpec(
            num_scalar_prefetch=1,
            grid=(1,),
            in_specs=[own_spec, their_spec, whole]
            + [pl.BlockSpec(memory_space=pl.ANY)] * len(sources),
            out_specs=[whole, whole],
            scratch_shapes=[
                pltpu.VMEM((4, 2, ZONES, 2 * HEAD_DIM, HEAD_DIM), jnp.bfloat16),
                pltpu.VMEM((ZONES, HEAD_DIM, SEGMENT), jnp.bfloat16),
                pltpu.VMEM((ITEMS, WIDTH, SEGMENT), jnp.bfloat16),
                pltpu.VMEM((ZONES + 1, HEAD_DIM + NOTE, SEGMENT), jnp.float32),
                pltpu.VMEM((ZONES, 8, SEGMENT), jnp.float32),
                pltpu.SemaphoreType.DMA((16,)),
            ],
        ),
        out_shape=[out, out],
        compiler_params=pltpu.CompilerParams(vmem_limit_bytes=58 << 20),
        cost_estimate=pl.CostEstimate(
            flops=4 * rows * KEYS * HEAD_DIM,
            bytes_accessed=4 * KEYS * HEAD_DIM + 4 * rows * HEAD_DIM,
            transcendentals=rows * KEYS // 2,
        ),
    )(info, own_q, their_q, ends, *sources)


def pack_first_kernel(head, queries_ref, keys_ref, values_ref, ids_ref, out_ref):
    groups = out_ref.shape[0]
    heads = keys_ref.shape[1] // HEAD_DIM // groups
    ids = jnp.broadcast_to(ids_ref[...].astype(jnp.float32), (HEAD_DIM, HEAD_DIM)).T
    lane = lax.broadcasted_iota(jnp.int32, (HEAD_DIM, HEAD_DIM), 1)
    counts = jnp.sum(jnp.where(ids <= lane.astype(jnp.float32), 1.0, 0.0), axis=0, keepdims=True)
    ones = jnp.ones((HEAD_DIM, HEAD_DIM), jnp.bfloat16)
    lane = lane[:1]
    for g in range(groups):
        at = slice((g * heads + head) * HEAD_DIM, (g * heads + head + 1) * HEAD_DIM)
        out_ref[g, :HEAD_DIM] = keys_ref[:, at]
        out_ref[g, HEAD_DIM : 2 * HEAD_DIM] = values_ref[:, at].T
        note = counts
        for first, ref in ((K_NORM, keys_ref), (Q_NORM, queries_ref)):
            for h in range(heads):
                start = (g * heads + h) * HEAD_DIM
                rows = ref[:, start : start + HEAD_DIM].astype(jnp.float32)
                norm = jnp.max(dot((rows * rows).astype(jnp.bfloat16), ones), axis=0, keepdims=True)
                note = jnp.where(lane == first + h, norm * 1.02, note)
        out_ref[g, 2 * HEAD_DIM :] = jnp.broadcast_to(note, (NOTE, HEAD_DIM)).astype(jnp.bfloat16)


def pack_rest_kernel(others, queries_ref, keys_ref, values_ref, out_ref):
    groups = out_ref.shape[0]
    heads = keys_ref.shape[1] // HEAD_DIM // groups
    for g in range(groups):
        parts = [p for head in others for p in ((keys_ref, head, False), (values_ref, head, True))]
        parts += [(queries_ref, head, True) for head in range(heads)]
        for j, (ref, head, turn) in enumerate(parts):
            at = slice((g * heads + head) * HEAD_DIM, (g * heads + head + 1) * HEAD_DIM)
            out_ref[g, j * HEAD_DIM : (j + 1) * HEAD_DIM] = ref[:, at].T if turn else ref[:, at]


def pack(kernel, rows, *args):
    return pl.pallas_call(
        kernel, out_shape=jax.ShapeDtypeStruct((ZONES, rows, HEAD_DIM), jnp.bfloat16)
    )(*args)


def merge_kernel(*refs):
    out = refs[-1]

    def level(ref, zone):
        note = ref[zone, HEAD_DIM:, :].astype(jnp.float32)
        return note[0:1] + note[1:2] + note[2:3]

    for head in range(len(refs) // 2):
        one, two = refs[2 * head], refs[2 * head + 1]
        at = slice(head * HEAD_DIM, (head + 1) * HEAD_DIM)
        for zone in range(ZONES):
            share = 1.0 / (1.0 + jnp.exp2(level(two, zone) - level(one, zone)))
            a, b = (ref[zone, :HEAD_DIM, :].astype(jnp.float32) for ref in (one, two))
            out[zone, at, :] = (b + (a - b) * share).astype(jnp.bfloat16)


def merge(parts):
    return pack(merge_kernel, len(parts) // 2 * HEAD_DIM, *parts)


def gate_kernel(gate_ref, mixed_ref, out_ref):
    groups, local, _ = mixed_ref.shape
    for g in range(groups):
        for h in range(0, local, HEAD_DIM):
            at = slice(g * local + h, g * local + h + HEAD_DIM)
            attended = mixed_ref[g, h : h + HEAD_DIM, :].T.astype(jnp.float32)
            out_ref[:, at] = (gate_ref[:, at] * attended).astype(jnp.bfloat16)


def gate_rows(span_ids, timesteps, time_weight):
    half = time_weight.shape[0] // 2
    freqs = jnp.exp(-math.log(10000.0) * jnp.arange(half, dtype=jnp.float32) / half)
    angles = timesteps.astype(jnp.float32)[:, None] * freqs[None, :]
    embed = jnp.concatenate([jnp.cos(angles), jnp.sin(angles)], axis=1).astype(jnp.bfloat16)
    gate_table = jnp.dot(embed, time_weight, preferred_element_type=jnp.float32)
    onehot = (span_ids[:, None] == jnp.arange(timesteps.shape[0], dtype=jnp.int32)[None, :]).astype(
        jnp.float32
    )
    return jnp.dot(onehot, gate_table, precision=lax.Precision.HIGHEST)


def per_device(queries, keys, values, span_ids, timesteps, time_weight):
    runs, groups = lax.axis_size("span"), lax.axis_size("head")
    run, rank = lax.axis_index("span"), lax.axis_index("head")
    spans = timesteps.shape[0]
    chunk, width = queries.shape
    local = width // groups
    heads = local // HEAD_DIM

    def device(zone, core, y, x):
        return (2 * zone + core) * groups + 2 * y + x

    across = [
        [device(zone, core, y, x) for zone in range(ZONES)]
        for core in range(2)
        for y in range(4)
        for x in range(2)
    ]
    up = [(h, (h + 2) % groups) for h in range(groups)]
    down = [(h, (h - 2) % groups) for h in range(groups)]
    core_swap = [(s, s ^ 1) for s in range(runs)]
    other = [((s * groups + h), ((s ^ 1) * groups + (h ^ 1))) for s in range(runs) for h in range(groups)]
    partner = [(h, h ^ 1) for h in range(groups)]

    def exchange(parts):
        return lax.all_to_all(
            parts, BOTH, split_axis=0, concat_axis=0, axis_index_groups=across, tiled=True
        )

    def after(*values):
        return lax.optimization_barrier(values)

    def swapped(block):
        return block, lax.ppermute(block, "span", core_swap)

    def sides(block):
        return lax.ppermute(block, "head", down), lax.ppermute(block, "head", up)

    pair = 2 * HEAD_DIM
    note_rows = span_ids.reshape(1, -1)
    first = pack(
        functools.partial(pack_first_kernel, 0), pair + NOTE, queries, keys, values, note_rows
    )
    first = exchange(first)
    above, below = sides(first)
    queries, first = after(queries, first)
    rest = pack(
        functools.partial(pack_rest_kernel, (1, 2)), 2 * pair + local, queries, keys, values
    )
    rest = exchange(rest)
    near = jnp.stack([first, above, below, lax.ppermute(above, "head", down)])

    def combined(notes):
        is_count = jnp.arange(HEAD_DIM) < K_NORM
        return jnp.where(is_count, jnp.sum(notes, axis=0), jnp.max(notes, axis=0))

    note = combined(near[:, :, pair].reshape(-1, HEAD_DIM).astype(jnp.float32))[None]
    rest, near, note = after(rest, near, note)
    own_q = [rest[:, start : start + HEAD_DIM] for start in range(2 * pair, rest.shape[1], HEAD_DIM)]
    own_q[0], block_one, block_two = after(own_q[0], rest[:, :pair], rest[:, pair : 2 * pair])
    above, below = sides(block_one)
    their_q = [lax.ppermute(own_q[0], "head", partner), None, None]
    near, far = swapped(near)
    note, their_q[0] = after(note, their_q[0])
    notes = [
        note,
        lax.ppermute(note, "span", core_swap),
        lax.ppermute(note, "head", partner),
        lax.ppermute(note, BOTH, other),
    ]
    note = combined(jnp.concatenate(notes))
    squares = note[K_NORM : K_NORM + heads] * note[Q_NORM : Q_NORM + heads]
    plain = (squares * (1.05 * SCALE**2) < PLAIN_LIMIT**2).astype(jnp.int32)
    ends = note[:spans].astype(jnp.int32)

    core, y, side = run % 2, rank // 2, rank % 2
    offsets = jnp.stack([side, 1 - side])[None, :, None] * HEAD_DIM
    position = jnp.arange(ZONES)[:, None, None] * 2048 + offsets + jnp.arange(HEAD_DIM)[None, None, :]
    position = (position + (core * 1024 + y * SEGMENT)).reshape(ZONES, SEGMENT)
    reach = jnp.min(
        jnp.where(ends > position[..., None], ends, runs * groups * chunk), axis=2
    )
    reach = jnp.maximum(reach - side * HEAD_DIM, 0)
    seen = (reach // SEGMENT) * HEAD_DIM + jnp.minimum(reach % SEGMENT, HEAD_DIM)
    seen = seen.astype(jnp.int32)
    counts = jnp.maximum((jnp.max(seen, axis=1) + WIDTH - 1) // WIDTH, 1)
    info = jnp.concatenate([jnp.stack([core, y]), counts, plain]).astype(jnp.int32)
    seen = seen.reshape(ZONES, 1, SEGMENT)

    parts = [None] * (2 * heads)

    def attended(info, head, their_q, at, sources):
        parts[2 * head], theirs = attend(info, rest, their_q, at, seen, sources, head)
        info, theirs = after(info, theirs)
        parts[2 * head + 1] = lax.ppermute(theirs, "head", partner)
        return info

    info, block_two, above, below = after(info, block_two, above, below)
    opposite = lax.ppermute(below, "head", up)
    above_two, below_two = sides(block_two)
    own_q[1], own_q[2], info = after(own_q[1], own_q[2], info)
    their_q[1] = lax.ppermute(own_q[1], "head", partner)
    info = attended(info, 0, their_q[0], 0, (near, far))
    info, opposite, above_two, below_two, their_q[1] = after(
        info, opposite, above_two, below_two, their_q[1]
    )
    near, far = swapped(jnp.stack([block_one, above, below, opposite]))
    opposite = lax.ppermute(above_two, "head", down)
    near_two, far_two = swapped(jnp.stack([block_two, above_two, below_two]))
    their_q[2] = lax.ppermute(own_q[2], "head", partner)
    info = attended(info, 1, their_q[1], 0, (near, far))
    info, opposite, their_q[2] = after(info, opposite, their_q[2])
    last, far_last = swapped(opposite[None])
    info = attended(info, 2, their_q[2], 0, (near_two, last, far_two, far_last))
    mixed = exchange(merge(parts))
    gates = gate_rows(span_ids, timesteps, time_weight)
    return pl.pallas_call(
        gate_kernel, out_shape=jax.ShapeDtypeStruct((chunk, width), jnp.bfloat16)
    )(gates, mixed)


def solution(mesh):
    return jax.shard_map(
        per_device,
        mesh=mesh,
        in_specs=(
            P(("span", "head"), None),
            P(("span", "head"), None),
            P(("span", "head"), None),
            P(("span", "head")),
            P(),
            P(),
        ),
        out_specs=P(("span", "head"), None),
        check_vma=False,
    )
```

```python
import functools
import math

import jax
import jax.numpy as jnp
from jax import lax
from jax.experimental import pallas as pl
from jax.experimental.pallas import tpu as pltpu
from jax.sharding import PartitionSpec as P

HEAD_DIM = 128
SCALE = HEAD_DIM**-0.5
SCALE_LOG2 = SCALE * math.log2(math.e)
BOTH = ("span", "head")
ZONES = 8
SEGMENT = 2 * HEAD_DIM
KEYS = 8192
WIDTH = 256
ITEMS = 8
FIRST_ZONES = 2
K_NORM, Q_NORM = 32, 40
NOTE = 16
PLAIN_LIMIT = 70.0
LOW = -1e30


def dot(a, b):
    return jnp.dot(a, b, preferred_element_type=jnp.float32)


def attend_kernel(head, info_ref, own_q, their_q, end_ref, *refs):
    sources, refs = refs[:-8], refs[-8:]
    own_out, their_out, kv_ref, qt_ref, weight_ref, acc_ref, top_ref, sems = refs
    core, rank = info_ref[0], info_ref[1]
    blocks = ZONES

    copies = []
    half = len(sources) // 2
    for j, zones in enumerate((pl.ds(0, FIRST_ZONES), pl.ds(FIRST_ZONES, ZONES - FIRST_ZONES))):
        for group, c in ((sources[:half], core), (sources[half:], 1 - core)):
            pieces = [src.at[k] for src in group for k in range(src.shape[0])]
            for piece, step in zip(pieces, (0, 1, 3, 2)):
                copies.append(
                    pltpu.make_async_copy(
                        piece.at[zones, pl.ds(0, 2 * HEAD_DIM)],
                        kv_ref.at[(rank + step) % 4, c, zones],
                        sems.at[len(copies)],
                    )
                )
    for copy in copies:
        copy.start()

    for zone in range(ZONES):
        qt_ref[zone] = jnp.concatenate([own_q[zone], their_q[zone]], axis=1)
    acc_ref[...] = jnp.zeros_like(acc_ref)
    top_ref[...] = jnp.zeros_like(top_ref)
    ones = jnp.ones((NOTE, WIDTH), jnp.bfloat16)
    for copy in copies[: len(copies) // 2]:
        copy.wait()

    def part(i, rows):
        return kv_ref[pl.ds((i % 2) * 2, 2), (i // 2) % 2, i // 4, rows]

    def keys_at(i):
        return part(i, slice(0, HEAD_DIM)).reshape(WIDTH, HEAD_DIM)

    def values_at(i):
        block = part(i, slice(HEAD_DIM, 2 * HEAD_DIM))
        return jnp.concatenate([jnp.concatenate([block[0], block[1]], axis=1), ones], axis=0)

    def visible_at(r, i):
        row = lax.broadcasted_iota(jnp.int32, (WIDTH, SEGMENT), 0)
        return row < end_ref[r] - i * WIDTH

    def score(item):
        r, i = item
        return dot(keys_at(i), qt_ref[jnp.minimum(r, blocks - 1)])

    def weigh(slot, item, scores):
        r, i = item
        weights = jnp.exp2(scores * SCALE_LOG2)
        weights = jnp.where(visible_at(jnp.minimum(r, blocks - 1), i), weights, 0.0)
        weight_ref[slot] = weights.astype(jnp.bfloat16)

    def absorb(slot, item):
        r, i = item
        acc_ref[r] += dot(values_at(i), weight_ref[slot])

    def careful(r, i):
        scores = dot(keys_at(i), qt_ref[r]) * SCALE_LOG2
        visible = visible_at(r, i)
        scores = jnp.where(visible, scores, LOW)
        old = top_ref[r, :1]
        new = jnp.maximum(old, jnp.max(scores, axis=0, keepdims=True))
        weights = jnp.where(visible, jnp.exp2(scores - new), 0.0).astype(jnp.bfloat16)
        acc_ref[r] = acc_ref[r] * jnp.exp2(old - new) + dot(values_at(i), weights)
        top_ref[r] = jnp.broadcast_to(new, top_ref.shape[1:])

    def count(r):
        return info_ref[2 + r]

    plain = info_ref[2 + blocks + head] == 1

    @pl.when(plain)
    def _():
        def following(item):
            r, i = item
            over = i + 1 >= count(jnp.minimum(r, blocks - 1))
            over = jnp.logical_or(over, r >= blocks)
            return jnp.where(over, jnp.minimum(r + 1, blocks), r), jnp.where(over, 0, i + 1)

        def run(item):
            items = [item]
            for _ in range(ITEMS - 1):
                items.append(following(items[-1]))
            return tuple(items)

        def step(_, items):
            later = run(following(items[-1]))
            scores = score(later[0])
            for slot in range(ITEMS):
                now = scores
                if slot + 1 < ITEMS:
                    scores = score(later[slot + 1])
                absorb(slot, items[slot])
                weigh(slot, later[slot], now)
            return later

        items = run((jnp.int32(0), jnp.int32(0)))
        for slot in range(ITEMS):
            weigh(slot, items[slot], score(items[slot]))
        for copy in copies[len(copies) // 2 :]:
            copy.wait()
        total = sum(count(r) for r in range(blocks))
        items = lax.fori_loop(0, (total + ITEMS - 1) // ITEMS - 1, step, items)
        for slot in range(ITEMS):
            absorb(slot, items[slot])

    @pl.when(jnp.logical_not(plain))
    def _():
        top_ref[...] = jnp.full_like(top_ref, LOW)
        for copy in copies[len(copies) // 2 :]:
            copy.wait()

        def over_block(r, carry):
            def over_chunk(i, carry):
                careful(r, i)
                return carry

            return lax.fori_loop(0, count(r), over_chunk, carry)

        lax.fori_loop(0, blocks, over_block, 0)

    for r in range(blocks):
        acc = acc_ref[r]
        total = acc[HEAD_DIM : HEAD_DIM + 1]
        some = total > 0.0
        safe = jnp.where(some, total, 1.0)
        mean = (acc[:HEAD_DIM] * jnp.where(some, 1.0 / safe, 0.0)).astype(jnp.bfloat16)
        level = jnp.where(some, top_ref[r, :1] + jnp.log2(safe), LOW)
        high = level.astype(jnp.bfloat16).astype(jnp.float32)
        middle = (level - high).astype(jnp.bfloat16).astype(jnp.float32)
        low = level - high - middle
        spare = jnp.zeros((NOTE - 3, SEGMENT), jnp.float32)
        note = jnp.concatenate([high, middle, low, spare]).astype(jnp.bfloat16)
        for out, at in ((own_out, slice(0, HEAD_DIM)), (their_out, slice(HEAD_DIM, SEGMENT))):
            out[r, :HEAD_DIM, :] = mean[:, at]
            out[r, HEAD_DIM:, :] = note[:, at]


def attend(info, own_q, at, their_q, ends, sources, head):
    rows = ZONES * SEGMENT
    out = jax.ShapeDtypeStruct((ZONES, HEAD_DIM + NOTE, HEAD_DIM), jnp.bfloat16)
    own_spec = pl.BlockSpec((ZONES, HEAD_DIM, HEAD_DIM), lambda i, *_: (0, at, 0))
    whole = pl.BlockSpec(memory_space=pltpu.VMEM)
    return pl.pallas_call(
        functools.partial(attend_kernel, head),
        grid_spec=pltpu.PrefetchScalarGridSpec(
            num_scalar_prefetch=1,
            grid=(1,),
            in_specs=[own_spec, whole, whole]
            + [pl.BlockSpec(memory_space=pl.ANY)] * len(sources),
            out_specs=[whole, whole],
            scratch_shapes=[
                pltpu.VMEM((4, 2, ZONES, 2 * HEAD_DIM, HEAD_DIM), jnp.bfloat16),
                pltpu.VMEM((ZONES, HEAD_DIM, SEGMENT), jnp.bfloat16),
                pltpu.VMEM((ITEMS, WIDTH, SEGMENT), jnp.bfloat16),
                pltpu.VMEM((ZONES + 1, HEAD_DIM + NOTE, SEGMENT), jnp.float32),
                pltpu.VMEM((ZONES, 8, SEGMENT), jnp.float32),
                pltpu.SemaphoreType.DMA((16,)),
            ],
        ),
        out_shape=[out, out],
        compiler_params=pltpu.CompilerParams(vmem_limit_bytes=24 << 20),
        cost_estimate=pl.CostEstimate(
            flops=4 * rows * KEYS * HEAD_DIM,
            bytes_accessed=4 * KEYS * HEAD_DIM + 4 * rows * HEAD_DIM,
            transcendentals=rows * KEYS // 2,
        ),
    )(info, own_q, their_q, ends, *sources)


def pack_kernel(queries_ref, keys_ref, values_ref, ids_ref, first_ref, rest_ref):
    groups = first_ref.shape[0]
    heads = keys_ref.shape[1] // HEAD_DIM // groups
    ids = jnp.broadcast_to(ids_ref[...].astype(jnp.float32), (HEAD_DIM, HEAD_DIM)).T
    lane = lax.broadcasted_iota(jnp.int32, (HEAD_DIM, HEAD_DIM), 1)
    counts = jnp.sum(jnp.where(ids <= lane.astype(jnp.float32), 1.0, 0.0), axis=0, keepdims=True)
    local = heads * HEAD_DIM
    row = lax.broadcasted_iota(jnp.int32, (2 * local, HEAD_DIM), 0) // HEAD_DIM
    column = lax.broadcasted_iota(jnp.int32, (2 * local, HEAD_DIM), 1)
    wanted = jnp.where(row < heads, row + K_NORM, row - heads + Q_NORM)
    pick = jnp.where(column == wanted, 1.0, 0.0).astype(jnp.bfloat16)
    is_count = lane[:1] < K_NORM
    queries, keys, values = (queries_ref, True), (keys_ref, False), (values_ref, True)
    first = [(queries, 0, 0), (keys, 0, 128), (values, 0, 256), (keys, 1, 400), (values, 1, 528)]
    rest = [(keys, 2, 0), (values, 2, 128), (queries, 1, 256), (queries, 2, 384)]
    for g in range(groups):
        for out_ref, parts in ((first_ref, first), (rest_ref, rest)):
            for (ref, turn), head, at in parts:
                start = g * local + head * HEAD_DIM
                block = ref[:, start : start + HEAD_DIM]
                out_ref[g, at : at + HEAD_DIM] = block.T if turn else block
        rows = [ref[:, g * local : (g + 1) * local].astype(jnp.float32) for ref in (keys_ref, queries_ref)]
        squares = jnp.concatenate([(x * x).astype(jnp.bfloat16) for x in rows], axis=1)
        norms = jnp.max(dot(squares, pick), axis=0, keepdims=True) * 1.02
        note = jnp.where(is_count, counts, norms)
        note = jnp.broadcast_to(note, (NOTE, HEAD_DIM)).astype(jnp.bfloat16)
        first_ref[g, 3 * HEAD_DIM : 3 * HEAD_DIM + NOTE] = note


def packed(rows):
    return jax.ShapeDtypeStruct((ZONES, rows, HEAD_DIM), jnp.bfloat16)


def merge_kernel(*refs):
    out = refs[-1]

    def level(ref, zone):
        note = ref[zone, HEAD_DIM:, :].astype(jnp.float32)
        return note[0:1] + note[1:2] + note[2:3]

    for head in range(len(refs) // 2):
        one, two = refs[2 * head], refs[2 * head + 1]
        at = slice(head * HEAD_DIM, (head + 1) * HEAD_DIM)
        for zone in range(ZONES):
            share = 1.0 / (1.0 + jnp.exp2(level(two, zone) - level(one, zone)))
            a, b = (ref[zone, :HEAD_DIM, :].astype(jnp.float32) for ref in (one, two))
            out[zone, at, :] = (b + (a - b) * share).astype(jnp.bfloat16)


def merge(parts):
    return pl.pallas_call(merge_kernel, out_shape=packed(len(parts) // 2 * HEAD_DIM))(*parts)


def gate_kernel(gate_ref, mixed_ref, out_ref):
    groups, local, _ = mixed_ref.shape
    for g in range(groups):
        for h in range(0, local, HEAD_DIM):
            at = slice(g * local + h, g * local + h + HEAD_DIM)
            attended = mixed_ref[g, h : h + HEAD_DIM, :].T.astype(jnp.float32)
            out_ref[:, at] = (gate_ref[:, at] * attended).astype(jnp.bfloat16)


def gate_rows(span_ids, timesteps, time_weight):
    half = time_weight.shape[0] // 2
    freqs = jnp.exp(-math.log(10000.0) * jnp.arange(half, dtype=jnp.float32) / half)
    angles = timesteps.astype(jnp.float32)[:, None] * freqs[None, :]
    embed = jnp.concatenate([jnp.cos(angles), jnp.sin(angles)], axis=1).astype(jnp.bfloat16)
    gate_table = jnp.dot(embed, time_weight, preferred_element_type=jnp.float32)
    onehot = (span_ids[:, None] == jnp.arange(timesteps.shape[0], dtype=jnp.int32)[None, :]).astype(
        jnp.float32
    )
    return jnp.dot(onehot, gate_table, precision=lax.Precision.HIGHEST)


def per_device(queries, keys, values, span_ids, timesteps, time_weight):
    runs, groups = lax.axis_size("span"), lax.axis_size("head")
    run, rank = lax.axis_index("span"), lax.axis_index("head")
    spans = timesteps.shape[0]
    chunk, width = queries.shape
    local = width // groups
    heads = local // HEAD_DIM

    def device(zone, core, y, x):
        return (2 * zone + core) * groups + 2 * y + x

    across = [
        [device(zone, core, y, x) for zone in range(ZONES)]
        for core in range(2)
        for y in range(4)
        for x in range(2)
    ]
    up = [(h, (h + 2) % groups) for h in range(groups)]
    down = [(h, (h - 2) % groups) for h in range(groups)]
    core_swap = [(s, s ^ 1) for s in range(runs)]
    other = [((s * groups + h), ((s ^ 1) * groups + (h ^ 1))) for s in range(runs) for h in range(groups)]
    partner = [(h, h ^ 1) for h in range(groups)]

    def exchange(parts):
        return lax.all_to_all(
            parts, BOTH, split_axis=0, concat_axis=0, axis_index_groups=across, tiled=True
        )

    def after(*values):
        return lax.optimization_barrier(values)

    def swapped(block):
        return block, lax.ppermute(block, "span", core_swap)

    def sides(block):
        return lax.ppermute(block, "head", down), lax.ppermute(block, "head", up)

    pair = 2 * HEAD_DIM
    first, rest = pl.pallas_call(
        pack_kernel, out_shape=[packed(5 * HEAD_DIM + NOTE), packed(4 * HEAD_DIM)]
    )(queries, keys, values, span_ids.reshape(1, -1))
    first = exchange(first)
    rest, first = after(rest, first)
    rest = exchange(rest)
    one_from = 3 * HEAD_DIM + NOTE
    own_q, block, block_one = after(
        first[:, :HEAD_DIM], first[:, HEAD_DIM:one_from], first[:, one_from:]
    )
    their_q = [lax.ppermute(own_q, "head", partner), None, None]
    above, below = sides(block)
    block_one, above, below = after(block_one, above, below)
    above_one, below_one = sides(block_one)
    near = jnp.stack([block, above, below, lax.ppermute(above, "head", down)])

    def combined(notes):
        is_count = jnp.arange(HEAD_DIM) < K_NORM
        return jnp.where(is_count, jnp.sum(notes, axis=0), jnp.max(notes, axis=0))

    note = combined(near[:, :, pair].reshape(-1, HEAD_DIM).astype(jnp.float32))[None]
    note, above_one, below_one = after(note, above_one, below_one)
    notes = [
        note,
        lax.ppermute(note, "span", core_swap),
        lax.ppermute(note, "head", partner),
        lax.ppermute(note, BOTH, other),
    ]
    near, far = swapped(near)
    block_two, *own_q = after(rest[:, :pair], rest[:, pair:-HEAD_DIM], rest[:, -HEAD_DIM:])
    note = combined(jnp.concatenate(notes))
    squares = note[K_NORM : K_NORM + heads] * note[Q_NORM : Q_NORM + heads]
    plain = (squares * (1.05 * SCALE**2) < PLAIN_LIMIT**2).astype(jnp.int32)
    ends = note[:spans].astype(jnp.int32)

    core, y, side = run % 2, rank // 2, rank % 2
    offsets = jnp.stack([side, 1 - side])[None, :, None] * HEAD_DIM
    position = jnp.arange(ZONES)[:, None, None] * 2048 + offsets + jnp.arange(HEAD_DIM)[None, None, :]
    position = (position + (core * 1024 + y * SEGMENT)).reshape(ZONES, SEGMENT)
    reach = jnp.min(
        jnp.where(ends > position[..., None], ends, runs * groups * chunk), axis=2
    )
    reach = jnp.maximum(reach - side * HEAD_DIM, 0)
    seen = (reach // SEGMENT) * HEAD_DIM + jnp.minimum(reach % SEGMENT, HEAD_DIM)
    seen = seen.astype(jnp.int32)
    counts = jnp.maximum((jnp.max(seen, axis=1) + WIDTH - 1) // WIDTH, 1)
    info = jnp.concatenate([jnp.stack([core, y]), counts, plain]).astype(jnp.int32)
    seen = seen.reshape(ZONES, 1, SEGMENT)

    parts = [None] * (2 * heads)

    def attended(info, head, sources):
        own, at = (first, 0) if head == 0 else (rest, 1 + head)
        parts[2 * head], theirs = attend(info, own, at, their_q[head], seen, sources, head)
        info, theirs = after(info, theirs)
        parts[2 * head + 1] = lax.ppermute(theirs, "head", partner)
        return info

    info, block_two, above, below = after(info, block_two, above_one, below_one)
    opposite = lax.ppermute(below, "head", up)
    above_two, below_two = sides(block_two)
    own_q[0], own_q[1], info = after(own_q[0], own_q[1], info)
    their_q[1] = lax.ppermute(own_q[0], "head", partner)
    info = attended(info, 0, (near, far))
    info, opposite, above_two, below_two, their_q[1] = after(
        info, opposite, above_two, below_two, their_q[1]
    )
    near, far = swapped(jnp.stack([block_one, above, below, opposite]))
    opposite = lax.ppermute(above_two, "head", down)
    near_two, far_two = swapped(jnp.stack([block_two, above_two, below_two]))
    their_q[2] = lax.ppermute(own_q[1], "head", partner)
    info = attended(info, 1, (near, far))
    info, opposite, their_q[2] = after(info, opposite, their_q[2])
    last, far_last = swapped(opposite[None])
    info = attended(info, 2, (near_two, last, far_two, far_last))
    mixed = exchange(merge(parts))
    gates = gate_rows(span_ids, timesteps, time_weight)
    return pl.pallas_call(
        gate_kernel, out_shape=jax.ShapeDtypeStruct((chunk, width), jnp.bfloat16)
    )(gates, mixed)


def solution(mesh):
    return jax.shard_map(
        per_device,
        mesh=mesh,
        in_specs=(
            P(("span", "head"), None),
            P(("span", "head"), None),
            P(("span", "head"), None),
            P(("span", "head")),
            P(),
            P(),
        ),
        out_specs=P(("span", "head"), None),
        check_vma=False,
    )
```

```python
import functools
import math

import jax
import jax.numpy as jnp
from jax import lax
from jax.experimental import pallas as pl
from jax.experimental.pallas import tpu as pltpu
from jax.sharding import PartitionSpec as P

HEAD_DIM = 128
SCALE = HEAD_DIM**-0.5
SCALE_LOG2 = SCALE * math.log2(math.e)
BOTH = ("span", "head")
ZONES = 8
SEGMENT = 2 * HEAD_DIM
KEYS = 8192
WIDTH = 256
ITEMS = 8
FIRST_ZONES = 2
K_NORM, Q_NORM = 32, 40
NOTE = 16
PLAIN_LIMIT = 70.0
LOW = -1e30
ROOMY = pltpu.CompilerParams(vmem_limit_bytes=24 << 20)


def dot(a, b):
    return jnp.dot(a, b, preferred_element_type=jnp.float32)


def attend_kernel(head, info_ref, own_q, their_q, end_ref, *refs):
    sources, refs = refs[:-8], refs[-8:]
    own_out, their_out, kv_ref, qt_ref, weight_ref, acc_ref, top_ref, sems = refs
    core, rank = info_ref[0], info_ref[1]
    blocks = ZONES

    copies = []
    half = len(sources) // 2
    for j, zones in enumerate((pl.ds(0, FIRST_ZONES), pl.ds(FIRST_ZONES, ZONES - FIRST_ZONES))):
        for group, c in ((sources[:half], core), (sources[half:], 1 - core)):
            pieces = [src.at[k] for src in group for k in range(src.shape[0])]
            for piece, step in zip(pieces, (0, 1, 3, 2)):
                copies.append(
                    pltpu.make_async_copy(
                        piece.at[zones, pl.ds(0, 2 * HEAD_DIM)],
                        kv_ref.at[(rank + step) % 4, c, zones],
                        sems.at[len(copies)],
                    )
                )
    for copy in copies:
        copy.start()

    for zone in range(ZONES):
        qt_ref[zone] = jnp.concatenate([own_q[zone], their_q[zone]], axis=1)
    acc_ref[...] = jnp.zeros_like(acc_ref)
    top_ref[...] = jnp.zeros_like(top_ref)
    ones = jnp.ones((NOTE, WIDTH), jnp.bfloat16)
    for copy in copies[: len(copies) // 2]:
        copy.wait()

    def part(i, rows):
        return kv_ref[pl.ds((i % 2) * 2, 2), (i // 2) % 2, i // 4, rows]

    def keys_at(i):
        return part(i, slice(0, HEAD_DIM)).reshape(WIDTH, HEAD_DIM)

    def values_at(i):
        block = part(i, slice(HEAD_DIM, 2 * HEAD_DIM))
        return jnp.concatenate([jnp.concatenate([block[0], block[1]], axis=1), ones], axis=0)

    def visible_at(r, i):
        row = lax.broadcasted_iota(jnp.int32, (WIDTH, SEGMENT), 0)
        return row < end_ref[r] - i * WIDTH

    def score(item):
        r, i = item
        return dot(keys_at(i), qt_ref[jnp.minimum(r, blocks - 1)])

    def weigh(slot, item, scores):
        r, i = item
        weights = jnp.exp2(scores * SCALE_LOG2)
        weights = jnp.where(visible_at(jnp.minimum(r, blocks - 1), i), weights, 0.0)
        weight_ref[slot] = weights.astype(jnp.bfloat16)

    def absorb(slot, item):
        r, i = item
        acc_ref[r] += dot(values_at(i), weight_ref[slot])

    def careful(r, i):
        scores = dot(keys_at(i), qt_ref[r]) * SCALE_LOG2
        visible = visible_at(r, i)
        scores = jnp.where(visible, scores, LOW)
        old = top_ref[r, :1]
        new = jnp.maximum(old, jnp.max(scores, axis=0, keepdims=True))
        weights = jnp.where(visible, jnp.exp2(scores - new), 0.0).astype(jnp.bfloat16)
        acc_ref[r] = acc_ref[r] * jnp.exp2(old - new) + dot(values_at(i), weights)
        top_ref[r] = jnp.broadcast_to(new, top_ref.shape[1:])

    def count(r):
        return info_ref[2 + r]

    plain = info_ref[2 + blocks + head] == 1

    @pl.when(plain)
    def _():
        def following(item):
            r, i = item
            over = i + 1 >= count(jnp.minimum(r, blocks - 1))
            over = jnp.logical_or(over, r >= blocks)
            return jnp.where(over, jnp.minimum(r + 1, blocks), r), jnp.where(over, 0, i + 1)

        def run(item):
            items = [item]
            for _ in range(ITEMS - 1):
                items.append(following(items[-1]))
            return tuple(items)

        def step(_, items):
            later = run(following(items[-1]))
            scores = score(later[0])
            for slot in range(ITEMS):
                now = scores
                if slot + 1 < ITEMS:
                    scores = score(later[slot + 1])
                absorb(slot, items[slot])
                weigh(slot, later[slot], now)
            return later

        items = run((jnp.int32(0), jnp.int32(0)))
        for slot in range(ITEMS):
            weigh(slot, items[slot], score(items[slot]))
        for copy in copies[len(copies) // 2 :]:
            copy.wait()
        total = sum(count(r) for r in range(blocks))
        items = lax.fori_loop(0, (total + ITEMS - 1) // ITEMS - 1, step, items)
        for slot in range(ITEMS):
            absorb(slot, items[slot])

    @pl.when(jnp.logical_not(plain))
    def _():
        top_ref[...] = jnp.full_like(top_ref, LOW)
        for copy in copies[len(copies) // 2 :]:
            copy.wait()

        def over_block(r, carry):
            def over_chunk(i, carry):
                careful(r, i)
                return carry

            return lax.fori_loop(0, count(r), over_chunk, carry)

        lax.fori_loop(0, blocks, over_block, 0)

    for r in range(blocks):
        acc = acc_ref[r]
        total = acc[HEAD_DIM : HEAD_DIM + 1]
        some = total > 0.0
        safe = jnp.where(some, total, 1.0)
        mean = (acc[:HEAD_DIM] * jnp.where(some, 1.0 / safe, 0.0)).astype(jnp.bfloat16)
        level = jnp.where(some, top_ref[r, :1] + jnp.log2(safe), LOW)
        high = level.astype(jnp.bfloat16).astype(jnp.float32)
        middle = (level - high).astype(jnp.bfloat16).astype(jnp.float32)
        low = level - high - middle
        spare = jnp.zeros((NOTE - 3, SEGMENT), jnp.float32)
        note = jnp.concatenate([high, middle, low, spare]).astype(jnp.bfloat16)
        for out, at in ((own_out, slice(0, HEAD_DIM)), (their_out, slice(HEAD_DIM, SEGMENT))):
            out[r, :HEAD_DIM, :] = mean[:, at]
            out[r, HEAD_DIM:, :] = note[:, at]


def attend(info, own_q, at, their_q, ends, sources, head):
    rows = ZONES * SEGMENT
    out = jax.ShapeDtypeStruct((ZONES, HEAD_DIM + NOTE, HEAD_DIM), jnp.bfloat16)
    own_spec = pl.BlockSpec((ZONES, HEAD_DIM, HEAD_DIM), lambda i, *_: (0, at, 0))
    whole = pl.BlockSpec(memory_space=pltpu.VMEM)
    return pl.pallas_call(
        functools.partial(attend_kernel, head),
        grid_spec=pltpu.PrefetchScalarGridSpec(
            num_scalar_prefetch=1,
            grid=(1,),
            in_specs=[own_spec, whole, whole]
            + [pl.BlockSpec(memory_space=pltpu.HBM)] * len(sources),
            out_specs=[whole, whole],
            scratch_shapes=[
                pltpu.VMEM((4, 2, ZONES, 2 * HEAD_DIM, HEAD_DIM), jnp.bfloat16),
                pltpu.VMEM((ZONES, HEAD_DIM, SEGMENT), jnp.bfloat16),
                pltpu.VMEM((ITEMS, WIDTH, SEGMENT), jnp.bfloat16),
                pltpu.VMEM((ZONES + 1, HEAD_DIM + NOTE, SEGMENT), jnp.float32),
                pltpu.VMEM((ZONES, 8, SEGMENT), jnp.float32),
                pltpu.SemaphoreType.DMA((16,)),
            ],
        ),
        out_shape=[out, out],
        compiler_params=ROOMY,
        cost_estimate=pl.CostEstimate(
            flops=4 * rows * KEYS * HEAD_DIM,
            bytes_accessed=4 * KEYS * HEAD_DIM + 4 * rows * HEAD_DIM,
            transcendentals=rows * KEYS // 2,
        ),
    )(info, own_q, their_q, ends, *sources)


def pack_kernel(queries_ref, keys_ref, values_ref, ids_ref, first_ref, rest_ref):
    groups = first_ref.shape[0]
    heads = keys_ref.shape[1] // HEAD_DIM // groups
    ids = jnp.broadcast_to(ids_ref[...].astype(jnp.float32), (HEAD_DIM, HEAD_DIM)).T
    lane = lax.broadcasted_iota(jnp.int32, (HEAD_DIM, HEAD_DIM), 1)
    counts = jnp.sum(jnp.where(ids <= lane.astype(jnp.float32), 1.0, 0.0), axis=0, keepdims=True)
    local = heads * HEAD_DIM
    row = lax.broadcasted_iota(jnp.int32, (2 * local, HEAD_DIM), 0) // HEAD_DIM
    column = lax.broadcasted_iota(jnp.int32, (2 * local, HEAD_DIM), 1)
    wanted = jnp.where(row < heads, row + K_NORM, row - heads + Q_NORM)
    pick = jnp.where(column == wanted, 1.0, 0.0).astype(jnp.bfloat16)
    is_count = lane[:1] < K_NORM
    queries, keys, values = (queries_ref, True), (keys_ref, False), (values_ref, True)
    first = [(keys, 0), (values, 0)]
    rest = [(part, head) for head in range(1, heads) for part in (keys, values)]
    rest += [(queries, head) for head in range(heads)]
    for g in range(groups):
        for out_ref, parts in ((first_ref, first), (rest_ref, rest)):
            for j, ((ref, turn), head) in enumerate(parts):
                start = g * local + head * HEAD_DIM
                block = ref[:, start : start + HEAD_DIM]
                out_ref[g, j * HEAD_DIM : (j + 1) * HEAD_DIM] = block.T if turn else block
        rows = [ref[:, g * local : (g + 1) * local].astype(jnp.float32) for ref in (keys_ref, queries_ref)]
        squares = jnp.concatenate([(x * x).astype(jnp.bfloat16) for x in rows], axis=1)
        norms = jnp.max(dot(squares, pick), axis=0, keepdims=True) * 1.02
        note = jnp.where(is_count, counts, norms)
        note = jnp.broadcast_to(note, (NOTE, HEAD_DIM)).astype(jnp.bfloat16)
        first_ref[g, len(first) * HEAD_DIM :] = note


def packed(rows):
    return jax.ShapeDtypeStruct((ZONES, rows, HEAD_DIM), jnp.bfloat16)


def merge_kernel(*refs):
    out = refs[-1]

    def level(ref, zone):
        note = ref[zone, HEAD_DIM:, :].astype(jnp.float32)
        return note[0:1] + note[1:2] + note[2:3]

    for head in range(len(refs) // 2):
        one, two = refs[2 * head], refs[2 * head + 1]
        at = slice(head * HEAD_DIM, (head + 1) * HEAD_DIM)
        for zone in range(ZONES):
            share = 1.0 / (1.0 + jnp.exp2(level(two, zone) - level(one, zone)))
            a, b = (ref[zone, :HEAD_DIM, :].astype(jnp.float32) for ref in (one, two))
            out[zone, at, :] = (b + (a - b) * share).astype(jnp.bfloat16)


def merge(parts):
    return pl.pallas_call(merge_kernel, out_shape=packed(len(parts) // 2 * HEAD_DIM), compiler_params=ROOMY)(*parts)


def gate_kernel(gate_ref, mixed_ref, out_ref):
    groups, local, _ = mixed_ref.shape
    for g in range(groups):
        for h in range(0, local, HEAD_DIM):
            at = slice(g * local + h, g * local + h + HEAD_DIM)
            attended = mixed_ref[g, h : h + HEAD_DIM, :].T.astype(jnp.float32)
            out_ref[:, at] = (gate_ref[:, at] * attended).astype(jnp.bfloat16)


def gate_rows(span_ids, timesteps, time_weight):
    half = time_weight.shape[0] // 2
    freqs = jnp.exp(-math.log(10000.0) * jnp.arange(half, dtype=jnp.float32) / half)
    angles = timesteps.astype(jnp.float32)[:, None] * freqs[None, :]
    embed = jnp.concatenate([jnp.cos(angles), jnp.sin(angles)], axis=1).astype(jnp.bfloat16)
    gate_table = jnp.dot(embed, time_weight, preferred_element_type=jnp.float32)
    onehot = (span_ids[:, None] == jnp.arange(timesteps.shape[0], dtype=jnp.int32)[None, :]).astype(
        jnp.float32
    )
    return jnp.dot(onehot, gate_table, precision=lax.Precision.HIGHEST)


def per_device(queries, keys, values, span_ids, timesteps, time_weight):
    runs, groups = lax.axis_size("span"), lax.axis_size("head")
    run, rank = lax.axis_index("span"), lax.axis_index("head")
    spans = timesteps.shape[0]
    chunk, width = queries.shape
    local = width // groups
    heads = local // HEAD_DIM

    def device(zone, core, y, x):
        return (2 * zone + core) * groups + 2 * y + x

    across = [
        [device(zone, core, y, x) for zone in range(ZONES)]
        for core in range(2)
        for y in range(4)
        for x in range(2)
    ]
    up = [(h, (h + 2) % groups) for h in range(groups)]
    down = [(h, (h - 2) % groups) for h in range(groups)]
    core_swap = [(s, s ^ 1) for s in range(runs)]
    other = [((s * groups + h), ((s ^ 1) * groups + (h ^ 1))) for s in range(runs) for h in range(groups)]
    partner = [(h, h ^ 1) for h in range(groups)]

    def exchange(parts):
        return lax.all_to_all(
            parts, BOTH, split_axis=0, concat_axis=0, axis_index_groups=across, tiled=True
        )

    def after(*values):
        return lax.optimization_barrier(values)

    def swapped(block):
        return block, lax.ppermute(block, "span", core_swap)

    def sides(block):
        return lax.ppermute(block, "head", down), lax.ppermute(block, "head", up)

    pair = 2 * HEAD_DIM
    first, rest = pl.pallas_call(
        pack_kernel, out_shape=[packed(pair + NOTE), packed((3 * heads - 2) * HEAD_DIM)], compiler_params=ROOMY
    )(queries, keys, values, span_ids.reshape(1, -1))
    first = exchange(first)
    rest, first = after(rest, first)
    rest = exchange(rest)
    above, below = sides(first)
    near = jnp.stack([first, above, below, lax.ppermute(above, "head", down)])

    def combined(notes):
        is_count = jnp.arange(HEAD_DIM) < K_NORM
        return jnp.where(is_count, jnp.sum(notes, axis=0), jnp.max(notes, axis=0))

    note = combined(near[:, :, pair].reshape(-1, HEAD_DIM).astype(jnp.float32))[None]
    rest, near, note = after(rest, near, note)
    own_q = [rest[:, start : start + HEAD_DIM] for start in range(2 * pair, rest.shape[1], HEAD_DIM)]
    own_q[0], block_one, block_two = after(own_q[0], rest[:, :pair], rest[:, pair : 2 * pair])
    above, below = sides(block_one)
    their_q = [lax.ppermute(own_q[0], "head", partner), None, None]
    near, far = swapped(near)
    note, above, below = after(note, above, below)
    notes = [
        note,
        lax.ppermute(note, "span", core_swap),
        lax.ppermute(note, "head", partner),
        lax.ppermute(note, BOTH, other),
    ]
    note = combined(jnp.concatenate(notes))
    squares = note[K_NORM : K_NORM + heads] * note[Q_NORM : Q_NORM + heads]
    plain = (squares * (1.05 * SCALE**2) < PLAIN_LIMIT**2).astype(jnp.int32)
    ends = note[:spans].astype(jnp.int32)

    core, y, side = run % 2, rank // 2, rank % 2
    offsets = jnp.stack([side, 1 - side])[None, :, None] * HEAD_DIM
    position = jnp.arange(ZONES)[:, None, None] * 2048 + offsets + jnp.arange(HEAD_DIM)[None, None, :]
    position = (position + (core * 1024 + y * SEGMENT)).reshape(ZONES, SEGMENT)
    reach = jnp.min(
        jnp.where(ends > position[..., None], ends, runs * groups * chunk), axis=2
    )
    reach = jnp.maximum(reach - side * HEAD_DIM, 0)
    seen = (reach // SEGMENT) * HEAD_DIM + jnp.minimum(reach % SEGMENT, HEAD_DIM)
    seen = seen.astype(jnp.int32)
    counts = jnp.maximum((jnp.max(seen, axis=1) + WIDTH - 1) // WIDTH, 1)
    info = jnp.concatenate([jnp.stack([core, y]), counts, plain]).astype(jnp.int32)
    seen = seen.reshape(ZONES, 1, SEGMENT)

    parts = [None] * (2 * heads)

    def attended(info, head, sources):
        parts[2 * head], theirs = attend(info, rest, 4 + head, their_q[head], seen, sources, head)
        info, theirs = after(info, theirs)
        parts[2 * head + 1] = lax.ppermute(theirs, "head", partner)
        return info

    info, block_two, above, below = after(info, block_two, above, below)
    opposite = lax.ppermute(below, "head", up)
    above_two, below_two = sides(block_two)
    own_q[1], own_q[2], info = after(own_q[1], own_q[2], info)
    their_q[1] = lax.ppermute(own_q[1], "head", partner)
    info = attended(info, 0, (near, far))
    info, opposite, above_two, below_two, their_q[1] = after(
        info, opposite, above_two, below_two, their_q[1]
    )
    near, far = swapped(jnp.stack([block_one, above, below, opposite]))
    opposite = lax.ppermute(above_two, "head", down)
    near_two, far_two = swapped(jnp.stack([block_two, above_two, below_two]))
    their_q[2] = lax.ppermute(own_q[2], "head", partner)
    info = attended(info, 1, (near, far))
    info, opposite, their_q[2] = after(info, opposite, their_q[2])
    last, far_last = swapped(opposite[None])
    info = attended(info, 2, (near_two, last, far_two, far_last))
    mixed = exchange(merge(parts))
    gates = gate_rows(span_ids, timesteps, time_weight)
    return pl.pallas_call(
        gate_kernel, out_shape=jax.ShapeDtypeStruct((chunk, width), jnp.bfloat16), compiler_params=ROOMY
    )(gates, mixed)


def solution(mesh):
    return jax.shard_map(
        per_device,
        mesh=mesh,
        in_specs=(
            P(("span", "head"), None),
            P(("span", "head"), None),
            P(("span", "head"), None),
            P(("span", "head")),
            P(),
            P(),
        ),
        out_specs=P(("span", "head"), None),
        check_vma=False,
    )
```

```python
import functools
import math

import jax
import jax.numpy as jnp
from jax import lax
from jax.experimental import pallas as pl
from jax.experimental.pallas import tpu as pltpu
from jax.sharding import PartitionSpec as P

HEAD_DIM = 128
SCALE = HEAD_DIM**-0.5
SCALE_LOG2 = SCALE * math.log2(math.e)
BOTH = ("span", "head")
ZONES = 8
SEGMENT = 2 * HEAD_DIM
KEYS = 8192
WIDTH = 256
ITEMS = 8
FIRST_ZONES = 2
K_NORM, Q_NORM = 32, 40
NOTE = 16
PLAIN_LIMIT = 70.0
LOW = -1e30
ROOMY = pltpu.CompilerParams(vmem_limit_bytes=24 << 20)


def dot(a, b):
    return jnp.dot(a, b, preferred_element_type=jnp.float32)


def attend_kernel(head, info_ref, own_q, their_q, end_ref, *refs):
    sources, refs = refs[:-8], refs[-8:]
    own_out, their_out, kv_ref, qt_ref, weight_ref, acc_ref, top_ref, sems = refs
    core, rank = info_ref[0], info_ref[1]
    blocks = ZONES

    copies = []
    half = len(sources) // 2
    for j, zones in enumerate((pl.ds(0, FIRST_ZONES), pl.ds(FIRST_ZONES, ZONES - FIRST_ZONES))):
        for group, c in ((sources[:half], core), (sources[half:], 1 - core)):
            pieces = [src.at[k] for src in group for k in range(src.shape[0])]
            for piece, step in zip(pieces, (0, 1, 3, 2)):
                copies.append(
                    pltpu.make_async_copy(
                        piece.at[zones, pl.ds(0, 2 * HEAD_DIM)],
                        kv_ref.at[(rank + step) % 4, c, zones],
                        sems.at[len(copies)],
                    )
                )
    for copy in copies:
        copy.start()

    for zone in range(ZONES):
        qt_ref[zone] = jnp.concatenate([own_q[zone], their_q[zone]], axis=1)
    acc_ref[...] = jnp.zeros_like(acc_ref)
    top_ref[...] = jnp.zeros_like(top_ref)
    ones = jnp.ones((NOTE, WIDTH), jnp.bfloat16)
    for copy in copies[: len(copies) // 2]:
        copy.wait()

    def part(i, rows):
        return kv_ref[pl.ds((i % 2) * 2, 2), (i // 2) % 2, i // 4, rows]

    def keys_at(i):
        return part(i, slice(0, HEAD_DIM)).reshape(WIDTH, HEAD_DIM)

    def values_at(i):
        block = part(i, slice(HEAD_DIM, 2 * HEAD_DIM))
        return jnp.concatenate([jnp.concatenate([block[0], block[1]], axis=1), ones], axis=0)

    def visible_at(r, i):
        row = lax.broadcasted_iota(jnp.int32, (WIDTH, SEGMENT), 0)
        return row < end_ref[r] - i * WIDTH

    def score(item):
        r, i = item
        return dot(keys_at(i), qt_ref[jnp.minimum(r, blocks - 1)])

    def weigh(slot, item, scores):
        r, i = item
        weights = jnp.exp2(scores * SCALE_LOG2)
        weights = jnp.where(visible_at(jnp.minimum(r, blocks - 1), i), weights, 0.0)
        weight_ref[slot] = weights.astype(jnp.bfloat16)

    def absorb(slot, item):
        r, i = item
        acc_ref[r] += dot(values_at(i), weight_ref[slot])

    def careful(r, i):
        scores = dot(keys_at(i), qt_ref[r]) * SCALE_LOG2
        visible = visible_at(r, i)
        scores = jnp.where(visible, scores, LOW)
        old = top_ref[r, :1]
        new = jnp.maximum(old, jnp.max(scores, axis=0, keepdims=True))
        weights = jnp.where(visible, jnp.exp2(scores - new), 0.0).astype(jnp.bfloat16)
        acc_ref[r] = acc_ref[r] * jnp.exp2(old - new) + dot(values_at(i), weights)
        top_ref[r] = jnp.broadcast_to(new, top_ref.shape[1:])

    def count(r):
        return info_ref[2 + r]

    plain = info_ref[2 + blocks + head] == 1

    @pl.when(plain)
    def _():
        def following(item):
            r, i = item
            over = i + 1 >= count(jnp.minimum(r, blocks - 1))
            over = jnp.logical_or(over, r >= blocks)
            return jnp.where(over, jnp.minimum(r + 1, blocks), r), jnp.where(over, 0, i + 1)

        def run(item):
            items = [item]
            for _ in range(ITEMS - 1):
                items.append(following(items[-1]))
            return tuple(items)

        def step(_, items):
            later = run(following(items[-1]))
            scores = score(later[0])
            for slot in range(ITEMS):
                now = scores
                if slot + 1 < ITEMS:
                    scores = score(later[slot + 1])
                absorb(slot, items[slot])
                weigh(slot, later[slot], now)
            return later

        items = run((jnp.int32(0), jnp.int32(0)))
        for slot in range(ITEMS):
            weigh(slot, items[slot], score(items[slot]))
        for copy in copies[len(copies) // 2 :]:
            copy.wait()
        total = sum(count(r) for r in range(blocks))
        items = lax.fori_loop(0, (total + ITEMS - 1) // ITEMS - 1, step, items)
        for slot in range(ITEMS):
            absorb(slot, items[slot])

    @pl.when(jnp.logical_not(plain))
    def _():
        top_ref[...] = jnp.full_like(top_ref, LOW)
        for copy in copies[len(copies) // 2 :]:
            copy.wait()

        def over_block(r, carry):
            def over_chunk(i, carry):
                careful(r, i)
                return carry

            return lax.fori_loop(0, count(r), over_chunk, carry)

        lax.fori_loop(0, blocks, over_block, 0)

    for r in range(blocks):
        acc = acc_ref[r]
        total = acc[HEAD_DIM : HEAD_DIM + 1]
        some = total > 0.0
        safe = jnp.where(some, total, 1.0)
        mean = (acc[:HEAD_DIM] * jnp.where(some, 1.0 / safe, 0.0)).astype(jnp.bfloat16)
        level = jnp.where(some, top_ref[r, :1] + jnp.log2(safe), LOW)
        high = level.astype(jnp.bfloat16).astype(jnp.float32)
        middle = (level - high).astype(jnp.bfloat16).astype(jnp.float32)
        low = level - high - middle
        spare = jnp.zeros((NOTE - 3, SEGMENT), jnp.float32)
        note = jnp.concatenate([high, middle, low, spare]).astype(jnp.bfloat16)
        for out, at in ((own_out, slice(0, HEAD_DIM)), (their_out, slice(HEAD_DIM, SEGMENT))):
            out[r, :HEAD_DIM, :] = mean[:, at]
            out[r, HEAD_DIM:, :] = note[:, at]


def attend(info, own_q, at, their_q, ends, sources, head):
    rows = ZONES * SEGMENT
    out = jax.ShapeDtypeStruct((ZONES, HEAD_DIM + NOTE, HEAD_DIM), jnp.bfloat16)
    own_spec = pl.BlockSpec((ZONES, HEAD_DIM, HEAD_DIM), lambda i, *_: (0, at, 0))
    whole = pl.BlockSpec(memory_space=pltpu.VMEM)
    return pl.pallas_call(
        functools.partial(attend_kernel, head),
        grid_spec=pltpu.PrefetchScalarGridSpec(
            num_scalar_prefetch=1,
            grid=(1,),
            in_specs=[own_spec, whole, whole]
            + [pl.BlockSpec(memory_space=pltpu.HBM)] * len(sources),
            out_specs=[whole, whole],
            scratch_shapes=[
                pltpu.VMEM((4, 2, ZONES, 2 * HEAD_DIM, HEAD_DIM), jnp.bfloat16),
                pltpu.VMEM((ZONES, HEAD_DIM, SEGMENT), jnp.bfloat16),
                pltpu.VMEM((ITEMS, WIDTH, SEGMENT), jnp.bfloat16),
                pltpu.VMEM((ZONES + 1, HEAD_DIM + NOTE, SEGMENT), jnp.float32),
                pltpu.VMEM((ZONES, 8, SEGMENT), jnp.float32),
                pltpu.SemaphoreType.DMA((16,)),
            ],
        ),
        out_shape=[out, out],
        compiler_params=ROOMY,
        cost_estimate=pl.CostEstimate(
            flops=4 * rows * KEYS * HEAD_DIM,
            bytes_accessed=4 * KEYS * HEAD_DIM + 4 * rows * HEAD_DIM,
            transcendentals=rows * KEYS // 2,
        ),
    )(info, own_q, their_q, ends, *sources)


def pack_kernel(queries_ref, keys_ref, values_ref, ids_ref, first_ref, rest_ref):
    groups = first_ref.shape[0]
    heads = keys_ref.shape[1] // HEAD_DIM // groups
    ids = jnp.broadcast_to(ids_ref[...].astype(jnp.float32), (HEAD_DIM, HEAD_DIM)).T
    lane = lax.broadcasted_iota(jnp.int32, (HEAD_DIM, HEAD_DIM), 1)
    counts = jnp.sum(jnp.where(ids <= lane.astype(jnp.float32), 1.0, 0.0), axis=0, keepdims=True)
    local = heads * HEAD_DIM
    row = lax.broadcasted_iota(jnp.int32, (2 * local, HEAD_DIM), 0) // HEAD_DIM
    column = lax.broadcasted_iota(jnp.int32, (2 * local, HEAD_DIM), 1)
    wanted = jnp.where(row < heads, row + K_NORM, row - heads + Q_NORM)
    pick = jnp.where(column == wanted, 1.0, 0.0).astype(jnp.bfloat16)
    is_count = lane[:1] < K_NORM
    queries, keys, values = (queries_ref, True), (keys_ref, False), (values_ref, True)
    first = [(keys, 0), (values, 0)]
    rest = [(part, head) for head in range(1, heads) for part in (keys, values)]
    rest += [(queries, head) for head in range(heads)]
    for g in range(groups):
        for out_ref, parts in ((first_ref, first), (rest_ref, rest)):
            for j, ((ref, turn), head) in enumerate(parts):
                start = g * local + head * HEAD_DIM
                block = ref[:, start : start + HEAD_DIM]
                out_ref[g, j * HEAD_DIM : (j + 1) * HEAD_DIM] = block.T if turn else block
        rows = [ref[:, g * local : (g + 1) * local].astype(jnp.float32) for ref in (keys_ref, queries_ref)]
        squares = jnp.concatenate([(x * x).astype(jnp.bfloat16) for x in rows], axis=1)
        norms = jnp.max(dot(squares, pick), axis=0, keepdims=True) * 1.02
        note = jnp.where(is_count, counts, norms)
        note = jnp.broadcast_to(note, (NOTE, HEAD_DIM)).astype(jnp.bfloat16)
        first_ref[g, len(first) * HEAD_DIM :] = note


def packed(rows):
    return jax.ShapeDtypeStruct((ZONES, rows, HEAD_DIM), jnp.bfloat16)


def merge_kernel(*refs):
    out = refs[-1]

    def level(ref, zone):
        note = ref[zone, HEAD_DIM:, :].astype(jnp.float32)
        return note[0:1] + note[1:2] + note[2:3]

    for head in range(len(refs) // 2):
        one, two = refs[2 * head], refs[2 * head + 1]
        at = slice(head * HEAD_DIM, (head + 1) * HEAD_DIM)
        for zone in range(ZONES):
            share = 1.0 / (1.0 + jnp.exp2(level(two, zone) - level(one, zone)))
            a, b = (ref[zone, :HEAD_DIM, :].astype(jnp.float32) for ref in (one, two))
            out[zone, at, :] = (b + (a - b) * share).astype(jnp.bfloat16)


def merge(parts):
    return pl.pallas_call(merge_kernel, out_shape=packed(len(parts) // 2 * HEAD_DIM), compiler_params=ROOMY)(*parts)


def gate_kernel(gate_ref, mixed_ref, out_ref):
    groups, local, _ = mixed_ref.shape
    for g in range(groups):
        for h in range(0, local, HEAD_DIM):
            at = slice(g * local + h, g * local + h + HEAD_DIM)
            attended = mixed_ref[g, h : h + HEAD_DIM, :].T.astype(jnp.float32)
            out_ref[:, at] = (gate_ref[:, at] * attended).astype(jnp.bfloat16)


def gate_rows(span_ids, timesteps, time_weight):
    half = time_weight.shape[0] // 2
    freqs = jnp.exp(-math.log(10000.0) * jnp.arange(half, dtype=jnp.float32) / half)
    angles = timesteps.astype(jnp.float32)[:, None] * freqs[None, :]
    embed = jnp.concatenate([jnp.cos(angles), jnp.sin(angles)], axis=1).astype(jnp.bfloat16)
    gate_table = jnp.dot(embed, time_weight, preferred_element_type=jnp.float32)
    onehot = (span_ids[:, None] == jnp.arange(timesteps.shape[0], dtype=jnp.int32)[None, :]).astype(
        jnp.float32
    )
    return jnp.dot(onehot, gate_table, precision=lax.Precision.HIGHEST)


def per_device(queries, keys, values, span_ids, timesteps, time_weight):
    runs, groups = lax.axis_size("span"), lax.axis_size("head")
    run, rank = lax.axis_index("span"), lax.axis_index("head")
    spans = timesteps.shape[0]
    chunk, width = queries.shape
    local = width // groups
    heads = local // HEAD_DIM

    def device(zone, core, y, x):
        return (2 * zone + core) * groups + 2 * y + x

    across = [
        [device(zone, core, y, x) for zone in range(ZONES)]
        for core in range(2)
        for y in range(4)
        for x in range(2)
    ]
    up = [(h, (h + 2) % groups) for h in range(groups)]
    down = [(h, (h - 2) % groups) for h in range(groups)]
    core_swap = [(s, s ^ 1) for s in range(runs)]
    partner = [(h, h ^ 1) for h in range(groups)]

    def exchange(parts):
        return lax.all_to_all(
            parts, BOTH, split_axis=0, concat_axis=0, axis_index_groups=across, tiled=True
        )

    def after(*values):
        return lax.optimization_barrier(values)

    def swapped(block):
        return block, lax.ppermute(block, "span", core_swap)

    def sides(block):
        return lax.ppermute(block, "head", down), lax.ppermute(block, "head", up)

    pair = 2 * HEAD_DIM
    first, rest = pl.pallas_call(
        pack_kernel, out_shape=[packed(pair + NOTE), packed((3 * heads - 2) * HEAD_DIM)]
    )(queries, keys, values, span_ids.reshape(1, -1))
    first = exchange(first)
    rest, first = after(rest, first)
    rest = exchange(rest)
    above, below = sides(first)
    near = jnp.stack([first, above, below, lax.ppermute(above, "head", down)])

    def combined(notes):
        is_count = jnp.arange(HEAD_DIM) < K_NORM
        return jnp.where(is_count, jnp.sum(notes, axis=0), jnp.max(notes, axis=0))

    def noted(blocks):
        return combined(blocks[:, :, pair].reshape(-1, HEAD_DIM).astype(jnp.float32))

    note = noted(near)
    rest, near, note = after(rest, near, note)
    own_q = [rest[:, start : start + HEAD_DIM] for start in range(2 * pair, rest.shape[1], HEAD_DIM)]
    own_q[0], block_one, block_two = after(own_q[0], rest[:, :pair], rest[:, pair : 2 * pair])
    above, below = sides(block_one)
    their_q = [lax.ppermute(own_q[0], "head", partner), None, None]
    near, far = swapped(near)
    note = combined(jnp.stack([note, noted(far)]))[None]
    note, above, below, their_q[0] = after(note, above, below, their_q[0])
    note = combined(jnp.concatenate([note, lax.ppermute(note, "head", partner)]))
    squares = note[K_NORM : K_NORM + heads] * note[Q_NORM : Q_NORM + heads]
    plain = (squares * (1.05 * SCALE**2) < PLAIN_LIMIT**2).astype(jnp.int32)
    ends = note[:spans].astype(jnp.int32)

    core, y, side = run % 2, rank // 2, rank % 2
    offsets = jnp.stack([side, 1 - side])[None, :, None] * HEAD_DIM
    position = jnp.arange(ZONES)[:, None, None] * 2048 + offsets + jnp.arange(HEAD_DIM)[None, None, :]
    position = (position + (core * 1024 + y * SEGMENT)).reshape(ZONES, SEGMENT)
    reach = jnp.min(
        jnp.where(ends > position[..., None], ends, runs * groups * chunk), axis=2
    )
    reach = jnp.maximum(reach - side * HEAD_DIM, 0)
    seen = (reach // SEGMENT) * HEAD_DIM + jnp.minimum(reach % SEGMENT, HEAD_DIM)
    seen = seen.astype(jnp.int32)
    counts = jnp.maximum((jnp.max(seen, axis=1) + WIDTH - 1) // WIDTH, 1)
    info = jnp.concatenate([jnp.stack([core, y]), counts, plain]).astype(jnp.int32)
    seen = seen.reshape(ZONES, 1, SEGMENT)

    parts = [None] * (2 * heads)

    def attended(info, head, sources):
        parts[2 * head], theirs = attend(info, rest, 4 + head, their_q[head], seen, sources, head)
        info, theirs = after(info, theirs)
        parts[2 * head + 1] = lax.ppermute(theirs, "head", partner)
        return info

    info, block_two, above, below = after(info, block_two, above, below)
    opposite = lax.ppermute(below, "head", up)
    above_two, below_two = sides(block_two)
    own_q[1], own_q[2], info = after(own_q[1], own_q[2], info)
    their_q[1] = lax.ppermute(own_q[1], "head", partner)
    info = attended(info, 0, (near, far))
    info, opposite, above_two, below_two, their_q[1] = after(
        info, opposite, above_two, below_two, their_q[1]
    )
    near, far = swapped(jnp.stack([block_one, above, below, opposite]))
    opposite = lax.ppermute(above_two, "head", down)
    near_two, far_two = swapped(jnp.stack([block_two, above_two, below_two]))
    their_q[2] = lax.ppermute(own_q[2], "head", partner)
    info = attended(info, 1, (near, far))
    info, opposite, their_q[2] = after(info, opposite, their_q[2])
    last, far_last = swapped(opposite[None])
    info = attended(info, 2, (near_two, last, far_two, far_last))
    mixed = exchange(merge(parts))
    gates = gate_rows(span_ids, timesteps, time_weight)
    return pl.pallas_call(
        gate_kernel, out_shape=jax.ShapeDtypeStruct((chunk, width), jnp.bfloat16), compiler_params=ROOMY
    )(gates, mixed)


def solution(mesh):
    return jax.shard_map(
        per_device,
        mesh=mesh,
        in_specs=(
            P(("span", "head"), None),
            P(("span", "head"), None),
            P(("span", "head"), None),
            P(("span", "head")),
            P(),
            P(),
        ),
        out_specs=P(("span", "head"), None),
        check_vma=False,
    )
```

```python
import functools
import math

import jax
import jax.numpy as jnp
from jax import lax
from jax.experimental import pallas as pl
from jax.experimental.pallas import tpu as pltpu
from jax.sharding import PartitionSpec as P

HEAD_DIM = 128
SCALE = HEAD_DIM**-0.5
SCALE_LOG2 = SCALE * math.log2(math.e)
BOTH = ("span", "head")
ZONES = 8
SEGMENT = 2 * HEAD_DIM
KEYS = 8192
WIDTH = 256
ITEMS = 8
FIRST_ZONES = 2
K_NORM, Q_NORM = 32, 40
NOTE = 16
PLAIN_LIMIT = 70.0
LOW = -1e30
ROOMY = pltpu.CompilerParams(vmem_limit_bytes=24 << 20)


def dot(a, b):
    return jnp.dot(a, b, preferred_element_type=jnp.float32)


def attend_kernel(head, info_ref, own_q, their_q, end_ref, *refs):
    sources, refs = refs[:-8], refs[-8:]
    own_out, their_out, kv_ref, qt_ref, weight_ref, acc_ref, top_ref, sems = refs
    core, rank = info_ref[0], info_ref[1]
    blocks = ZONES

    copies = []
    half = len(sources) // 2
    for j, zones in enumerate((pl.ds(0, FIRST_ZONES), pl.ds(FIRST_ZONES, ZONES - FIRST_ZONES))):
        for group, c in ((sources[:half], core), (sources[half:], 1 - core)):
            pieces = [src.at[k] for src in group for k in range(src.shape[0])]
            for piece, step in zip(pieces, (0, 1, 3, 2)):
                copies.append(
                    pltpu.make_async_copy(
                        piece.at[zones, pl.ds(0, 2 * HEAD_DIM)],
                        kv_ref.at[(rank + step) % 4, c, zones],
                        sems.at[len(copies)],
                    )
                )
    for copy in copies:
        copy.start()

    for zone in range(ZONES):
        qt_ref[zone] = jnp.concatenate([own_q[zone], their_q[zone]], axis=1)
    acc_ref[...] = jnp.zeros_like(acc_ref)
    top_ref[...] = jnp.zeros_like(top_ref)
    ones = jnp.ones((NOTE, WIDTH), jnp.bfloat16)
    for copy in copies[: len(copies) // 2]:
        copy.wait()

    def part(i, rows):
        return kv_ref[pl.ds((i % 2) * 2, 2), (i // 2) % 2, i // 4, rows]

    def keys_at(i):
        return part(i, slice(0, HEAD_DIM)).reshape(WIDTH, HEAD_DIM)

    def values_at(i):
        block = part(i, slice(HEAD_DIM, 2 * HEAD_DIM))
        return jnp.concatenate([jnp.concatenate([block[0], block[1]], axis=1), ones], axis=0)

    def visible_at(r, i):
        row = lax.broadcasted_iota(jnp.int32, (WIDTH, SEGMENT), 0)
        return row < end_ref[r] - i * WIDTH

    def score(item):
        r, i = item
        return dot(keys_at(i), qt_ref[jnp.minimum(r, blocks - 1)])

    def weigh(slot, item, scores):
        r, i = item
        weights = jnp.exp2(scores * SCALE_LOG2)
        weights = jnp.where(visible_at(jnp.minimum(r, blocks - 1), i), weights, 0.0)
        weight_ref[slot] = weights.astype(jnp.bfloat16)

    def absorb(slot, item):
        r, i = item
        acc_ref[r] += dot(values_at(i), weight_ref[slot])

    def careful(r, i):
        scores = dot(keys_at(i), qt_ref[r]) * SCALE_LOG2
        visible = visible_at(r, i)
        scores = jnp.where(visible, scores, LOW)
        old = top_ref[r, :1]
        new = jnp.maximum(old, jnp.max(scores, axis=0, keepdims=True))
        weights = jnp.where(visible, jnp.exp2(scores - new), 0.0).astype(jnp.bfloat16)
        acc_ref[r] = acc_ref[r] * jnp.exp2(old - new) + dot(values_at(i), weights)
        top_ref[r] = jnp.broadcast_to(new, top_ref.shape[1:])

    def count(r):
        return info_ref[2 + r]

    plain = info_ref[2 + blocks + head] == 1

    @pl.when(plain)
    def _():
        def following(item):
            r, i = item
            over = i + 1 >= count(jnp.minimum(r, blocks - 1))
            over = jnp.logical_or(over, r >= blocks)
            return jnp.where(over, jnp.minimum(r + 1, blocks), r), jnp.where(over, 0, i + 1)

        def run(item):
            items = [item]
            for _ in range(ITEMS - 1):
                items.append(following(items[-1]))
            return tuple(items)

        def step(_, items):
            later = run(following(items[-1]))
            scores = score(later[0])
            for slot in range(ITEMS):
                now = scores
                if slot + 1 < ITEMS:
                    scores = score(later[slot + 1])
                absorb(slot, items[slot])
                weigh(slot, later[slot], now)
            return later

        items = run((jnp.int32(0), jnp.int32(0)))
        for slot in range(ITEMS):
            weigh(slot, items[slot], score(items[slot]))
        for copy in copies[len(copies) // 2 :]:
            copy.wait()
        total = sum(count(r) for r in range(blocks))
        items = lax.fori_loop(0, (total + ITEMS - 1) // ITEMS - 1, step, items)
        for slot in range(ITEMS):
            absorb(slot, items[slot])

    @pl.when(jnp.logical_not(plain))
    def _():
        top_ref[...] = jnp.full_like(top_ref, LOW)
        for copy in copies[len(copies) // 2 :]:
            copy.wait()

        def over_block(r, carry):
            def over_chunk(i, carry):
                careful(r, i)
                return carry

            return lax.fori_loop(0, count(r), over_chunk, carry)

        lax.fori_loop(0, blocks, over_block, 0)

    for r in range(blocks):
        acc = acc_ref[r]
        total = acc[HEAD_DIM : HEAD_DIM + 1]
        some = total > 0.0
        safe = jnp.where(some, total, 1.0)
        mean = (acc[:HEAD_DIM] * jnp.where(some, 1.0 / safe, 0.0)).astype(jnp.bfloat16)
        level = jnp.where(some, top_ref[r, :1] + jnp.log2(safe), LOW)
        high = level.astype(jnp.bfloat16).astype(jnp.float32)
        middle = (level - high).astype(jnp.bfloat16).astype(jnp.float32)
        low = level - high - middle
        spare = jnp.zeros((NOTE - 3, SEGMENT), jnp.float32)
        note = jnp.concatenate([high, middle, low, spare]).astype(jnp.bfloat16)
        for out, at in ((own_out, slice(0, HEAD_DIM)), (their_out, slice(HEAD_DIM, SEGMENT))):
            out[r, :HEAD_DIM, :] = mean[:, at]
            out[r, HEAD_DIM:, :] = note[:, at]


def attend(info, own_q, at, their_q, ends, sources, head):
    rows = ZONES * SEGMENT
    out = jax.ShapeDtypeStruct((ZONES, HEAD_DIM + NOTE, HEAD_DIM), jnp.bfloat16)
    own_spec = pl.BlockSpec((ZONES, HEAD_DIM, HEAD_DIM), lambda i, *_: (0, at, 0))
    whole = pl.BlockSpec(memory_space=pltpu.VMEM)
    return pl.pallas_call(
        functools.partial(attend_kernel, head),
        grid_spec=pltpu.PrefetchScalarGridSpec(
            num_scalar_prefetch=1,
            grid=(1,),
            in_specs=[own_spec, whole, whole]
            + [pl.BlockSpec(memory_space=pltpu.HBM)] * len(sources),
            out_specs=[whole, whole],
            scratch_shapes=[
                pltpu.VMEM((4, 2, ZONES, 2 * HEAD_DIM, HEAD_DIM), jnp.bfloat16),
                pltpu.VMEM((ZONES, HEAD_DIM, SEGMENT), jnp.bfloat16),
                pltpu.VMEM((ITEMS, WIDTH, SEGMENT), jnp.bfloat16),
                pltpu.VMEM((ZONES + 1, HEAD_DIM + NOTE, SEGMENT), jnp.float32),
                pltpu.VMEM((ZONES, 8, SEGMENT), jnp.float32),
                pltpu.SemaphoreType.DMA((16,)),
            ],
        ),
        out_shape=[out, out],
        compiler_params=ROOMY,
        cost_estimate=pl.CostEstimate(
            flops=4 * rows * KEYS * HEAD_DIM,
            bytes_accessed=4 * KEYS * HEAD_DIM + 4 * rows * HEAD_DIM,
            transcendentals=rows * KEYS // 2,
        ),
    )(info, own_q, their_q, ends, *sources)


def pack_kernel(queries_ref, keys_ref, values_ref, ids_ref, first_ref, rest_ref):
    groups = first_ref.shape[0]
    heads = keys_ref.shape[1] // HEAD_DIM // groups
    ids = jnp.broadcast_to(ids_ref[...].astype(jnp.float32), (HEAD_DIM, HEAD_DIM)).T
    lane = lax.broadcasted_iota(jnp.int32, (HEAD_DIM, HEAD_DIM), 1)
    counts = jnp.sum(jnp.where(ids <= lane.astype(jnp.float32), 1.0, 0.0), axis=0, keepdims=True)
    local = heads * HEAD_DIM
    row = lax.broadcasted_iota(jnp.int32, (2 * local, HEAD_DIM), 0) // HEAD_DIM
    column = lax.broadcasted_iota(jnp.int32, (2 * local, HEAD_DIM), 1)
    wanted = jnp.where(row < heads, row + K_NORM, row - heads + Q_NORM)
    pick = jnp.where(column == wanted, 1.0, 0.0).astype(jnp.bfloat16)
    is_count = lane[:1] < K_NORM
    queries, keys, values = (queries_ref, True), (keys_ref, False), (values_ref, True)
    first = [(keys, 0), (values, 0)]
    rest = [(part, head) for head in range(1, heads) for part in (keys, values)]
    rest += [(queries, head) for head in range(heads)]
    for g in range(groups):
        for out_ref, parts in ((first_ref, first), (rest_ref, rest)):
            for j, ((ref, turn), head) in enumerate(parts):
                start = g * local + head * HEAD_DIM
                block = ref[:, start : start + HEAD_DIM]
                out_ref[g, j * HEAD_DIM : (j + 1) * HEAD_DIM] = block.T if turn else block
        rows = [ref[:, g * local : (g + 1) * local].astype(jnp.float32) for ref in (keys_ref, queries_ref)]
        squares = jnp.concatenate([(x * x).astype(jnp.bfloat16) for x in rows], axis=1)
        norms = jnp.max(dot(squares, pick), axis=0, keepdims=True) * 1.02
        note = jnp.where(is_count, counts, norms)
        note = jnp.broadcast_to(note, (NOTE, HEAD_DIM)).astype(jnp.bfloat16)
        first_ref[g, len(first) * HEAD_DIM :] = note


def packed(rows):
    return jax.ShapeDtypeStruct((ZONES, rows, HEAD_DIM), jnp.bfloat16)


def merge_kernel(*refs):
    out = refs[-1]

    def level(ref, zone):
        note = ref[zone, HEAD_DIM:, :].astype(jnp.float32)
        return note[0:1] + note[1:2] + note[2:3]

    for head in range(len(refs) // 2):
        one, two = refs[2 * head], refs[2 * head + 1]
        at = slice(head * HEAD_DIM, (head + 1) * HEAD_DIM)
        for zone in range(ZONES):
            share = 1.0 / (1.0 + jnp.exp2(level(two, zone) - level(one, zone)))
            a, b = (ref[zone, :HEAD_DIM, :].astype(jnp.float32) for ref in (one, two))
            out[zone, at, :] = (b + (a - b) * share).astype(jnp.bfloat16)


def merge(parts):
    return pl.pallas_call(merge_kernel, out_shape=packed(len(parts) // 2 * HEAD_DIM), compiler_params=ROOMY)(*parts)


def gate_kernel(gate_ref, mixed_ref, out_ref):
    groups, local, _ = mixed_ref.shape
    for g in range(groups):
        for h in range(0, local, HEAD_DIM):
            at = slice(g * local + h, g * local + h + HEAD_DIM)
            attended = mixed_ref[g, h : h + HEAD_DIM, :].T.astype(jnp.float32)
            out_ref[:, at] = (gate_ref[:, at] * attended).astype(jnp.bfloat16)


def gate_rows(span_ids, timesteps, time_weight):
    half = time_weight.shape[0] // 2
    freqs = jnp.exp(-math.log(10000.0) * jnp.arange(half, dtype=jnp.float32) / half)
    angles = timesteps.astype(jnp.float32)[:, None] * freqs[None, :]
    embed = jnp.concatenate([jnp.cos(angles), jnp.sin(angles)], axis=1).astype(jnp.bfloat16)
    gate_table = jnp.dot(embed, time_weight, preferred_element_type=jnp.float32)
    onehot = (span_ids[:, None] == jnp.arange(timesteps.shape[0], dtype=jnp.int32)[None, :]).astype(
        jnp.float32
    )
    return jnp.dot(onehot, gate_table, precision=lax.Precision.HIGHEST)


def per_device(queries, keys, values, span_ids, timesteps, time_weight):
    runs, groups = lax.axis_size("span"), lax.axis_size("head")
    run, rank = lax.axis_index("span"), lax.axis_index("head")
    spans = timesteps.shape[0]
    chunk, width = queries.shape
    local = width // groups
    heads = local // HEAD_DIM

    def device(zone, core, y, x):
        return (2 * zone + core) * groups + 2 * y + x

    across = [
        [device(zone, core, y, x) for zone in range(ZONES)]
        for core in range(2)
        for y in range(4)
        for x in range(2)
    ]
    up = [(h, (h + 2) % groups) for h in range(groups)]
    down = [(h, (h - 2) % groups) for h in range(groups)]
    core_swap = [(s, s ^ 1) for s in range(runs)]
    partner = [(h, h ^ 1) for h in range(groups)]

    def exchange(parts):
        return lax.all_to_all(
            parts, BOTH, split_axis=0, concat_axis=0, axis_index_groups=across, tiled=True
        )

    def after(*values):
        return lax.optimization_barrier(values)

    def swapped(block):
        return block, lax.ppermute(block, "span", core_swap)

    def sides(block):
        return lax.ppermute(block, "head", down), lax.ppermute(block, "head", up)

    pair = 2 * HEAD_DIM
    first, rest = pl.pallas_call(
        pack_kernel, out_shape=[packed(pair + NOTE), packed((3 * heads - 2) * HEAD_DIM)]
    )(queries, keys, values, span_ids.reshape(1, -1))
    first = exchange(first)
    rest, first = after(rest, first)
    rest = exchange(rest)
    above, below = sides(first)
    half = ZONES // 2
    opposite = [lax.ppermute(below[:half], "head", up), lax.ppermute(above[half:], "head", down)]
    near = jnp.stack([first, above, below, jnp.concatenate(opposite)])

    def combined(notes):
        is_count = jnp.arange(HEAD_DIM) < K_NORM
        return jnp.where(is_count, jnp.sum(notes, axis=0), jnp.max(notes, axis=0))

    def noted(blocks):
        return combined(blocks[:, :, pair].reshape(-1, HEAD_DIM).astype(jnp.float32))

    note = noted(near)
    rest, near, note = after(rest, near, note)
    own_q = [rest[:, start : start + HEAD_DIM] for start in range(2 * pair, rest.shape[1], HEAD_DIM)]
    own_q[0], block_one, block_two = after(own_q[0], rest[:, :pair], rest[:, pair : 2 * pair])
    above, below = sides(block_one)
    their_q = [lax.ppermute(own_q[0], "head", partner), None, None]
    near, far = swapped(near)
    note = combined(jnp.stack([note, noted(far)]))[None]
    note, above, below, their_q[0] = after(note, above, below, their_q[0])
    note = combined(jnp.concatenate([note, lax.ppermute(note, "head", partner)]))
    squares = note[K_NORM : K_NORM + heads] * note[Q_NORM : Q_NORM + heads]
    plain = (squares * (1.05 * SCALE**2) < PLAIN_LIMIT**2).astype(jnp.int32)
    ends = note[:spans].astype(jnp.int32)

    core, y, side = run % 2, rank // 2, rank % 2
    offsets = jnp.stack([side, 1 - side])[None, :, None] * HEAD_DIM
    position = jnp.arange(ZONES)[:, None, None] * 2048 + offsets + jnp.arange(HEAD_DIM)[None, None, :]
    position = (position + (core * 1024 + y * SEGMENT)).reshape(ZONES, SEGMENT)
    reach = jnp.min(
        jnp.where(ends > position[..., None], ends, runs * groups * chunk), axis=2
    )
    reach = jnp.maximum(reach - side * HEAD_DIM, 0)
    seen = (reach // SEGMENT) * HEAD_DIM + jnp.minimum(reach % SEGMENT, HEAD_DIM)
    seen = seen.astype(jnp.int32)
    counts = jnp.maximum((jnp.max(seen, axis=1) + WIDTH - 1) // WIDTH, 1)
    info = jnp.concatenate([jnp.stack([core, y]), counts, plain]).astype(jnp.int32)
    seen = seen.reshape(ZONES, 1, SEGMENT)

    parts = [None] * (2 * heads)

    def attended(info, head, sources):
        parts[2 * head], theirs = attend(info, rest, 4 + head, their_q[head], seen, sources, head)
        info, theirs = after(info, theirs)
        parts[2 * head + 1] = lax.ppermute(theirs, "head", partner)
        return info

    info, block_two, above, below = after(info, block_two, above, below)
    opposite = lax.ppermute(below, "head", up)
    above_two, below_two = sides(block_two)
    own_q[1], own_q[2], info = after(own_q[1], own_q[2], info)
    their_q[1] = lax.ppermute(own_q[1], "head", partner)
    info = attended(info, 0, (near, far))
    info, opposite, above_two, below_two, their_q[1] = after(
        info, opposite, above_two, below_two, their_q[1]
    )
    near, far = swapped(jnp.stack([block_one, above, below, opposite]))
    opposite = lax.ppermute(above_two, "head", down)
    near_two, far_two = swapped(jnp.stack([block_two, above_two, below_two]))
    their_q[2] = lax.ppermute(own_q[2], "head", partner)
    info = attended(info, 1, (near, far))
    info, opposite, their_q[2] = after(info, opposite, their_q[2])
    last, far_last = swapped(opposite[None])
    info = attended(info, 2, (near_two, last, far_two, far_last))
    mixed = exchange(merge(parts))
    gates = gate_rows(span_ids, timesteps, time_weight)
    return pl.pallas_call(
        gate_kernel, out_shape=jax.ShapeDtypeStruct((chunk, width), jnp.bfloat16), compiler_params=ROOMY
    )(gates, mixed)


def solution(mesh):
    return jax.shard_map(
        per_device,
        mesh=mesh,
        in_specs=(
            P(("span", "head"), None),
            P(("span", "head"), None),
            P(("span", "head"), None),
            P(("span", "head")),
            P(),
            P(),
        ),
        out_specs=P(("span", "head"), None),
        check_vma=False,
    )
```

```python
import functools
import math

import jax
import jax.numpy as jnp
from jax import lax
from jax.experimental import pallas as pl
from jax.experimental.pallas import tpu as pltpu
from jax.sharding import PartitionSpec as P

HEAD_DIM = 128
SCALE = HEAD_DIM**-0.5
SCALE_LOG2 = SCALE * math.log2(math.e)
BOTH = ("span", "head")
ZONES = 8
SEGMENT = 2 * HEAD_DIM
KEYS = 8192
WIDTH = 256
ITEMS = 8
FIRST_ZONES = 2
K_NORM, Q_NORM = 32, 40
NOTE = 16
PLAIN_LIMIT = 70.0
LOW = -1e30
ROOMY = pltpu.CompilerParams(vmem_limit_bytes=24 << 20)


def dot(a, b):
    return jnp.dot(a, b, preferred_element_type=jnp.float32)


def attend_kernel(head, info_ref, own_q, their_q, end_ref, *refs):
    sources, refs = refs[:-8], refs[-8:]
    own_out, their_out, kv_ref, qt_ref, weight_ref, acc_ref, top_ref, sems = refs
    core, rank = info_ref[0], info_ref[1]
    blocks = ZONES

    copies = []
    half = len(sources) // 2
    for j, zones in enumerate((pl.ds(0, FIRST_ZONES), pl.ds(FIRST_ZONES, ZONES - FIRST_ZONES))):
        for group, c in ((sources[:half], core), (sources[half:], 1 - core)):
            pieces = [src.at[k] for src in group for k in range(src.shape[0])]
            for piece, step in zip(pieces, (0, 1, 3, 2)):
                copies.append(
                    pltpu.make_async_copy(
                        piece.at[zones, pl.ds(0, 2 * HEAD_DIM)],
                        kv_ref.at[(rank + step) % 4, c, zones],
                        sems.at[len(copies)],
                    )
                )
    for copy in copies:
        copy.start()

    for zone in range(ZONES):
        qt_ref[zone] = jnp.concatenate([own_q[zone], their_q[zone]], axis=1)
    acc_ref[...] = jnp.zeros_like(acc_ref)
    top_ref[...] = jnp.zeros_like(top_ref)
    ones = jnp.ones((NOTE, WIDTH), jnp.bfloat16)
    for copy in copies[: len(copies) // 2]:
        copy.wait()

    def part(i, rows):
        return kv_ref[pl.ds((i % 2) * 2, 2), (i // 2) % 2, i // 4, rows]

    def keys_at(i):
        return part(i, slice(0, HEAD_DIM)).reshape(WIDTH, HEAD_DIM)

    def values_at(i):
        block = part(i, slice(HEAD_DIM, 2 * HEAD_DIM))
        return jnp.concatenate([jnp.concatenate([block[0], block[1]], axis=1), ones], axis=0)

    def visible_at(r, i):
        row = lax.broadcasted_iota(jnp.int32, (WIDTH, SEGMENT), 0)
        return row < end_ref[r] - i * WIDTH

    def score(item):
        r, i = item
        return dot(keys_at(i), qt_ref[jnp.minimum(r, blocks - 1)])

    def weigh(slot, item, scores):
        r, i = item
        weights = jnp.exp2(scores * SCALE_LOG2)
        weights = jnp.where(visible_at(jnp.minimum(r, blocks - 1), i), weights, 0.0)
        weight_ref[slot] = weights.astype(jnp.bfloat16)

    def absorb(slot, item):
        r, i = item
        acc_ref[r] += dot(values_at(i), weight_ref[slot])

    def careful(r, i):
        scores = dot(keys_at(i), qt_ref[r]) * SCALE_LOG2
        visible = visible_at(r, i)
        scores = jnp.where(visible, scores, LOW)
        old = top_ref[r, :1]
        new = jnp.maximum(old, jnp.max(scores, axis=0, keepdims=True))
        weights = jnp.where(visible, jnp.exp2(scores - new), 0.0).astype(jnp.bfloat16)
        acc_ref[r] = acc_ref[r] * jnp.exp2(old - new) + dot(values_at(i), weights)
        top_ref[r] = jnp.broadcast_to(new, top_ref.shape[1:])

    def count(r):
        return info_ref[2 + r]

    plain = info_ref[2 + blocks + head] == 1

    @pl.when(plain)
    def _():
        def following(item):
            r, i = item
            over = i + 1 >= count(jnp.minimum(r, blocks - 1))
            over = jnp.logical_or(over, r >= blocks)
            return jnp.where(over, jnp.minimum(r + 1, blocks), r), jnp.where(over, 0, i + 1)

        def run(item):
            items = [item]
            for _ in range(ITEMS - 1):
                items.append(following(items[-1]))
            return tuple(items)

        def step(_, items):
            later = run(following(items[-1]))
            scores = score(later[0])
            for slot in range(ITEMS):
                now = scores
                if slot + 1 < ITEMS:
                    scores = score(later[slot + 1])
                absorb(slot, items[slot])
                weigh(slot, later[slot], now)
            return later

        items = run((jnp.int32(0), jnp.int32(0)))
        for slot in range(ITEMS):
            weigh(slot, items[slot], score(items[slot]))
        for copy in copies[len(copies) // 2 :]:
            copy.wait()
        total = sum(count(r) for r in range(blocks))
        items = lax.fori_loop(0, (total + ITEMS - 1) // ITEMS - 1, step, items)
        for slot in range(ITEMS):
            absorb(slot, items[slot])

    @pl.when(jnp.logical_not(plain))
    def _():
        top_ref[...] = jnp.full_like(top_ref, LOW)
        for copy in copies[len(copies) // 2 :]:
            copy.wait()

        def over_block(r, carry):
            def over_chunk(i, carry):
                careful(r, i)
                return carry

            return lax.fori_loop(0, count(r), over_chunk, carry)

        lax.fori_loop(0, blocks, over_block, 0)

    for r in range(blocks):
        acc = acc_ref[r]
        total = acc[HEAD_DIM : HEAD_DIM + 1]
        some = total > 0.0
        safe = jnp.where(some, total, 1.0)
        mean = (acc[:HEAD_DIM] * jnp.where(some, 1.0 / safe, 0.0)).astype(jnp.bfloat16)
        level = jnp.where(some, top_ref[r, :1] + jnp.log2(safe), LOW)
        high = level.astype(jnp.bfloat16).astype(jnp.float32)
        middle = (level - high).astype(jnp.bfloat16).astype(jnp.float32)
        low = level - high - middle
        spare = jnp.zeros((NOTE - 3, SEGMENT), jnp.float32)
        note = jnp.concatenate([high, middle, low, spare]).astype(jnp.bfloat16)
        for out, at in ((own_out, slice(0, HEAD_DIM)), (their_out, slice(HEAD_DIM, SEGMENT))):
            out[r, :HEAD_DIM, :] = mean[:, at]
            out[r, HEAD_DIM:, :] = note[:, at]


def attend(info, own_q, at, their_q, ends, sources, head):
    rows = ZONES * SEGMENT
    out = jax.ShapeDtypeStruct((ZONES, HEAD_DIM + NOTE, HEAD_DIM), jnp.bfloat16)
    own_spec = pl.BlockSpec((ZONES, HEAD_DIM, HEAD_DIM), lambda i, *_: (0, at, 0))
    whole = pl.BlockSpec(memory_space=pltpu.VMEM)
    return pl.pallas_call(
        functools.partial(attend_kernel, head),
        grid_spec=pltpu.PrefetchScalarGridSpec(
            num_scalar_prefetch=1,
            grid=(1,),
            in_specs=[own_spec, whole, whole]
            + [pl.BlockSpec(memory_space=pltpu.HBM)] * len(sources),
            out_specs=[whole, whole],
            scratch_shapes=[
                pltpu.VMEM((4, 2, ZONES, 2 * HEAD_DIM, HEAD_DIM), jnp.bfloat16),
                pltpu.VMEM((ZONES, HEAD_DIM, SEGMENT), jnp.bfloat16),
                pltpu.VMEM((ITEMS, WIDTH, SEGMENT), jnp.bfloat16),
                pltpu.VMEM((ZONES + 1, HEAD_DIM + NOTE, SEGMENT), jnp.float32),
                pltpu.VMEM((ZONES, 8, SEGMENT), jnp.float32),
                pltpu.SemaphoreType.DMA((16,)),
            ],
        ),
        out_shape=[out, out],
        compiler_params=ROOMY,
        cost_estimate=pl.CostEstimate(
            flops=4 * rows * KEYS * HEAD_DIM,
            bytes_accessed=4 * KEYS * HEAD_DIM + 4 * rows * HEAD_DIM,
            transcendentals=rows * KEYS // 2,
        ),
    )(info, own_q, their_q, ends, *sources)


def pack_kernel(queries_ref, keys_ref, values_ref, ids_ref, first_ref, rest_ref):
    groups = first_ref.shape[0]
    heads = keys_ref.shape[1] // HEAD_DIM // groups
    ids = jnp.broadcast_to(ids_ref[...].astype(jnp.float32), (HEAD_DIM, HEAD_DIM)).T
    lane = lax.broadcasted_iota(jnp.int32, (HEAD_DIM, HEAD_DIM), 1)
    counts = jnp.sum(jnp.where(ids <= lane.astype(jnp.float32), 1.0, 0.0), axis=0, keepdims=True)
    local = heads * HEAD_DIM
    row = lax.broadcasted_iota(jnp.int32, (2 * local, HEAD_DIM), 0) // HEAD_DIM
    column = lax.broadcasted_iota(jnp.int32, (2 * local, HEAD_DIM), 1)
    wanted = jnp.where(row < heads, row + K_NORM, row - heads + Q_NORM)
    pick = jnp.where(column == wanted, 1.0, 0.0).astype(jnp.bfloat16)
    is_count = lane[:1] < K_NORM
    queries, keys, values = (queries_ref, True), (keys_ref, False), (values_ref, True)
    first = [(keys, 0), (values, 0)]
    rest = [(part, head) for head in range(1, heads) for part in (keys, values)]
    rest += [(queries, head) for head in range(heads)]
    for g in range(groups):
        for out_ref, parts in ((first_ref, first), (rest_ref, rest)):
            for j, ((ref, turn), head) in enumerate(parts):
                start = g * local + head * HEAD_DIM
                block = ref[:, start : start + HEAD_DIM]
                out_ref[g, j * HEAD_DIM : (j + 1) * HEAD_DIM] = block.T if turn else block
        rows = [ref[:, g * local : (g + 1) * local].astype(jnp.float32) for ref in (keys_ref, queries_ref)]
        squares = jnp.concatenate([(x * x).astype(jnp.bfloat16) for x in rows], axis=1)
        norms = jnp.max(dot(squares, pick), axis=0, keepdims=True) * 1.02
        note = jnp.where(is_count, counts, norms)
        note = jnp.broadcast_to(note, (NOTE, HEAD_DIM)).astype(jnp.bfloat16)
        first_ref[g, len(first) * HEAD_DIM :] = note


def packed(rows):
    return jax.ShapeDtypeStruct((ZONES, rows, HEAD_DIM), jnp.bfloat16)


def merge_kernel(*refs):
    out = refs[-1]

    def level(ref, zone):
        note = ref[zone, HEAD_DIM:, :].astype(jnp.float32)
        return note[0:1] + note[1:2] + note[2:3]

    for head in range(len(refs) // 2):
        one, two = refs[2 * head], refs[2 * head + 1]
        at = slice(head * HEAD_DIM, (head + 1) * HEAD_DIM)
        for zone in range(ZONES):
            share = 1.0 / (1.0 + jnp.exp2(level(two, zone) - level(one, zone)))
            a, b = (ref[zone, :HEAD_DIM, :].astype(jnp.float32) for ref in (one, two))
            out[zone, at, :] = (b + (a - b) * share).astype(jnp.bfloat16)


def merge(parts):
    return pl.pallas_call(merge_kernel, out_shape=packed(len(parts) // 2 * HEAD_DIM), compiler_params=ROOMY)(*parts)


def gate_kernel(gate_ref, mixed_ref, out_ref):
    groups, local, _ = mixed_ref.shape
    for g in range(groups):
        for h in range(0, local, HEAD_DIM):
            at = slice(g * local + h, g * local + h + HEAD_DIM)
            attended = mixed_ref[g, h : h + HEAD_DIM, :].T.astype(jnp.float32)
            out_ref[:, at] = (gate_ref[:, at] * attended).astype(jnp.bfloat16)


def gate_rows(span_ids, timesteps, time_weight):
    half = time_weight.shape[0] // 2
    freqs = jnp.exp(-math.log(10000.0) * jnp.arange(half, dtype=jnp.float32) / half)
    angles = timesteps.astype(jnp.float32)[:, None] * freqs[None, :]
    embed = jnp.concatenate([jnp.cos(angles), jnp.sin(angles)], axis=1).astype(jnp.bfloat16)
    gate_table = jnp.dot(embed, time_weight, preferred_element_type=jnp.float32)
    onehot = (span_ids[:, None] == jnp.arange(timesteps.shape[0], dtype=jnp.int32)[None, :]).astype(
        jnp.float32
    )
    return jnp.dot(onehot, gate_table, precision=lax.Precision.HIGHEST)


def per_device(queries, keys, values, span_ids, timesteps, time_weight):
    runs, groups = lax.axis_size("span"), lax.axis_size("head")
    run, rank = lax.axis_index("span"), lax.axis_index("head")
    spans = timesteps.shape[0]
    chunk, width = queries.shape
    local = width // groups
    heads = local // HEAD_DIM

    def device(zone, core, y, x):
        return (2 * zone + core) * groups + 2 * y + x

    across = [
        [device(zone, core, y, x) for zone in range(ZONES)]
        for core in range(2)
        for y in range(4)
        for x in range(2)
    ]
    up = [(h, (h + 2) % groups) for h in range(groups)]
    down = [(h, (h - 2) % groups) for h in range(groups)]
    core_swap = [(s, s ^ 1) for s in range(runs)]
    partner = [(h, h ^ 1) for h in range(groups)]

    def exchange(parts):
        return lax.all_to_all(
            parts, BOTH, split_axis=0, concat_axis=0, axis_index_groups=across, tiled=True
        )

    def after(*values):
        return lax.optimization_barrier(values)

    def when(value, *ended):
        return value + sum(x[0, 0, 0].astype(value.dtype) for x in ended) * 0.0

    def swapped(block):
        return block, lax.ppermute(block, "span", core_swap)

    def sides(block):
        return lax.ppermute(block, "head", down), lax.ppermute(block, "head", up)

    pair = 2 * HEAD_DIM
    first, rest = pl.pallas_call(
        pack_kernel, out_shape=[packed(pair + NOTE), packed((3 * heads - 2) * HEAD_DIM)]
    )(queries, keys, values, span_ids.reshape(1, -1))
    first = exchange(first)
    rest, first = after(rest, first)
    rest = exchange(rest)
    above, below = sides(first)
    half = ZONES // 2
    opposite = [lax.ppermute(below[:half], "head", up), lax.ppermute(above[half:], "head", down)]
    near = jnp.stack([first, above, below, jnp.concatenate(opposite)])

    def combined(notes):
        is_count = jnp.arange(HEAD_DIM) < K_NORM
        return jnp.where(is_count, jnp.sum(notes, axis=0), jnp.max(notes, axis=0))

    def noted(blocks):
        return combined(blocks[:, :, pair].reshape(-1, HEAD_DIM).astype(jnp.float32))

    note = noted(near)
    rest, note = after(rest, note)
    own_q = [rest[:, start : start + HEAD_DIM] for start in range(2 * pair, rest.shape[1], HEAD_DIM)]
    own_q[0], block_one, block_two = after(own_q[0], rest[:, :pair], rest[:, pair : 2 * pair])
    above, below = sides(block_one)
    their_q = [lax.ppermute(own_q[0], "head", partner), None, None]
    near, far = swapped(near)
    note = combined(jnp.stack([note, noted(far)]))[None]
    note = when(note, above, below, their_q[0])
    note = combined(jnp.concatenate([note, lax.ppermute(note, "head", partner)]))
    squares = note[K_NORM : K_NORM + heads] * note[Q_NORM : Q_NORM + heads]
    plain = (squares * (1.05 * SCALE**2) < PLAIN_LIMIT**2).astype(jnp.int32)
    ends = note[:spans].astype(jnp.int32)

    core, y, side = run % 2, rank // 2, rank % 2
    offsets = jnp.stack([side, 1 - side])[None, :, None] * HEAD_DIM
    position = jnp.arange(ZONES)[:, None, None] * 2048 + offsets + jnp.arange(HEAD_DIM)[None, None, :]
    position = (position + (core * 1024 + y * SEGMENT)).reshape(ZONES, SEGMENT)
    reach = jnp.min(
        jnp.where(ends > position[..., None], ends, runs * groups * chunk), axis=2
    )
    reach = jnp.maximum(reach - side * HEAD_DIM, 0)
    seen = (reach // SEGMENT) * HEAD_DIM + jnp.minimum(reach % SEGMENT, HEAD_DIM)
    seen = seen.astype(jnp.int32)
    counts = jnp.maximum((jnp.max(seen, axis=1) + WIDTH - 1) // WIDTH, 1)
    info = jnp.concatenate([jnp.stack([core, y]), counts, plain]).astype(jnp.int32)
    seen = seen.reshape(ZONES, 1, SEGMENT)

    parts = [None] * (2 * heads)

    def attended(info, head, sources):
        parts[2 * head], theirs = attend(info, rest, 4 + head, their_q[head], seen, sources, head)
        info, theirs = after(info, theirs)
        parts[2 * head + 1] = lax.ppermute(theirs, "head", partner)
        return info

    info, block_two, above, below = after(info, block_two, above, below)
    opposite = lax.ppermute(below, "head", up)
    above_two, below_two = sides(block_two)
    own_q[1], own_q[2], info = after(own_q[1], own_q[2], info)
    their_q[1] = lax.ppermute(own_q[1], "head", partner)
    info = attended(info, 0, (near, far))
    info, opposite, above_two, below_two, their_q[1] = after(
        info, opposite, above_two, below_two, their_q[1]
    )
    near, far = swapped(jnp.stack([block_one, above, below, opposite]))
    opposite = lax.ppermute(above_two, "head", down)
    near_two, far_two = swapped(jnp.stack([block_two, above_two, below_two]))
    their_q[2] = lax.ppermute(own_q[2], "head", partner)
    info = attended(info, 1, (near, far))
    info, opposite, their_q[2] = after(info, opposite, their_q[2])
    last, far_last = swapped(opposite[None])
    info = attended(info, 2, (near_two, last, far_two, far_last))
    mixed = exchange(merge(parts))
    gates = gate_rows(span_ids, timesteps, time_weight)
    return pl.pallas_call(
        gate_kernel, out_shape=jax.ShapeDtypeStruct((chunk, width), jnp.bfloat16), compiler_params=ROOMY
    )(gates, mixed)


def solution(mesh):
    return jax.shard_map(
        per_device,
        mesh=mesh,
        in_specs=(
            P(("span", "head"), None),
            P(("span", "head"), None),
            P(("span", "head"), None),
            P(("span", "head")),
            P(),
            P(),
        ),
        out_specs=P(("span", "head"), None),
        check_vma=False,
    )
```

```python
import functools
import math

import jax
import jax.numpy as jnp
from jax import lax
from jax.experimental import pallas as pl
from jax.experimental.pallas import tpu as pltpu
from jax.sharding import PartitionSpec as P

HEAD_DIM = 128
SCALE = HEAD_DIM**-0.5
SCALE_LOG2 = SCALE * math.log2(math.e)
BOTH = ("span", "head")
ZONES = 8
SEGMENT = 2 * HEAD_DIM
KEYS = 8192
WIDTH = 256
ITEMS = 8
K_NORM, Q_NORM = 32, 40
NOTE = 16
PLAIN_LIMIT = 70.0
LOW = -1e30
ROOMY = pltpu.CompilerParams(vmem_limit_bytes=24 << 20)


def dot(a, b):
    return jnp.dot(a, b, preferred_element_type=jnp.float32)


def attend_kernel(head, info_ref, own_q, their_q, end_ref, *refs):
    sources, refs = refs[:-8], refs[-8:]
    own_out, their_out, kv_ref, qt_ref, weight_ref, acc_ref, top_ref, sems = refs
    core, rank = info_ref[0], info_ref[1]
    blocks = ZONES

    copies = []
    half = len(sources) // 2
    for zones in (pl.ds(0, 2), pl.ds(2, 3), pl.ds(5, 3)):
        for group, c in ((sources[:half], core), (sources[half:], 1 - core)):
            pieces = [src.at[k] for src in group for k in range(src.shape[0])]
            for piece, step in zip(pieces, (0, 1, 3, 2)):
                copies.append(
                    pltpu.make_async_copy(
                        piece.at[zones, pl.ds(0, 2 * HEAD_DIM)],
                        kv_ref.at[(rank + step) % 4, c, zones],
                        sems.at[len(copies)],
                    )
                )
    for copy in copies:
        copy.start()

    for zone in range(ZONES):
        qt_ref[zone] = jnp.concatenate([own_q[zone], their_q[zone]], axis=1)
    acc_ref[...] = jnp.zeros_like(acc_ref)
    top_ref[...] = jnp.zeros_like(top_ref)
    ones = jnp.ones((NOTE, WIDTH), jnp.bfloat16)
    for copy in copies[:8]:
        copy.wait()

    def part(i, rows):
        return kv_ref[pl.ds((i % 2) * 2, 2), (i // 2) % 2, i // 4, rows]

    def keys_at(i):
        return part(i, slice(0, HEAD_DIM)).reshape(WIDTH, HEAD_DIM)

    def values_at(i):
        block = part(i, slice(HEAD_DIM, 2 * HEAD_DIM))
        return jnp.concatenate([jnp.concatenate([block[0], block[1]], axis=1), ones], axis=0)

    def visible_at(r, i):
        row = lax.broadcasted_iota(jnp.int32, (WIDTH, SEGMENT), 0)
        return row < end_ref[r] - i * WIDTH

    def score(item):
        r, i = item
        return dot(keys_at(i), qt_ref[jnp.minimum(r, blocks - 1)])

    def weigh(slot, item, scores):
        r, i = item
        weights = jnp.exp2(scores * SCALE_LOG2)
        weights = jnp.where(visible_at(jnp.minimum(r, blocks - 1), i), weights, 0.0)
        weight_ref[slot] = weights.astype(jnp.bfloat16)

    def absorb(slot, item):
        r, i = item
        acc_ref[r] += dot(values_at(i), weight_ref[slot])

    def careful(r, i):
        scores = dot(keys_at(i), qt_ref[r]) * SCALE_LOG2
        visible = visible_at(r, i)
        scores = jnp.where(visible, scores, LOW)
        old = top_ref[r, :1]
        new = jnp.maximum(old, jnp.max(scores, axis=0, keepdims=True))
        weights = jnp.where(visible, jnp.exp2(scores - new), 0.0).astype(jnp.bfloat16)
        acc_ref[r] = acc_ref[r] * jnp.exp2(old - new) + dot(values_at(i), weights)
        top_ref[r] = jnp.broadcast_to(new, top_ref.shape[1:])

    def count(r):
        return info_ref[2 + r]

    plain = info_ref[2 + blocks + head] == 1

    @pl.when(plain)
    def _():
        def following(item):
            r, i = item
            over = i + 1 >= count(jnp.minimum(r, blocks - 1))
            over = jnp.logical_or(over, r >= blocks)
            return jnp.where(over, jnp.minimum(r + 1, blocks), r), jnp.where(over, 0, i + 1)

        def run(item):
            items = [item]
            for _ in range(ITEMS - 1):
                items.append(following(items[-1]))
            return tuple(items)

        def step(number, items):
            @pl.when(number == lasting)
            def _():
                for copy in copies[16:]:
                    copy.wait()

            later = run(following(items[-1]))
            scores = score(later[0])
            for slot in range(ITEMS):
                now = scores
                if slot + 1 < ITEMS:
                    scores = score(later[slot + 1])
                absorb(slot, items[slot])
                weigh(slot, later[slot], now)
            return later

        items = run((jnp.int32(0), jnp.int32(0)))
        for slot in range(ITEMS):
            weigh(slot, items[slot], score(items[slot]))
        for copy in copies[8:16]:
            copy.wait()
        total = sum(count(r) for r in range(blocks))
        lasting = jnp.maximum(sum(count(r) for r in range(4)) // ITEMS - 1, 0)
        items = lax.fori_loop(0, (total + ITEMS - 1) // ITEMS - 1, step, items)
        for slot in range(ITEMS):
            absorb(slot, items[slot])

    @pl.when(jnp.logical_not(plain))
    def _():
        top_ref[...] = jnp.full_like(top_ref, LOW)
        for copy in copies[8:]:
            copy.wait()

        def over_block(r, carry):
            def over_chunk(i, carry):
                careful(r, i)
                return carry

            return lax.fori_loop(0, count(r), over_chunk, carry)

        lax.fori_loop(0, blocks, over_block, 0)

    for r in range(blocks):
        acc = acc_ref[r]
        total = acc[HEAD_DIM : HEAD_DIM + 1]
        some = total > 0.0
        safe = jnp.where(some, total, 1.0)
        mean = (acc[:HEAD_DIM] * jnp.where(some, 1.0 / safe, 0.0)).astype(jnp.bfloat16)
        level = jnp.where(some, top_ref[r, :1] + jnp.log2(safe), LOW)
        high = level.astype(jnp.bfloat16).astype(jnp.float32)
        middle = (level - high).astype(jnp.bfloat16).astype(jnp.float32)
        low = level - high - middle
        spare = jnp.zeros((NOTE - 3, SEGMENT), jnp.float32)
        note = jnp.concatenate([high, middle, low, spare]).astype(jnp.bfloat16)
        for out, at in ((own_out, slice(0, HEAD_DIM)), (their_out, slice(HEAD_DIM, SEGMENT))):
            out[r, :HEAD_DIM, :] = mean[:, at]
            out[r, HEAD_DIM:, :] = note[:, at]


def attend(info, own_q, at, their_q, ends, sources, head):
    rows = ZONES * SEGMENT
    out = jax.ShapeDtypeStruct((ZONES, HEAD_DIM + NOTE, HEAD_DIM), jnp.bfloat16)
    own_spec = pl.BlockSpec((ZONES, HEAD_DIM, HEAD_DIM), lambda i, *_: (0, at, 0))
    whole = pl.BlockSpec(memory_space=pltpu.VMEM)
    return pl.pallas_call(
        functools.partial(attend_kernel, head),
        grid_spec=pltpu.PrefetchScalarGridSpec(
            num_scalar_prefetch=1,
            grid=(1,),
            in_specs=[own_spec, whole, whole]
            + [pl.BlockSpec(memory_space=pltpu.HBM)] * len(sources),
            out_specs=[whole, whole],
            scratch_shapes=[
                pltpu.VMEM((4, 2, ZONES, 2 * HEAD_DIM, HEAD_DIM), jnp.bfloat16),
                pltpu.VMEM((ZONES, HEAD_DIM, SEGMENT), jnp.bfloat16),
                pltpu.VMEM((ITEMS, WIDTH, SEGMENT), jnp.bfloat16),
                pltpu.VMEM((ZONES + 1, HEAD_DIM + NOTE, SEGMENT), jnp.float32),
                pltpu.VMEM((ZONES, 8, SEGMENT), jnp.float32),
                pltpu.SemaphoreType.DMA((24,)),
            ],
        ),
        out_shape=[out, out],
        compiler_params=ROOMY,
        cost_estimate=pl.CostEstimate(
            flops=4 * rows * KEYS * HEAD_DIM,
            bytes_accessed=4 * KEYS * HEAD_DIM + 4 * rows * HEAD_DIM,
            transcendentals=rows * KEYS // 2,
        ),
    )(info, own_q, their_q, ends, *sources)


def pack_kernel(queries_ref, keys_ref, values_ref, ids_ref, first_ref, rest_ref):
    groups = first_ref.shape[0]
    heads = keys_ref.shape[1] // HEAD_DIM // groups
    ids = jnp.broadcast_to(ids_ref[...].astype(jnp.float32), (HEAD_DIM, HEAD_DIM)).T
    lane = lax.broadcasted_iota(jnp.int32, (HEAD_DIM, HEAD_DIM), 1)
    counts = jnp.sum(jnp.where(ids <= lane.astype(jnp.float32), 1.0, 0.0), axis=0, keepdims=True)
    local = heads * HEAD_DIM
    row = lax.broadcasted_iota(jnp.int32, (2 * local, HEAD_DIM), 0) // HEAD_DIM
    column = lax.broadcasted_iota(jnp.int32, (2 * local, HEAD_DIM), 1)
    wanted = jnp.where(row < heads, row + K_NORM, row - heads + Q_NORM)
    pick = jnp.where(column == wanted, 1.0, 0.0).astype(jnp.bfloat16)
    is_count = lane[:1] < K_NORM
    queries, keys, values = (queries_ref, True), (keys_ref, False), (values_ref, True)
    first = [(keys, 0), (values, 0)]
    rest = [(part, head) for head in range(1, heads) for part in (keys, values)]
    rest += [(queries, head) for head in range(heads)]
    for g in range(groups):
        for out_ref, parts in ((first_ref, first), (rest_ref, rest)):
            for j, ((ref, turn), head) in enumerate(parts):
                start = g * local + head * HEAD_DIM
                block = ref[:, start : start + HEAD_DIM]
                out_ref[g, j * HEAD_DIM : (j + 1) * HEAD_DIM] = block.T if turn else block
        rows = [ref[:, g * local : (g + 1) * local].astype(jnp.float32) for ref in (keys_ref, queries_ref)]
        squares = jnp.concatenate([(x * x).astype(jnp.bfloat16) for x in rows], axis=1)
        norms = jnp.max(dot(squares, pick), axis=0, keepdims=True) * 1.02
        note = jnp.where(is_count, counts, norms)
        note = jnp.broadcast_to(note, (NOTE, HEAD_DIM)).astype(jnp.bfloat16)
        first_ref[g, len(first) * HEAD_DIM :] = note


def packed(rows):
    return jax.ShapeDtypeStruct((ZONES, rows, HEAD_DIM), jnp.bfloat16)


def merge_kernel(*refs):
    out = refs[-1]

    def level(ref, zone):
        note = ref[zone, HEAD_DIM:, :].astype(jnp.float32)
        return note[0:1] + note[1:2] + note[2:3]

    for head in range(len(refs) // 2):
        one, two = refs[2 * head], refs[2 * head + 1]
        at = slice(head * HEAD_DIM, (head + 1) * HEAD_DIM)
        for zone in range(ZONES):
            share = 1.0 / (1.0 + jnp.exp2(level(two, zone) - level(one, zone)))
            a, b = (ref[zone, :HEAD_DIM, :].astype(jnp.float32) for ref in (one, two))
            out[zone, at, :] = (b + (a - b) * share).astype(jnp.bfloat16)


def merge(parts):
    return pl.pallas_call(merge_kernel, out_shape=packed(len(parts) // 2 * HEAD_DIM), compiler_params=ROOMY)(*parts)


def gate_kernel(gate_ref, mixed_ref, out_ref):
    groups, local, _ = mixed_ref.shape
    for g in range(groups):
        for h in range(0, local, HEAD_DIM):
            at = slice(g * local + h, g * local + h + HEAD_DIM)
            attended = mixed_ref[g, h : h + HEAD_DIM, :].T.astype(jnp.float32)
            out_ref[:, at] = (gate_ref[:, at] * attended).astype(jnp.bfloat16)


def gate_rows(span_ids, timesteps, time_weight):
    half = time_weight.shape[0] // 2
    freqs = jnp.exp(-math.log(10000.0) * jnp.arange(half, dtype=jnp.float32) / half)
    angles = timesteps.astype(jnp.float32)[:, None] * freqs[None, :]
    embed = jnp.concatenate([jnp.cos(angles), jnp.sin(angles)], axis=1).astype(jnp.bfloat16)
    gate_table = jnp.dot(embed, time_weight, preferred_element_type=jnp.float32)
    onehot = (span_ids[:, None] == jnp.arange(timesteps.shape[0], dtype=jnp.int32)[None, :]).astype(
        jnp.float32
    )
    return jnp.dot(onehot, gate_table, precision=lax.Precision.HIGHEST)


def per_device(queries, keys, values, span_ids, timesteps, time_weight):
    runs, groups = lax.axis_size("span"), lax.axis_size("head")
    run, rank = lax.axis_index("span"), lax.axis_index("head")
    spans = timesteps.shape[0]
    chunk, width = queries.shape
    local = width // groups
    heads = local // HEAD_DIM

    def device(zone, core, y, x):
        return (2 * zone + core) * groups + 2 * y + x

    across = [
        [device(zone, core, y, x) for zone in range(ZONES)]
        for core in range(2)
        for y in range(4)
        for x in range(2)
    ]
    up = [(h, (h + 2) % groups) for h in range(groups)]
    down = [(h, (h - 2) % groups) for h in range(groups)]
    core_swap = [(s, s ^ 1) for s in range(runs)]
    partner = [(h, h ^ 1) for h in range(groups)]

    def exchange(parts):
        return lax.all_to_all(
            parts, BOTH, split_axis=0, concat_axis=0, axis_index_groups=across, tiled=True
        )

    def after(*values):
        return lax.optimization_barrier(values)

    def swapped(block):
        return block, lax.ppermute(block, "span", core_swap)

    def sides(block):
        return lax.ppermute(block, "head", down), lax.ppermute(block, "head", up)

    pair = 2 * HEAD_DIM
    first, rest = pl.pallas_call(
        pack_kernel, out_shape=[packed(pair + NOTE), packed((3 * heads - 2) * HEAD_DIM)]
    )(queries, keys, values, span_ids.reshape(1, -1))
    first = exchange(first)
    rest, first = after(rest, first)
    rest = exchange(rest)
    above, below = sides(first)
    half = ZONES // 2
    opposite = [lax.ppermute(below[:half], "head", up), lax.ppermute(above[half:], "head", down)]
    near = jnp.stack([first, above, below, jnp.concatenate(opposite)])

    def combined(notes):
        is_count = jnp.arange(HEAD_DIM) < K_NORM
        return jnp.where(is_count, jnp.sum(notes, axis=0), jnp.max(notes, axis=0))

    def noted(blocks):
        return combined(blocks[:, :, pair].reshape(-1, HEAD_DIM).astype(jnp.float32))

    note = noted(near)
    rest, near, note = after(rest, near, note)
    own_q = [rest[:, start : start + HEAD_DIM] for start in range(2 * pair, rest.shape[1], HEAD_DIM)]
    own_q[0], block_one, block_two = after(own_q[0], rest[:, :pair], rest[:, pair : 2 * pair])
    above, below = sides(block_one)
    their_q = [lax.ppermute(own_q[0], "head", partner), None, None]
    near, far = swapped(near)
    note = combined(jnp.stack([note, noted(far)]))[None]
    note, above, below, their_q[0] = after(note, above, below, their_q[0])
    note = combined(jnp.concatenate([note, lax.ppermute(note, "head", partner)]))
    squares = note[K_NORM : K_NORM + heads] * note[Q_NORM : Q_NORM + heads]
    plain = (squares * (1.05 * SCALE**2) < PLAIN_LIMIT**2).astype(jnp.int32)
    ends = note[:spans].astype(jnp.int32)

    core, y, side = run % 2, rank // 2, rank % 2
    offsets = jnp.stack([side, 1 - side])[None, :, None] * HEAD_DIM
    position = jnp.arange(ZONES)[:, None, None] * 2048 + offsets + jnp.arange(HEAD_DIM)[None, None, :]
    position = (position + (core * 1024 + y * SEGMENT)).reshape(ZONES, SEGMENT)
    reach = jnp.min(
        jnp.where(ends > position[..., None], ends, runs * groups * chunk), axis=2
    )
    reach = jnp.maximum(reach - side * HEAD_DIM, 0)
    seen = (reach // SEGMENT) * HEAD_DIM + jnp.minimum(reach % SEGMENT, HEAD_DIM)
    seen = seen.astype(jnp.int32)
    counts = jnp.maximum((jnp.max(seen, axis=1) + WIDTH - 1) // WIDTH, 1)
    info = jnp.concatenate([jnp.stack([core, y]), counts, plain]).astype(jnp.int32)
    seen = seen.reshape(ZONES, 1, SEGMENT)

    parts = [None] * (2 * heads)

    def attended(info, head, sources):
        parts[2 * head], theirs = attend(info, rest, 4 + head, their_q[head], seen, sources, head)
        info, theirs = after(info, theirs)
        parts[2 * head + 1] = lax.ppermute(theirs, "head", partner)
        return info

    info, block_two, above, below = after(info, block_two, above, below)
    opposite = lax.ppermute(below, "head", up)
    above_two, below_two = sides(block_two)
    own_q[1], own_q[2], info = after(own_q[1], own_q[2], info)
    their_q[1] = lax.ppermute(own_q[1], "head", partner)
    info = attended(info, 0, (near, far))
    info, opposite, above_two, below_two, their_q[1] = after(
        info, opposite, above_two, below_two, their_q[1]
    )
    near, far = swapped(jnp.stack([block_one, above, below, opposite]))
    opposite = lax.ppermute(above_two, "head", down)
    near_two, far_two = swapped(jnp.stack([block_two, above_two, below_two]))
    their_q[2] = lax.ppermute(own_q[2], "head", partner)
    info = attended(info, 1, (near, far))
    info, opposite, their_q[2] = after(info, opposite, their_q[2])
    last, far_last = swapped(opposite[None])
    info = attended(info, 2, (near_two, last, far_two, far_last))
    mixed = exchange(merge(parts))
    gates = gate_rows(span_ids, timesteps, time_weight)
    return pl.pallas_call(
        gate_kernel, out_shape=jax.ShapeDtypeStruct((chunk, width), jnp.bfloat16), compiler_params=ROOMY
    )(gates, mixed)


def solution(mesh):
    return jax.shard_map(
        per_device,
        mesh=mesh,
        in_specs=(
            P(("span", "head"), None),
            P(("span", "head"), None),
            P(("span", "head"), None),
            P(("span", "head")),
            P(),
            P(),
        ),
        out_specs=P(("span", "head"), None),
        check_vma=False,
    )
```

```python
import functools
import math

import jax
import jax.numpy as jnp
from jax import lax
from jax.experimental import pallas as pl
from jax.experimental.pallas import tpu as pltpu
from jax.sharding import PartitionSpec as P

HEAD_DIM = 128
SCALE = HEAD_DIM**-0.5
SCALE_LOG2 = SCALE * math.log2(math.e)
BOTH = ("span", "head")
ZONES = 8
SEGMENT = 2 * HEAD_DIM
KEYS = 8192
WIDTH = 256
ITEMS = 8
K_NORM, Q_NORM = 32, 40
NOTE = 16
PLAIN_LIMIT = 70.0
LOW = -1e30
ROOMY = pltpu.CompilerParams(vmem_limit_bytes=24 << 20)


def dot(a, b):
    return jnp.dot(a, b, preferred_element_type=jnp.float32)


def attend_kernel(head, info_ref, own_q, their_q, end_ref, *refs):
    sources, refs = refs[:-8], refs[-8:]
    own_out, their_out, kv_ref, qt_ref, weight_ref, acc_ref, top_ref, sems = refs
    core, rank = info_ref[0], info_ref[1]
    blocks = ZONES

    copies = []
    half = len(sources) // 2
    for group, c in ((sources[:half], core), (sources[half:], 1 - core)):
        pieces = [src.at[k] for src in group for k in range(src.shape[0])]
        for piece, step in zip(pieces, (0, 1, 3, 2)):
            copies.append(
                pltpu.make_async_copy(
                    piece.at[:, pl.ds(0, 2 * HEAD_DIM)],
                    kv_ref.at[(rank + step) % 4, c],
                    sems.at[len(copies)],
                )
            )
    for copy in copies:
        copy.start()

    for zone in range(ZONES):
        qt_ref[zone] = jnp.concatenate([own_q[zone], their_q[zone]], axis=1)
    acc_ref[...] = jnp.zeros_like(acc_ref)
    top_ref[...] = jnp.zeros_like(top_ref)
    ones = jnp.ones((NOTE, WIDTH), jnp.bfloat16)
    for copy in copies:
        copy.wait()

    def part(i, rows):
        return kv_ref[pl.ds((i % 2) * 2, 2), (i // 2) % 2, i // 4, rows]

    def keys_at(i):
        return part(i, slice(0, HEAD_DIM)).reshape(WIDTH, HEAD_DIM)

    def values_at(i):
        block = part(i, slice(HEAD_DIM, 2 * HEAD_DIM))
        return jnp.concatenate([jnp.concatenate([block[0], block[1]], axis=1), ones], axis=0)

    def visible_at(r, i):
        row = lax.broadcasted_iota(jnp.int32, (WIDTH, SEGMENT), 0)
        return row < end_ref[r] - i * WIDTH

    def score(item):
        r, i = item
        return dot(keys_at(i), qt_ref[jnp.minimum(r, blocks - 1)])

    def weigh(slot, item, scores):
        r, i = item
        weights = jnp.exp2(scores * SCALE_LOG2)
        weights = jnp.where(visible_at(jnp.minimum(r, blocks - 1), i), weights, 0.0)
        weight_ref[slot] = weights.astype(jnp.bfloat16)

    def absorb(slot, item):
        r, i = item
        acc_ref[r] += dot(values_at(i), weight_ref[slot])

    def careful(r, i):
        scores = dot(keys_at(i), qt_ref[r]) * SCALE_LOG2
        visible = visible_at(r, i)
        scores = jnp.where(visible, scores, LOW)
        old = top_ref[r, :1]
        new = jnp.maximum(old, jnp.max(scores, axis=0, keepdims=True))
        weights = jnp.where(visible, jnp.exp2(scores - new), 0.0).astype(jnp.bfloat16)
        acc_ref[r] = acc_ref[r] * jnp.exp2(old - new) + dot(values_at(i), weights)
        top_ref[r] = jnp.broadcast_to(new, top_ref.shape[1:])

    def count(r):
        return info_ref[2 + r]

    plain = info_ref[2 + blocks + head] == 1

    @pl.when(plain)
    def _():
        def following(item):
            r, i = item
            over = i + 1 >= count(jnp.minimum(r, blocks - 1))
            over = jnp.logical_or(over, r >= blocks)
            return jnp.where(over, jnp.minimum(r + 1, blocks), r), jnp.where(over, 0, i + 1)

        def run(item):
            items = [item]
            for _ in range(ITEMS - 1):
                items.append(following(items[-1]))
            return tuple(items)

        def step(_, items):
            later = run(following(items[-1]))
            scores = score(later[0])
            for slot in range(ITEMS):
                now = scores
                if slot + 1 < ITEMS:
                    scores = score(later[slot + 1])
                absorb(slot, items[slot])
                weigh(slot, later[slot], now)
            return later

        items = run((jnp.int32(0), jnp.int32(0)))
        for slot in range(ITEMS):
            weigh(slot, items[slot], score(items[slot]))
        total = sum(count(r) for r in range(blocks))
        items = lax.fori_loop(0, (total + ITEMS - 1) // ITEMS - 1, step, items)
        for slot in range(ITEMS):
            absorb(slot, items[slot])

    @pl.when(jnp.logical_not(plain))
    def _():
        top_ref[...] = jnp.full_like(top_ref, LOW)

        def over_block(r, carry):
            def over_chunk(i, carry):
                careful(r, i)
                return carry

            return lax.fori_loop(0, count(r), over_chunk, carry)

        lax.fori_loop(0, blocks, over_block, 0)

    for r in range(blocks):
        acc = acc_ref[r]
        total = acc[HEAD_DIM : HEAD_DIM + 1]
        some = total > 0.0
        safe = jnp.where(some, total, 1.0)
        mean = (acc[:HEAD_DIM] * jnp.where(some, 1.0 / safe, 0.0)).astype(jnp.bfloat16)
        level = jnp.where(some, top_ref[r, :1] + jnp.log2(safe), LOW)
        high = level.astype(jnp.bfloat16).astype(jnp.float32)
        middle = (level - high).astype(jnp.bfloat16).astype(jnp.float32)
        low = level - high - middle
        spare = jnp.zeros((NOTE - 3, SEGMENT), jnp.float32)
        note = jnp.concatenate([high, middle, low, spare]).astype(jnp.bfloat16)
        for out, at in ((own_out, slice(0, HEAD_DIM)), (their_out, slice(HEAD_DIM, SEGMENT))):
            out[r, :HEAD_DIM, :] = mean[:, at]
            out[r, HEAD_DIM:, :] = note[:, at]


def attend(info, own_q, at, their_q, ends, sources, head):
    rows = ZONES * SEGMENT
    out = jax.ShapeDtypeStruct((ZONES, HEAD_DIM + NOTE, HEAD_DIM), jnp.bfloat16)
    own_spec = pl.BlockSpec((ZONES, HEAD_DIM, HEAD_DIM), lambda i, *_: (0, at, 0))
    whole = pl.BlockSpec(memory_space=pltpu.VMEM)
    return pl.pallas_call(
        functools.partial(attend_kernel, head),
        grid_spec=pltpu.PrefetchScalarGridSpec(
            num_scalar_prefetch=1,
            grid=(1,),
            in_specs=[own_spec, whole, whole]
            + [pl.BlockSpec(memory_space=pltpu.HBM)] * len(sources),
            out_specs=[whole, whole],
            scratch_shapes=[
                pltpu.VMEM((4, 2, ZONES, 2 * HEAD_DIM, HEAD_DIM), jnp.bfloat16),
                pltpu.VMEM((ZONES, HEAD_DIM, SEGMENT), jnp.bfloat16),
                pltpu.VMEM((ITEMS, WIDTH, SEGMENT), jnp.bfloat16),
                pltpu.VMEM((ZONES + 1, HEAD_DIM + NOTE, SEGMENT), jnp.float32),
                pltpu.VMEM((ZONES, 8, SEGMENT), jnp.float32),
                pltpu.SemaphoreType.DMA((8,)),
            ],
        ),
        out_shape=[out, out],
        compiler_params=ROOMY,
        cost_estimate=pl.CostEstimate(
            flops=4 * rows * KEYS * HEAD_DIM,
            bytes_accessed=4 * KEYS * HEAD_DIM + 4 * rows * HEAD_DIM,
            transcendentals=rows * KEYS // 2,
        ),
    )(info, own_q, their_q, ends, *sources)


def pack_kernel(queries_ref, keys_ref, values_ref, ids_ref, first_ref, rest_ref):
    groups = first_ref.shape[0]
    heads = keys_ref.shape[1] // HEAD_DIM // groups
    ids = jnp.broadcast_to(ids_ref[...].astype(jnp.float32), (HEAD_DIM, HEAD_DIM)).T
    lane = lax.broadcasted_iota(jnp.int32, (HEAD_DIM, HEAD_DIM), 1)
    counts = jnp.sum(jnp.where(ids <= lane.astype(jnp.float32), 1.0, 0.0), axis=0, keepdims=True)
    local = heads * HEAD_DIM
    row = lax.broadcasted_iota(jnp.int32, (2 * local, HEAD_DIM), 0) // HEAD_DIM
    column = lax.broadcasted_iota(jnp.int32, (2 * local, HEAD_DIM), 1)
    wanted = jnp.where(row < heads, row + K_NORM, row - heads + Q_NORM)
    pick = jnp.where(column == wanted, 1.0, 0.0).astype(jnp.bfloat16)
    is_count = lane[:1] < K_NORM
    queries, keys, values = (queries_ref, True), (keys_ref, False), (values_ref, True)
    first = [(keys, 0), (values, 0)]
    rest = [(part, head) for head in range(1, heads) for part in (keys, values)]
    rest += [(queries, head) for head in range(heads)]
    for g in range(groups):
        for out_ref, parts in ((first_ref, first), (rest_ref, rest)):
            for j, ((ref, turn), head) in enumerate(parts):
                start = g * local + head * HEAD_DIM
                block = ref[:, start : start + HEAD_DIM]
                out_ref[g, j * HEAD_DIM : (j + 1) * HEAD_DIM] = block.T if turn else block
        rows = [ref[:, g * local : (g + 1) * local].astype(jnp.float32) for ref in (keys_ref, queries_ref)]
        squares = jnp.concatenate([(x * x).astype(jnp.bfloat16) for x in rows], axis=1)
        norms = jnp.max(dot(squares, pick), axis=0, keepdims=True) * 1.02
        note = jnp.where(is_count, counts, norms)
        note = jnp.broadcast_to(note, (NOTE, HEAD_DIM)).astype(jnp.bfloat16)
        first_ref[g, len(first) * HEAD_DIM :] = note


def packed(rows):
    return jax.ShapeDtypeStruct((ZONES, rows, HEAD_DIM), jnp.bfloat16)


def merge_kernel(*refs):
    out = refs[-1]

    def level(ref, zone):
        note = ref[zone, HEAD_DIM:, :].astype(jnp.float32)
        return note[0:1] + note[1:2] + note[2:3]

    for head in range(len(refs) // 2):
        one, two = refs[2 * head], refs[2 * head + 1]
        at = slice(head * HEAD_DIM, (head + 1) * HEAD_DIM)
        for zone in range(ZONES):
            share = 1.0 / (1.0 + jnp.exp2(level(two, zone) - level(one, zone)))
            a, b = (ref[zone, :HEAD_DIM, :].astype(jnp.float32) for ref in (one, two))
            out[zone, at, :] = (b + (a - b) * share).astype(jnp.bfloat16)


def merge(parts):
    return pl.pallas_call(merge_kernel, out_shape=packed(len(parts) // 2 * HEAD_DIM), compiler_params=ROOMY)(*parts)


def gate_kernel(gate_ref, mixed_ref, out_ref):
    groups, local, _ = mixed_ref.shape
    for g in range(groups):
        for h in range(0, local, HEAD_DIM):
            at = slice(g * local + h, g * local + h + HEAD_DIM)
            attended = mixed_ref[g, h : h + HEAD_DIM, :].T.astype(jnp.float32)
            out_ref[:, at] = (gate_ref[:, at] * attended).astype(jnp.bfloat16)


def gate_rows(span_ids, timesteps, time_weight):
    half = time_weight.shape[0] // 2
    freqs = jnp.exp(-math.log(10000.0) * jnp.arange(half, dtype=jnp.float32) / half)
    angles = timesteps.astype(jnp.float32)[:, None] * freqs[None, :]
    embed = jnp.concatenate([jnp.cos(angles), jnp.sin(angles)], axis=1).astype(jnp.bfloat16)
    gate_table = jnp.dot(embed, time_weight, preferred_element_type=jnp.float32)
    onehot = (span_ids[:, None] == jnp.arange(timesteps.shape[0], dtype=jnp.int32)[None, :]).astype(
        jnp.float32
    )
    return jnp.dot(onehot, gate_table, precision=lax.Precision.HIGHEST)


def per_device(queries, keys, values, span_ids, timesteps, time_weight):
    runs, groups = lax.axis_size("span"), lax.axis_size("head")
    run, rank = lax.axis_index("span"), lax.axis_index("head")
    spans = timesteps.shape[0]
    chunk, width = queries.shape
    local = width // groups
    heads = local // HEAD_DIM

    def device(zone, core, y, x):
        return (2 * zone + core) * groups + 2 * y + x

    across = [
        [device(zone, core, y, x) for zone in range(ZONES)]
        for core in range(2)
        for y in range(4)
        for x in range(2)
    ]
    up = [(h, (h + 2) % groups) for h in range(groups)]
    down = [(h, (h - 2) % groups) for h in range(groups)]
    core_swap = [(s, s ^ 1) for s in range(runs)]
    partner = [(h, h ^ 1) for h in range(groups)]

    def exchange(parts):
        return lax.all_to_all(
            parts, BOTH, split_axis=0, concat_axis=0, axis_index_groups=across, tiled=True
        )

    def after(*values):
        return lax.optimization_barrier(values)

    def swapped(block):
        return block, lax.ppermute(block, "span", core_swap)

    def sides(block):
        return lax.ppermute(block, "head", down), lax.ppermute(block, "head", up)

    pair = 2 * HEAD_DIM
    first, rest = pl.pallas_call(
        pack_kernel, out_shape=[packed(pair + NOTE), packed((3 * heads - 2) * HEAD_DIM)]
    )(queries, keys, values, span_ids.reshape(1, -1))
    first = exchange(first)
    rest, first = after(rest, first)
    rest = exchange(rest)
    above, below = sides(first)
    half = ZONES // 2
    opposite = [lax.ppermute(below[:half], "head", up), lax.ppermute(above[half:], "head", down)]
    near = jnp.stack([first, above, below, jnp.concatenate(opposite)])

    def combined(notes):
        is_count = jnp.arange(HEAD_DIM) < K_NORM
        return jnp.where(is_count, jnp.sum(notes, axis=0), jnp.max(notes, axis=0))

    def noted(blocks):
        return combined(blocks[:, :, pair].reshape(-1, HEAD_DIM).astype(jnp.float32))

    note = noted(near)
    rest, near, note = after(rest, near, note)
    own_q = [rest[:, start : start + HEAD_DIM] for start in range(2 * pair, rest.shape[1], HEAD_DIM)]
    own_q[0], block_one, block_two = after(own_q[0], rest[:, :pair], rest[:, pair : 2 * pair])
    above, below = sides(block_one)
    their_q = [lax.ppermute(own_q[0], "head", partner), None, None]
    near, far = swapped(near)
    note = combined(jnp.stack([note, noted(far)]))[None]
    note, above, below, their_q[0] = after(note, above, below, their_q[0])
    note = combined(jnp.concatenate([note, lax.ppermute(note, "head", partner)]))
    squares = note[K_NORM : K_NORM + heads] * note[Q_NORM : Q_NORM + heads]
    plain = (squares * (1.05 * SCALE**2) < PLAIN_LIMIT**2).astype(jnp.int32)
    ends = note[:spans].astype(jnp.int32)

    core, y, side = run % 2, rank // 2, rank % 2
    offsets = jnp.stack([side, 1 - side])[None, :, None] * HEAD_DIM
    position = jnp.arange(ZONES)[:, None, None] * 2048 + offsets + jnp.arange(HEAD_DIM)[None, None, :]
    position = (position + (core * 1024 + y * SEGMENT)).reshape(ZONES, SEGMENT)
    reach = jnp.min(
        jnp.where(ends > position[..., None], ends, runs * groups * chunk), axis=2
    )
    reach = jnp.maximum(reach - side * HEAD_DIM, 0)
    seen = (reach // SEGMENT) * HEAD_DIM + jnp.minimum(reach % SEGMENT, HEAD_DIM)
    seen = seen.astype(jnp.int32)
    counts = jnp.maximum((jnp.max(seen, axis=1) + WIDTH - 1) // WIDTH, 1)
    info = jnp.concatenate([jnp.stack([core, y]), counts, plain]).astype(jnp.int32)
    seen = seen.reshape(ZONES, 1, SEGMENT)

    parts = [None] * (2 * heads)

    def attended(info, head, sources):
        parts[2 * head], theirs = attend(info, rest, 4 + head, their_q[head], seen, sources, head)
        info, theirs = after(info, theirs)
        parts[2 * head + 1] = lax.ppermute(theirs, "head", partner)
        return info

    info, block_two, above, below = after(info, block_two, above, below)
    opposite = lax.ppermute(below, "head", up)
    above_two, below_two = sides(block_two)
    own_q[1], own_q[2], info = after(own_q[1], own_q[2], info)
    their_q[1] = lax.ppermute(own_q[1], "head", partner)
    info = attended(info, 0, (near, far))
    info, opposite, above_two, below_two, their_q[1] = after(
        info, opposite, above_two, below_two, their_q[1]
    )
    near, far = swapped(jnp.stack([block_one, above, below, opposite]))
    opposite = lax.ppermute(above_two, "head", down)
    near_two, far_two = swapped(jnp.stack([block_two, above_two, below_two]))
    their_q[2] = lax.ppermute(own_q[2], "head", partner)
    info = attended(info, 1, (near, far))
    info, opposite, their_q[2] = after(info, opposite, their_q[2])
    last, far_last = swapped(opposite[None])
    info = attended(info, 2, (near_two, last, far_two, far_last))
    mixed = exchange(merge(parts))
    gates = gate_rows(span_ids, timesteps, time_weight)
    return pl.pallas_call(
        gate_kernel, out_shape=jax.ShapeDtypeStruct((chunk, width), jnp.bfloat16), compiler_params=ROOMY
    )(gates, mixed)


def solution(mesh):
    return jax.shard_map(
        per_device,
        mesh=mesh,
        in_specs=(
            P(("span", "head"), None),
            P(("span", "head"), None),
            P(("span", "head"), None),
            P(("span", "head")),
            P(),
            P(),
        ),
        out_specs=P(("span", "head"), None),
        check_vma=False,
    )
```

```python
import functools
import math

import jax
import jax.numpy as jnp
from jax import lax
from jax.experimental import pallas as pl
from jax.experimental.pallas import tpu as pltpu
from jax.sharding import PartitionSpec as P

HEAD_DIM = 128
SCALE = HEAD_DIM**-0.5
SCALE_LOG2 = SCALE * math.log2(math.e)
BOTH = ("span", "head")
ZONES = 8
SEGMENT = 2 * HEAD_DIM
KEYS = 8192
WIDTH = 256
ITEMS = 12
K_NORM, Q_NORM = 32, 40
NOTE = 16
PLAIN_LIMIT = 70.0
LOW = -1e30
ROOMY = pltpu.CompilerParams(vmem_limit_bytes=24 << 20)


def dot(a, b):
    return jnp.dot(a, b, preferred_element_type=jnp.float32)


def attend_kernel(head, info_ref, own_q, their_q, end_ref, *refs):
    sources, refs = refs[:-8], refs[-8:]
    own_out, their_out, kv_ref, qt_ref, weight_ref, acc_ref, top_ref, sems = refs
    core, rank = info_ref[0], info_ref[1]
    blocks = ZONES

    copies = []
    half = len(sources) // 2
    for group, c in ((sources[:half], core), (sources[half:], 1 - core)):
        pieces = [src.at[k] for src in group for k in range(src.shape[0])]
        for piece, step in zip(pieces, (0, 1, 3, 2)):
            copies.append(
                pltpu.make_async_copy(
                    piece.at[:, pl.ds(0, 2 * HEAD_DIM)],
                    kv_ref.at[(rank + step) % 4, c],
                    sems.at[len(copies)],
                )
            )
    for copy in copies:
        copy.start()

    for zone in range(ZONES):
        qt_ref[zone] = jnp.concatenate([own_q[zone], their_q[zone]], axis=1)
    acc_ref[...] = jnp.zeros_like(acc_ref)
    top_ref[...] = jnp.zeros_like(top_ref)
    ones = jnp.ones((NOTE, WIDTH), jnp.bfloat16)
    for copy in copies:
        copy.wait()

    def part(i, rows):
        return kv_ref[pl.ds((i % 2) * 2, 2), (i // 2) % 2, i // 4, rows]

    def keys_at(i):
        return part(i, slice(0, HEAD_DIM)).reshape(WIDTH, HEAD_DIM)

    def values_at(i):
        block = part(i, slice(HEAD_DIM, 2 * HEAD_DIM))
        return jnp.concatenate([jnp.concatenate([block[0], block[1]], axis=1), ones], axis=0)

    def visible_at(r, i):
        row = lax.broadcasted_iota(jnp.int32, (WIDTH, SEGMENT), 0)
        return row < end_ref[r] - i * WIDTH

    def score(item):
        r, i = item
        return dot(keys_at(i), qt_ref[jnp.minimum(r, blocks - 1)])

    def weigh(slot, item, scores):
        r, i = item
        weights = jnp.exp2(scores * SCALE_LOG2)
        weights = jnp.where(visible_at(jnp.minimum(r, blocks - 1), i), weights, 0.0)
        weight_ref[slot] = weights.astype(jnp.bfloat16)

    def absorb(slot, item):
        r, i = item
        acc_ref[r] += dot(values_at(i), weight_ref[slot])

    def careful(r, i):
        scores = dot(keys_at(i), qt_ref[r]) * SCALE_LOG2
        visible = visible_at(r, i)
        scores = jnp.where(visible, scores, LOW)
        old = top_ref[r, :1]
        new = jnp.maximum(old, jnp.max(scores, axis=0, keepdims=True))
        weights = jnp.where(visible, jnp.exp2(scores - new), 0.0).astype(jnp.bfloat16)
        acc_ref[r] = acc_ref[r] * jnp.exp2(old - new) + dot(values_at(i), weights)
        top_ref[r] = jnp.broadcast_to(new, top_ref.shape[1:])

    def count(r):
        return info_ref[2 + r]

    plain = info_ref[2 + blocks + head] == 1

    @pl.when(plain)
    def _():
        def following(item):
            r, i = item
            over = i + 1 >= count(jnp.minimum(r, blocks - 1))
            over = jnp.logical_or(over, r >= blocks)
            return jnp.where(over, jnp.minimum(r + 1, blocks), r), jnp.where(over, 0, i + 1)

        def run(item):
            items = [item]
            for _ in range(ITEMS - 1):
                items.append(following(items[-1]))
            return tuple(items)

        def step(_, items):
            later = run(following(items[-1]))
            scores = score(later[0])
            for slot in range(ITEMS):
                now = scores
                if slot + 1 < ITEMS:
                    scores = score(later[slot + 1])
                absorb(slot, items[slot])
                weigh(slot, later[slot], now)
            return later

        items = run((jnp.int32(0), jnp.int32(0)))
        for slot in range(ITEMS):
            weigh(slot, items[slot], score(items[slot]))
        total = sum(count(r) for r in range(blocks))
        items = lax.fori_loop(0, (total + ITEMS - 1) // ITEMS - 1, step, items)
        for slot in range(ITEMS):
            absorb(slot, items[slot])

    @pl.when(jnp.logical_not(plain))
    def _():
        top_ref[...] = jnp.full_like(top_ref, LOW)

        def over_block(r, carry):
            def over_chunk(i, carry):
                careful(r, i)
                return carry

            return lax.fori_loop(0, count(r), over_chunk, carry)

        lax.fori_loop(0, blocks, over_block, 0)

    for r in range(blocks):
        acc = acc_ref[r]
        total = acc[HEAD_DIM : HEAD_DIM + 1]
        some = total > 0.0
        safe = jnp.where(some, total, 1.0)
        mean = (acc[:HEAD_DIM] * jnp.where(some, 1.0 / safe, 0.0)).astype(jnp.bfloat16)
        level = jnp.where(some, top_ref[r, :1] + jnp.log2(safe), LOW)
        high = level.astype(jnp.bfloat16).astype(jnp.float32)
        middle = (level - high).astype(jnp.bfloat16).astype(jnp.float32)
        low = level - high - middle
        spare = jnp.zeros((NOTE - 3, SEGMENT), jnp.float32)
        note = jnp.concatenate([high, middle, low, spare]).astype(jnp.bfloat16)
        for out, at in ((own_out, slice(0, HEAD_DIM)), (their_out, slice(HEAD_DIM, SEGMENT))):
            out[r, :HEAD_DIM, :] = mean[:, at]
            out[r, HEAD_DIM:, :] = note[:, at]


def attend(info, own_q, at, their_q, ends, sources, head):
    rows = ZONES * SEGMENT
    out = jax.ShapeDtypeStruct((ZONES, HEAD_DIM + NOTE, HEAD_DIM), jnp.bfloat16)
    own_spec = pl.BlockSpec((ZONES, HEAD_DIM, HEAD_DIM), lambda i, *_: (0, at, 0))
    whole = pl.BlockSpec(memory_space=pltpu.VMEM)
    return pl.pallas_call(
        functools.partial(attend_kernel, head),
        grid_spec=pltpu.PrefetchScalarGridSpec(
            num_scalar_prefetch=1,
            grid=(1,),
            in_specs=[own_spec, whole, whole]
            + [pl.BlockSpec(memory_space=pltpu.HBM)] * len(sources),
            out_specs=[whole, whole],
            scratch_shapes=[
                pltpu.VMEM((4, 2, ZONES, 2 * HEAD_DIM, HEAD_DIM), jnp.bfloat16),
                pltpu.VMEM((ZONES, HEAD_DIM, SEGMENT), jnp.bfloat16),
                pltpu.VMEM((ITEMS, WIDTH, SEGMENT), jnp.bfloat16),
                pltpu.VMEM((ZONES + 1, HEAD_DIM + NOTE, SEGMENT), jnp.float32),
                pltpu.VMEM((ZONES, 8, SEGMENT), jnp.float32),
                pltpu.SemaphoreType.DMA((8,)),
            ],
        ),
        out_shape=[out, out],
        compiler_params=ROOMY,
        cost_estimate=pl.CostEstimate(
            flops=4 * rows * KEYS * HEAD_DIM,
            bytes_accessed=4 * KEYS * HEAD_DIM + 4 * rows * HEAD_DIM,
            transcendentals=rows * KEYS // 2,
        ),
    )(info, own_q, their_q, ends, *sources)


def pack_kernel(queries_ref, keys_ref, values_ref, ids_ref, first_ref, rest_ref):
    groups = first_ref.shape[0]
    heads = keys_ref.shape[1] // HEAD_DIM // groups
    ids = jnp.broadcast_to(ids_ref[...].astype(jnp.float32), (HEAD_DIM, HEAD_DIM)).T
    lane = lax.broadcasted_iota(jnp.int32, (HEAD_DIM, HEAD_DIM), 1)
    counts = jnp.sum(jnp.where(ids <= lane.astype(jnp.float32), 1.0, 0.0), axis=0, keepdims=True)
    local = heads * HEAD_DIM
    row = lax.broadcasted_iota(jnp.int32, (2 * local, HEAD_DIM), 0) // HEAD_DIM
    column = lax.broadcasted_iota(jnp.int32, (2 * local, HEAD_DIM), 1)
    wanted = jnp.where(row < heads, row + K_NORM, row - heads + Q_NORM)
    pick = jnp.where(column == wanted, 1.0, 0.0).astype(jnp.bfloat16)
    is_count = lane[:1] < K_NORM
    queries, keys, values = (queries_ref, True), (keys_ref, False), (values_ref, True)
    first = [(keys, 0), (values, 0)]
    rest = [(part, head) for head in range(1, heads) for part in (keys, values)]
    rest += [(queries, head) for head in range(heads)]
    for g in range(groups):
        for out_ref, parts in ((first_ref, first), (rest_ref, rest)):
            for j, ((ref, turn), head) in enumerate(parts):
                start = g * local + head * HEAD_DIM
                block = ref[:, start : start + HEAD_DIM]
                out_ref[g, j * HEAD_DIM : (j + 1) * HEAD_DIM] = block.T if turn else block
        rows = [ref[:, g * local : (g + 1) * local].astype(jnp.float32) for ref in (keys_ref, queries_ref)]
        squares = jnp.concatenate([(x * x).astype(jnp.bfloat16) for x in rows], axis=1)
        norms = jnp.max(dot(squares, pick), axis=0, keepdims=True) * 1.02
        note = jnp.where(is_count, counts, norms)
        note = jnp.broadcast_to(note, (NOTE, HEAD_DIM)).astype(jnp.bfloat16)
        first_ref[g, len(first) * HEAD_DIM :] = note


def packed(rows):
    return jax.ShapeDtypeStruct((ZONES, rows, HEAD_DIM), jnp.bfloat16)


def merge_kernel(*refs):
    out = refs[-1]

    def level(ref, zone):
        note = ref[zone, HEAD_DIM:, :].astype(jnp.float32)
        return note[0:1] + note[1:2] + note[2:3]

    for head in range(len(refs) // 2):
        one, two = refs[2 * head], refs[2 * head + 1]
        at = slice(head * HEAD_DIM, (head + 1) * HEAD_DIM)
        for zone in range(ZONES):
            share = 1.0 / (1.0 + jnp.exp2(level(two, zone) - level(one, zone)))
            a, b = (ref[zone, :HEAD_DIM, :].astype(jnp.float32) for ref in (one, two))
            out[zone, at, :] = (b + (a - b) * share).astype(jnp.bfloat16)


def merge(parts):
    return pl.pallas_call(merge_kernel, out_shape=packed(len(parts) // 2 * HEAD_DIM), compiler_params=ROOMY)(*parts)


def gate_kernel(gate_ref, mixed_ref, out_ref):
    groups, local, _ = mixed_ref.shape
    for g in range(groups):
        for h in range(0, local, HEAD_DIM):
            at = slice(g * local + h, g * local + h + HEAD_DIM)
            attended = mixed_ref[g, h : h + HEAD_DIM, :].T.astype(jnp.float32)
            out_ref[:, at] = (gate_ref[:, at] * attended).astype(jnp.bfloat16)


def gate_rows(span_ids, timesteps, time_weight):
    half = time_weight.shape[0] // 2
    freqs = jnp.exp(-math.log(10000.0) * jnp.arange(half, dtype=jnp.float32) / half)
    angles = timesteps.astype(jnp.float32)[:, None] * freqs[None, :]
    embed = jnp.concatenate([jnp.cos(angles), jnp.sin(angles)], axis=1).astype(jnp.bfloat16)
    gate_table = jnp.dot(embed, time_weight, preferred_element_type=jnp.float32)
    onehot = (span_ids[:, None] == jnp.arange(timesteps.shape[0], dtype=jnp.int32)[None, :]).astype(
        jnp.float32
    )
    return jnp.dot(onehot, gate_table, precision=lax.Precision.HIGHEST)


def per_device(queries, keys, values, span_ids, timesteps, time_weight):
    runs, groups = lax.axis_size("span"), lax.axis_size("head")
    run, rank = lax.axis_index("span"), lax.axis_index("head")
    spans = timesteps.shape[0]
    chunk, width = queries.shape
    local = width // groups
    heads = local // HEAD_DIM

    def device(zone, core, y, x):
        return (2 * zone + core) * groups + 2 * y + x

    across = [
        [device(zone, core, y, x) for zone in range(ZONES)]
        for core in range(2)
        for y in range(4)
        for x in range(2)
    ]
    up = [(h, (h + 2) % groups) for h in range(groups)]
    down = [(h, (h - 2) % groups) for h in range(groups)]
    core_swap = [(s, s ^ 1) for s in range(runs)]
    partner = [(h, h ^ 1) for h in range(groups)]

    def exchange(parts):
        return lax.all_to_all(
            parts, BOTH, split_axis=0, concat_axis=0, axis_index_groups=across, tiled=True
        )

    def after(*values):
        return lax.optimization_barrier(values)

    def swapped(block):
        return block, lax.ppermute(block, "span", core_swap)

    def sides(block):
        return lax.ppermute(block, "head", down), lax.ppermute(block, "head", up)

    pair = 2 * HEAD_DIM
    first, rest = pl.pallas_call(
        pack_kernel, out_shape=[packed(pair + NOTE), packed((3 * heads - 2) * HEAD_DIM)]
    )(queries, keys, values, span_ids.reshape(1, -1))
    first = exchange(first)
    rest, first = after(rest, first)
    rest = exchange(rest)
    above, below = sides(first)
    half = ZONES // 2
    opposite = [lax.ppermute(below[:half], "head", up), lax.ppermute(above[half:], "head", down)]
    near = jnp.stack([first, above, below, jnp.concatenate(opposite)])

    def combined(notes):
        is_count = jnp.arange(HEAD_DIM) < K_NORM
        return jnp.where(is_count, jnp.sum(notes, axis=0), jnp.max(notes, axis=0))

    def noted(blocks):
        return combined(blocks[:, :, pair].reshape(-1, HEAD_DIM).astype(jnp.float32))

    note = noted(near)
    rest, near, note = after(rest, near, note)
    own_q = [rest[:, start : start + HEAD_DIM] for start in range(2 * pair, rest.shape[1], HEAD_DIM)]
    own_q[0], block_one, block_two = after(own_q[0], rest[:, :pair], rest[:, pair : 2 * pair])
    above, below = sides(block_one)
    their_q = [lax.ppermute(own_q[0], "head", partner), None, None]
    near, far = swapped(near)
    note = combined(jnp.stack([note, noted(far)]))[None]
    note, above, below, their_q[0] = after(note, above, below, their_q[0])
    note = combined(jnp.concatenate([note, lax.ppermute(note, "head", partner)]))
    squares = note[K_NORM : K_NORM + heads] * note[Q_NORM : Q_NORM + heads]
    plain = (squares * (1.05 * SCALE**2) < PLAIN_LIMIT**2).astype(jnp.int32)
    ends = note[:spans].astype(jnp.int32)

    core, y, side = run % 2, rank // 2, rank % 2
    offsets = jnp.stack([side, 1 - side])[None, :, None] * HEAD_DIM
    position = jnp.arange(ZONES)[:, None, None] * 2048 + offsets + jnp.arange(HEAD_DIM)[None, None, :]
    position = (position + (core * 1024 + y * SEGMENT)).reshape(ZONES, SEGMENT)
    reach = jnp.min(
        jnp.where(ends > position[..., None], ends, runs * groups * chunk), axis=2
    )
    reach = jnp.maximum(reach - side * HEAD_DIM, 0)
    seen = (reach // SEGMENT) * HEAD_DIM + jnp.minimum(reach % SEGMENT, HEAD_DIM)
    seen = seen.astype(jnp.int32)
    counts = jnp.maximum((jnp.max(seen, axis=1) + WIDTH - 1) // WIDTH, 1)
    info = jnp.concatenate([jnp.stack([core, y]), counts, plain]).astype(jnp.int32)
    seen = seen.reshape(ZONES, 1, SEGMENT)

    parts = [None] * (2 * heads)

    def attended(info, head, sources):
        parts[2 * head], theirs = attend(info, rest, 4 + head, their_q[head], seen, sources, head)
        info, theirs = after(info, theirs)
        parts[2 * head + 1] = lax.ppermute(theirs, "head", partner)
        return info

    info, block_two, above, below = after(info, block_two, above, below)
    opposite = lax.ppermute(below, "head", up)
    above_two, below_two = sides(block_two)
    own_q[1], own_q[2], info = after(own_q[1], own_q[2], info)
    their_q[1] = lax.ppermute(own_q[1], "head", partner)
    info = attended(info, 0, (near, far))
    info, opposite, above_two, below_two, their_q[1] = after(
        info, opposite, above_two, below_two, their_q[1]
    )
    near, far = swapped(jnp.stack([block_one, above, below, opposite]))
    opposite = lax.ppermute(above_two, "head", down)
    near_two, far_two = swapped(jnp.stack([block_two, above_two, below_two]))
    their_q[2] = lax.ppermute(own_q[2], "head", partner)
    info = attended(info, 1, (near, far))
    info, opposite, their_q[2] = after(info, opposite, their_q[2])
    last, far_last = swapped(opposite[None])
    info = attended(info, 2, (near_two, last, far_two, far_last))
    mixed = exchange(merge(parts))
    gates = gate_rows(span_ids, timesteps, time_weight)
    return pl.pallas_call(
        gate_kernel, out_shape=jax.ShapeDtypeStruct((chunk, width), jnp.bfloat16), compiler_params=ROOMY
    )(gates, mixed)


def solution(mesh):
    return jax.shard_map(
        per_device,
        mesh=mesh,
        in_specs=(
            P(("span", "head"), None),
            P(("span", "head"), None),
            P(("span", "head"), None),
            P(("span", "head")),
            P(),
            P(),
        ),
        out_specs=P(("span", "head"), None),
        check_vma=False,
    )
```
